256 devices in a mesh: space: 16 (over z_hi, y), chan: 16 (over x, z_lo, core).
Axes of the slice: x: 4, y: 4, z: 8 (z_hi: 4, z_lo: 2; z = z_hi * 2 + z_lo), core: 2. Of those that a mesh axis runs over, the one named last changes fastest.
Arguments:
- image: bfloat16 [3, 32, 8192], P(None, None, 'space'), may hold values from -6 to 6
- mask: int32 [32, 8192], P(None, 'space'), may hold values from 0 to 1, as said below
- anchors: bfloat16 [1024, 75], P('chan'), may hold values from -0.75 to 0.75
- whiten: bfloat16 [1024, 1024], P(None, 'chan'), may hold values from -0.1875 to 0.1875
- cotangent: bfloat16 [1024, 16, 4096], P('chan', None, 'space'), may hold values from -0.59765625 to 0.59765625
Outputs:
- grad_anchors: float32 [1024, 75], P('chan')
- grad_whiten: float32 [1024, 1024], P('space', 'chan')
- grad_image: float32 [3, 32, 8192], P(None, 'chan', 'space')
The draws below stay inside these ranges and needn't reach their ends.
Inputs may be any that keep to these rules, and one draw needn't show every extreme that they name: `mask`: 1 where a pixel holds tissue.
All inputs are finite; a program needn't handle non-finite values.
Results may differ from the reference program's by a relative error of at most 0.011.
Values may be sent and summed in bfloat16 or wider, within the bound.
No kernel may reach another device: no remote copies, remote signals or barrier semaphores. Data moves between devices by JAX's collectives and lax.ppermute only.
A program may use at most 128 MiB of HBM per device.

```python
import math
import jax
import jax.numpy as jnp
from jax import lax

CH = 1024
PATCH = 75
R = 32
NCOL = 8192


def draw_mask(key, part):
    key = jax.random.fold_in(key, 5)
    region_key, roll_key = jax.random.split(key)
    regions = jax.random.randint(region_key, (R // 8, NCOL // 8), 0, 3)
    regions = jnp.repeat(jnp.repeat(regions, 8, axis=0), 8, axis=1)
    dice_rolls = jax.random.randint(roll_key, (R, NCOL), 0, 10)
    thresholds = jnp.where(regions == 0, 0, jnp.where(regions == 1, 5, 9))
    return (dice_rolls < thresholds).astype(jnp.int32)


def with_spikes(entries, key, source, target, shards_of, factor):
    owner, partner = [(jnp.arange(entries.shape[dim]) // (entries.shape[dim] // shards_of)).reshape([-1 if axis == dim else 1 for axis in range(entries.ndim)]) for dim in (source, target)]
    chosen = jax.random.permutation(key, shards_of)[partner]
    strong = (owner == chosen) | (owner == (partner + shards_of // 2) % shards_of)
    return jnp.where(strong, factor * entries, entries)


def level_of(own_key, shape, cuts, low, top_value):
    factor_of = 1.0
    for axis_at, blocks in cuts:
        steps = jax.random.uniform(jax.random.fold_in(jax.random.fold_in(own_key, 6), axis_at), (blocks,), jnp.float32, low / len(cuts), top_value / len(cuts))
        factor_of = factor_of * jnp.repeat(jnp.exp(steps), shape[axis_at] // blocks).reshape((-1,) + (1,) * (len(shape) - 1 - axis_at))
    return factor_of


def noise(stream_key, extent, scale, most, cuts=(), dtype=jnp.bfloat16):
    entries = scale * jax.random.normal(stream_key, extent, jnp.float32)
    if cuts:
        entries = entries * level_of(stream_key, extent, cuts, -0.22, 0.18)
    return jnp.clip(entries, -most, most).astype(dtype)


def bell_draw_with(own_key, shape, deviation, bound, cuts, heavy, held_as=jnp.bfloat16):
    drawn = deviation * jax.random.normal(own_key, shape, jnp.float32)
    if cuts:
        drawn = drawn * level_of(own_key, shape, cuts, -0.22, 0.18)
    return jnp.clip(with_spikes(drawn, jax.random.fold_in(own_key, 3), *heavy), -bound, bound).astype(held_as)


def setup_inputs(seed: int = 0) -> dict:
    streams_of = jax.random.split(jax.random.key(seed), 6)
    return {
        "image": noise(streams_of[0], (3, R, NCOL), 1.0, 6.0, ((2, 16),)),
        "mask": draw_mask(jax.random.fold_in(streams_of[5], 71), 0),
        "anchors": noise(streams_of[2], (CH, PATCH), PATCH ** -0.5, 0.75, ((0, 16),)),
        "whiten": noise(streams_of[3], (CH, CH), CH ** -0.5, 0.1875, ((1, 16),)),
        "cotangent": bell_draw_with(streams_of[4], (CH, R // 2, NCOL // 2), 0.1, 0.59765625, ((0, 16), (2, 16)), (2, 0, 16, 2.0)),
    }


EPS = 1e-05
ALPHA = 4.0
TAPS = [(offset, math.exp(-offset * offset / 8.0)) for offset in range(-4, 5)]
block_anchors = 64

def row_matrix(rows):
    output_row = lax.broadcasted_iota(jnp.int32, (rows // 2, rows), 0)
    input_row = lax.broadcasted_iota(jnp.int32, (rows // 2, rows), 1)
    distance = (2 * output_row - input_row).astype(jnp.float32)
    return jnp.where(jnp.abs(distance) <= 4.0, jnp.exp(-distance * distance / 8.0), 0.0).astype(jnp.float32)

def gather_patches(padded, rows, cols, col_start):
    pieces = []
    for channel in range(3):
        for row_off in range(-2, 3):
            for col_off in range(-2, 3):
                pieces.append(padded[channel, 2 + row_off:2 + row_off + rows, col_start + col_off:col_start + col_off + cols])
    return jnp.stack(pieces)

def scatter_patches(padded, rows, cols, col_start):
    result = []
    for channel in range(3):
        total = jnp.zeros((rows, cols), jnp.float32)
        for row_off in range(-2, 3):
            for col_off in range(-2, 3):
                index = channel * 25 + (row_off + 2) * 5 + (col_off + 2)
                total = total + padded[index, 2 - row_off:2 - row_off + rows, col_start - col_off:col_start - col_off + cols]
        result.append(total)
    return jnp.stack(result)

def pool_columns(values, count, start):
    total = None
    for offset, factor in TAPS:
        piece = lax.slice_in_dim(values, start - offset, start - offset + 2 * (count - 1) + 1, 2, 2)
        total = factor * piece if total is None else total + factor * piece
    return total

def spread_columns(values, count, start):
    total = None
    for offset, factor in TAPS:
        piece = lax.slice_in_dim(values, start + offset, start + offset + count, 1, 2)
        total = factor * piece if total is None else total + factor * piece
    return total

def pool_both(values, weights, count):
    rowed = jnp.einsum('ai,cij->caj', weights, values)
    return pool_columns(rowed, count, 4)

def reference(image, mask, anchors, whiten, cotangent):
    padded = jnp.pad(image.astype(jnp.float32), ((0, 0), (2, 2), (2, 2)))
    patch = gather_patches(padded, R, NCOL, 2)
    patch_norm = jnp.sqrt(lax.optimization_barrier(jnp.sum(patch * patch, axis=0)) + EPS)
    unit_patch = patch / patch_norm
    unit_low = unit_patch.astype(jnp.bfloat16).reshape(75, R * NCOL)
    weights = row_matrix(R)
    tissue = mask.astype(jnp.float32)
    density = pool_both(jnp.pad(tissue, ((0, 0), (4, 4)))[None], weights, NCOL // 2)[0]
    density = jnp.maximum(density, 1.0)
    blocks = CH // block_anchors
    anchor_blocks = anchors.reshape(blocks, block_anchors, 75)

    def kernel_of(anchor_block):
        similarity = jnp.dot(anchor_block, unit_low, preferred_element_type=jnp.float32)
        return jnp.exp(ALPHA * (similarity - 1.0)).reshape(block_anchors, R, NCOL)

    def forward_block(anchor_block):
        lifted = tissue * patch_norm * kernel_of(anchor_block)
        pooled = pool_both(jnp.pad(lifted, ((0, 0), (0, 0), (4, 4))), weights, NCOL // 2)
        return (pooled / density).astype(jnp.bfloat16)
    whitened_in = lax.map(forward_block, anchor_blocks).reshape(CH, -1)
    flat_cot = cotangent.reshape(CH, -1)
    grad_whiten = lax.dot_general(flat_cot, whitened_in, (((1,), (1,)), ((), ())), preferred_element_type=jnp.float32)
    pooled_grad = lax.dot_general(whiten, flat_cot, (((0,), (0,)), ((), ())), preferred_element_type=jnp.float32).astype(jnp.bfloat16)
    pooled_grad = pooled_grad.reshape(blocks, block_anchors, R // 2, NCOL // 2)

    def backward_block(total, inputs):
        anchor_block, grad_block = inputs
        scaled = grad_block.astype(jnp.float32) / density
        stacked = jnp.stack([scaled, jnp.zeros_like(scaled)], axis=3).reshape(block_anchors, R // 2, NCOL)
        stacked = jnp.pad(stacked, ((0, 0), (0, 0), (4, 4)))
        spread = spread_columns(stacked, NCOL, 4)
        spread = jnp.einsum('ai,caj->cij', weights, spread)
        kernel_grad = (spread * patch_norm * tissue * ALPHA * kernel_of(anchor_block)).astype(jnp.bfloat16)
        kernel_grad = kernel_grad.reshape(block_anchors, -1)
        anchor_grad = lax.dot_general(kernel_grad, unit_low, (((1,), (1,)), ((), ())), preferred_element_type=jnp.float32)
        unit_grad = lax.dot_general(anchor_block, kernel_grad, (((0,), (0,)), ((), ())), preferred_element_type=jnp.float32)
        return (total + unit_grad, anchor_grad)
    unit_grad, anchor_grads = lax.scan(backward_block, jnp.zeros((75, R * NCOL), jnp.float32), (anchor_blocks, pooled_grad))
    unit_grad = unit_grad.reshape(75, R, NCOL)
    patch_grad = (unit_grad - unit_patch * lax.optimization_barrier(jnp.sum(unit_patch * unit_grad, axis=0))) / patch_norm
    grad_image = scatter_patches(jnp.pad(patch_grad, ((0, 0), (2, 2), (2, 2))), R, NCOL, 2)
    return (anchor_grads.reshape(CH, 75), grad_whiten, grad_image)
```

```python
import functools
import math

import jax
import jax.numpy as jnp
from jax import lax
from jax.experimental import pallas as pl
from jax.experimental.pallas import tpu as pltpu
from jax.sharding import PartitionSpec as P

EPS = 1e-05
RIM = 6
LANES = 384
HALF = 128
ROWS = 32
GROUP = 16
OWN = 64
VMEM = 56 * 1024 * 1024

CHIPS = ((0, 0), (0, 1), (1, 0), (3, 0), (1, 1), (3, 1), (2, 0), (2, 1))

CORE = [(i, i ^ 1) for i in range(16)]
ZED = [(i, i ^ 2) for i in range(16)]
RIGHT = [(i, (i + 4) % 16) for i in range(16)]
LEFT = [(i, (i - 4) % 16) for i in range(16)]

f32 = jnp.float32
bf16 = jnp.bfloat16


def tap(distance):
    return math.exp(-distance * distance / 8.0)


def column_pool():
    lane = lax.broadcasted_iota(jnp.int32, (LANES, HALF), 0)
    target = lax.broadcasted_iota(jnp.int32, (LANES, HALF), 1)
    distance = (2 * target - lane + 4).astype(f32)
    return jnp.where(jnp.abs(distance) <= 4.0, jnp.exp(-distance * distance / 8.0), 0.0).astype(bf16)


def row_pool():
    a = lax.broadcasted_iota(jnp.int32, (ROWS // 2, ROWS), 0)
    i = lax.broadcasted_iota(jnp.int32, (ROWS // 2, ROWS), 1)
    distance = (2 * a - i).astype(f32)
    return jnp.where(jnp.abs(distance) <= 4.0, jnp.exp(-distance * distance / 8.0), 0.0)


def fold_rows():
    out = lax.broadcasted_iota(jnp.int32, (96, 36 * GROUP), 0)
    src = lax.broadcasted_iota(jnp.int32, (96, 36 * GROUP), 1)
    i = 2 * (out // 6) + out % 2
    colour = (out % 6) // 2
    hit = (src // GROUP == i + 2) & ((src % GROUP) // 5 == colour)
    return jnp.where(hit, 1.0, 0.0).astype(bf16)


def forward_kernel(
    blk, rep, mask, anch, pool, rows, wcat,
    patches, masked, whitened, inv_density, inv_square, wturned,
    scale, norm, columned,
):
    x = rep[...].astype(f32)
    offset = (lax.broadcasted_iota(jnp.int32, x.shape, 0) % GROUP) % 5
    s = x
    for b in range(1, 5):
        s = jnp.where(offset == b, pltpu.roll(x, LANES - b, 1), s)
    patches[...] = s.astype(bf16)
    square = jnp.sum((s * s).reshape(36, GROUP, LANES), axis=1)
    total = square[0:ROWS]
    for a in range(1, 5):
        total = total + square[a : a + ROWS]
    total = total + EPS
    root = lax.rsqrt(total)
    scale[...] = 4.0 * root
    norm[...] = total * root
    inv_square[...] = 1.0 / total
    counted = jnp.dot(mask[...].astype(bf16), pool[...], preferred_element_type=f32)
    density = jnp.dot(rows[...], counted, precision=lax.Precision.HIGHEST, preferred_element_type=f32)
    inv_density[...] = 1.0 / jnp.maximum(density, 1.0)

    @pl.loop(0, ROWS)
    def _(i):
        patch = patches[pl.ds(pl.multiple_of(i * GROUP, GROUP), 80), :]
        raw = jnp.dot(anch[...], patch, preferred_element_type=f32)
        value = jnp.exp(raw * scale[pl.ds(i, 1), :] - 4.0) * mask[pl.ds(i, 1), :]
        masked[i] = value.astype(bf16)
        lifted = (value * norm[pl.ds(i, 1), :]).astype(bf16)
        columned[i] = jnp.dot(lifted, pool[...], preferred_element_type=f32)

    for a in range(ROWS // 2):
        acc = None
        for i in range(max(0, 2 * a - 4), min(ROWS, 2 * a + 5)):
            term = tap(2 * a - i) * columned[i]
            acc = term if acc is None else acc + term
        whitened[:, a * HALF : (a + 1) * HALF] = (acc * inv_density[a : a + 1, :]).astype(bf16)

    ordered = jnp.concatenate(
        [wcat[pl.ds(pl.multiple_of(blk[p] * OWN, OWN), OWN), :] for p in range(16)], axis=0
    )
    wturned[...] = ordered.astype(f32).T.astype(bf16)


def fold(block, rows):
    top, low = block[:rows], block[rows:]
    left = lax.broadcasted_iota(jnp.int32, top.shape, 1) < OWN
    own = jnp.where(left, top, pltpu.roll(low, OWN, 1))
    partner = jnp.where(left, pltpu.roll(top, OWN, 1), low)
    return own.astype(bf16), partner.astype(bf16)


def backward_kernel(
    blk, b0, bz, br, bl, bzr, bzl, b2a, b2b, b2za, b2zb,
    wturned, whitened, inv_density, masked, patches, inv_square, anch_t, pool_t, folder,
    own_w, partner_w, own_a, partner_a, image,
    rowed, spread_grad, anchor_grad,
):
    refs = (b0, bz, br, bl, bzr, bzl, b2a, b2b, b2za, b2zb)
    grad_w = None
    pooled = []
    for n in range(8):
        cols = pl.ds(n * 256, 256)
        stack = jnp.concatenate([ref[:, cols] for ref in refs], axis=0)
        pooled.append(jnp.dot(wturned[...], stack, preferred_element_type=f32))
        term = lax.dot_general(
            stack, whitened[:, cols], (((1,), (1,)), ((), ())), preferred_element_type=f32
        )
        grad_w = term if grad_w is None else grad_w + term
    for p in range(16):
        own, partner = fold(grad_w[p * OWN : (p + 1) * OWN], OWN // 2)
        own_w[blk[p]] = own
        partner_w[blk[p]] = partner
    scaled = []
    for a in range(ROWS // 2):
        part = pooled[a // 2][:, (a % 2) * HALF : (a % 2 + 1) * HALF]
        scaled.append(part.astype(bf16).astype(f32) * inv_density[a : a + 1, :])
    for i in range(ROWS):
        acc = None
        for a in range(ROWS // 2):
            if abs(2 * a - i) <= 4:
                term = (4.0 * tap(2 * a - i)) * scaled[a]
                acc = term if acc is None else acc + term
        rowed[i] = acc.astype(bf16)
    spread_grad[...] = jnp.zeros_like(spread_grad)
    anchor_grad[...] = jnp.zeros_like(anchor_grad)

    @pl.loop(0, ROWS)
    def _(i):
        here = pl.ds(pl.multiple_of(i * GROUP, GROUP), 80)
        spread = jnp.dot(rowed[i], pool_t[...], preferred_element_type=f32)
        grad = (spread * masked[i].astype(f32)).astype(bf16)
        patch = patches[here, :]
        anchor_grad[...] += lax.dot_general(
            patch, grad, (((1,), (1,)), ((), ())), preferred_element_type=f32
        )
        unit = jnp.dot(anch_t[...], grad, preferred_element_type=f32)
        wide = patch.astype(f32)
        along = jnp.sum(wide * unit, axis=0, keepdims=True) * inv_square[pl.ds(i, 1), :]
        spread_grad[here, :] += unit - wide * along

    own, partner = fold(anchor_grad[...], 40)
    own_a[...] = own
    partner_a[...] = partner
    t = spread_grad[...]
    offset = (lax.broadcasted_iota(jnp.int32, t.shape, 0) % GROUP) % 5
    moved = t
    for b in range(1, 5):
        moved = jnp.where(offset == b, pltpu.roll(t, b, 1), moved)
    high = moved.astype(bf16)
    low = (moved - high.astype(f32)).astype(bf16)
    image[...] = (
        jnp.dot(folder[...], high, preferred_element_type=f32)
        + jnp.dot(folder[...], low, preferred_element_type=f32)
    ).astype(bf16)


def call(kernel, outs, scratch, flops, bytes_accessed, *args):
    specs = [pl.BlockSpec(memory_space=pltpu.SMEM)]
    specs += [pl.BlockSpec(memory_space=pltpu.VMEM)] * (len(args) - 1)
    return pl.pallas_call(
        kernel,
        out_shape=[jax.ShapeDtypeStruct(shape, dtype) for shape, dtype in outs],
        in_specs=specs,
        out_specs=[pl.BlockSpec(memory_space=pltpu.VMEM)] * len(outs),
        scratch_shapes=[pltpu.VMEM(shape, dtype) for shape, dtype in scratch],
        compiler_params=pltpu.CompilerParams(vmem_limit_bytes=VMEM),
        cost_estimate=pl.CostEstimate(
            flops=flops, bytes_accessed=bytes_accessed, transcendentals=ROWS * 128 * LANES
        ),
    )(*args)


def neighbours(first, last, axis):
    count = lax.axis_size(axis)
    up = [(i, i + 1) for i in range(count - 1)]
    down = [(i + 1, i) for i in range(count - 1)]
    return lax.ppermute(last, axis, up), lax.ppermute(first, axis, down)


def shards(image, mask, anchors, whiten, cotangent):
    chan = lax.axis_index("chan")
    core = chan % 2
    zed = (chan // 2) % 2
    ex = chan // 4
    blk = jnp.stack(
        [((ex + dx) % 4) * 4 + (zed ^ dz) * 2 + (core ^ o) for dx, dz in CHIPS for o in (0, 1)]
    ).astype(jnp.int32)

    left, right = cotangent[:, :, :HALF], cotangent[:, :, HALF:]
    own = jnp.where(core == 0, left, right).reshape(OWN, -1)
    away = jnp.where(core == 0, right, left).reshape(OWN, -1)
    b0 = jnp.concatenate([own, lax.ppermute(away, "chan", CORE)], axis=0)
    bz = lax.ppermute(b0, "chan", ZED)
    bl = lax.ppermute(b0, "chan", RIGHT)
    br = lax.ppermute(b0, "chan", LEFT)
    b2a = lax.ppermute(bl[:OWN], "chan", RIGHT)
    b2b = lax.ppermute(br[OWN:], "chan", LEFT)
    bzl = lax.ppermute(bz, "chan", RIGHT)
    bzr = lax.ppermute(bz, "chan", LEFT)
    b2za = lax.ppermute(b2a, "chan", ZED)
    b2zb = lax.ppermute(b2b, "chan", ZED)

    stacked = jnp.concatenate([image, mask.astype(bf16)[None]], axis=0)
    width = stacked.shape[2]
    before, after = neighbours(stacked[:, :, :RIM], stacked[:, :, width - RIM :], "space")
    first = jnp.concatenate([before, stacked[:, :, : 256 + RIM]], axis=2)
    second = jnp.concatenate([stacked[:, :, 256 - RIM :], after], axis=2)
    extended = jnp.where(core == 0, first, second)
    extended = jnp.pad(extended, ((0, 0), (0, 0), (0, LANES - 256 - 2 * RIM)))
    tissue = jnp.pad(extended[3, :, 2:], ((0, 0), (0, 2))).astype(f32)
    tall = jnp.pad(jnp.transpose(extended[:3], (1, 0, 2)), ((2, 2), (0, 0), (0, 0)))
    rep = jnp.broadcast_to(tall[:, :, None, :], (36, 3, 5, LANES)).reshape(36, 15, LANES)
    rep = jnp.pad(rep, ((0, 0), (0, 1), (0, 0))).reshape(36 * GROUP, LANES)

    turned = jnp.transpose(anchors.reshape(OWN, 3, 5, 5), (0, 2, 1, 3)).reshape(OWN, 5, 15)
    turned = jnp.pad(turned, ((0, 0), (0, 0), (0, 1))).reshape(OWN, 80)
    anch = jnp.concatenate([turned, lax.ppermute(turned, "chan", CORE)], axis=0)
    wcat = jnp.concatenate([whiten, lax.ppermute(whiten, "chan", CORE)], axis=1)

    pool = column_pool()
    patches, masked, whitened, inv_density, inv_square, wturned = call(
        forward_kernel,
        [
            ((36 * GROUP, LANES), bf16),
            ((ROWS, 128, LANES), bf16),
            ((128, 16 * HALF), bf16),
            ((16, HALF), f32),
            ((ROWS, LANES), f32),
            ((128, 1024), bf16),
        ],
        [((ROWS, LANES), f32), ((ROWS, LANES), f32), ((ROWS, 128, HALF), f32)],
        4_000_000_000,
        6_000_000,
        blk, rep, tissue, anch, pool, row_pool(), wcat,
    )
    own_w, partner_w, own_a, partner_a, image_part = call(
        backward_kernel,
        [
            ((16, 32, 128), bf16),
            ((16, 32, 128), bf16),
            ((40, 128), bf16),
            ((40, 128), bf16),
            ((96, LANES), bf16),
        ],
        [((ROWS, 128, HALF), bf16), ((36 * GROUP, LANES), f32), ((80, 128), f32)],
        4_000_000_000,
        9_000_000,
        blk, b0, bz, br, bl, bzr, bzl, b2a, b2b, b2za, b2zb,
        wturned, whitened, inv_density, masked, patches, inv_square,
        jnp.transpose(anch), jnp.transpose(pool), fold_rows(),
    )

    send_w = (own_w.astype(f32) + lax.ppermute(partner_w, "chan", CORE).astype(f32)).astype(bf16)
    send_a = (own_a.astype(f32) + lax.ppermute(partner_a, "chan", CORE).astype(f32)).astype(bf16)
    packed = jnp.concatenate([send_w, jnp.broadcast_to(send_a[None], (16, 40, 128))], axis=1)
    summed = jnp.sum(lax.all_to_all(packed, "space", 0, 0).astype(f32), axis=0)
    grad_whiten = jnp.concatenate([summed[:32, :OWN], summed[:32, OWN:]], axis=0)
    turned = jnp.concatenate([summed[32:, :OWN], summed[32:, OWN:]], axis=0)
    turned = turned.reshape(5, GROUP, OWN)[:, :15].reshape(5, 3, 5, OWN)
    grad_anchors = jnp.transpose(turned, (3, 1, 0, 2)).reshape(OWN, 75)

    parts = lax.all_to_all(image_part.reshape(16, 6, LANES), "chan", 0, 0)
    parts = jnp.sum(parts.astype(f32).reshape(8, 2, 6, LANES), axis=0)
    whole = jnp.pad(parts[0], ((0, 0), (0, 256))) + jnp.pad(parts[1], ((0, 0), (256, 0)))
    from_before, from_after = neighbours(
        whole[:, :RIM], whole[:, RIM + width : 2 * RIM + width], "space"
    )
    middle = jnp.zeros((6, width - 2 * RIM), f32)
    rims = jnp.concatenate([from_before, middle, from_after], axis=1)
    grad_image = (whole[:, RIM : RIM + width] + rims).reshape(3, 2, width)
    return (grad_anchors, grad_whiten, grad_image)


def solution(mesh):
    placed = (
        P(None, None, "space"),
        P(None, "space"),
        P("chan", None),
        P(None, "chan"),
        P("chan", None, "space"),
    )
    return jax.shard_map(
        shards,
        mesh=mesh,
        in_specs=placed,
        out_specs=(P("chan", None), P("space", "chan"), P(None, "chan", "space")),
        check_vma=False,
    )
```

```python
import math

import jax
import jax.numpy as jnp
import ml_dtypes
import numpy as np
from jax import lax
from jax.experimental import pallas as pl
from jax.experimental.pallas import tpu as pltpu
from jax.sharding import PartitionSpec as P

EPS = 1e-05
LANES = 384
HALF = 128
ROWS = 32
GROUP = 16
OWN = 64
STEP = 4
VMEM = 56 * 1024 * 1024

CHIPS = ((0, 0), (0, 1), (1, 0), (3, 0), (1, 1), (3, 1), (2, 0), (2, 1))


def route(dx, dz, core):
    return [(i, ((i // 4 + dx) % 4) * 4 + ((i // 2) % 2 ^ dz) * 2 + (i % 2 ^ core)) for i in range(16)]


f32 = jnp.float32
bf16 = jnp.bfloat16


def tap(distance):
    return math.exp(-distance * distance / 8.0) if abs(distance) <= 4 else 0.0


def as_bf16(array):
    return array.astype(ml_dtypes.bfloat16)


def column_pool():
    return np.array([[tap(2 * b - l + 4) for b in range(HALF)] for l in range(LANES)], np.float32)


def row_pool():
    return np.array([[tap(2 * a - i) for i in range(ROWS)] for a in range(ROWS // 2)], np.float32)


def replicate_rows():
    out = np.zeros((36, GROUP, 3, ROWS), np.float32)
    for i in range(ROWS):
        for q in range(15):
            out[i + 2, q, q // 5, i] = 1.0
    return out.reshape(36 * GROUP, 96)


def fold_rows():
    out = np.zeros((128, 36, GROUP), np.float32)
    for i in range(ROWS):
        for q in range(15):
            out[8 * (i // 2) + 2 * (q // 5) + i % 2, i + 2, q] = 1.0
    return out.reshape(128, 36 * GROUP)


def entry_order():
    out = np.zeros((75, 80), np.float32)
    for c in range(3):
        for a in range(5):
            for b in range(5):
                out[25 * c + 5 * a + b, GROUP * a + 5 * c + b] = 1.0
    return out


def block_of(p):
    chan = lax.axis_index("chan")
    dx, dz = CHIPS[p // 2]
    ex = lax.rem(chan // 4 + dx, 4)
    zed = lax.rem(chan // 2 + dz, 2)
    core = lax.rem(chan + p % 2, 2)
    return ex * 4 + zed * 2 + core


def dot(a, b):
    return jnp.dot(a, b, preferred_element_type=f32)


def dot_nt(a, b):
    return lax.dot_general(a, b, (((1,), (1,)), ((), ())), preferred_element_type=f32)


def forward_kernel(
    image, mask, before, after, anch_own, anch_partner, w_own, w_partner, pool, rows, repeat, order,
    patches, masked, whitened, inv_density, inv_square, wturned, anch_t,
    scale, norm, tissue, columned,
):
    second = lax.rem(lax.axis_index("chan"), 2) == 1

    def half(left, middle, right, shift):
        wide = jnp.concatenate([left, middle, right], axis=1)
        part = jnp.where(second, wide[:, 256:], wide[:, :512])
        return pltpu.roll(part, 512 - shift, 1)[:, :LANES]

    colours = [
        half(before[c].astype(f32), image[c].astype(f32), after[c].astype(f32), 122) for c in range(3)
    ]
    here = half(before[3].astype(f32), mask[...].astype(f32), after[3].astype(f32), 124)
    lane = lax.broadcasted_iota(jnp.int32, here.shape, 1)
    here = jnp.where(lane < 263, here, 0.0)
    tissue[...] = here
    x = dot(repeat[...], jnp.concatenate(colours, axis=0).astype(bf16))
    offset = (lax.broadcasted_iota(jnp.int32, x.shape, 0) % GROUP) % 5
    s = x
    for b in range(1, 5):
        s = jnp.where(offset == b, pltpu.roll(x, LANES - b, 1), s)
    patches[...] = s.astype(bf16)
    square = jnp.sum((s * s).reshape(36, GROUP, LANES), axis=1)
    total = square[0:ROWS]
    for a in range(1, 5):
        total = total + square[a : a + ROWS]
    total = total + EPS
    root = lax.rsqrt(total)
    scale[...] = 4.0 * root
    norm[...] = total * root
    inv_square[...] = 1.0 / total
    counted = dot(here.astype(bf16), pool[...])
    density = jnp.dot(rows[...], counted, precision=lax.Precision.HIGHEST, preferred_element_type=f32)
    inv_density[...] = 1.0 / jnp.maximum(density, 1.0)
    both = jnp.concatenate([anch_own[...], anch_partner[...]], axis=0)
    anch = dot(both, order[...]).astype(bf16)
    anch_t[...] = anch.astype(f32).T.astype(bf16)

    @pl.loop(0, ROWS // STEP)
    def _(t):
        lifted = []
        for r in range(STEP):
            i = t * STEP + r
            patch = patches[pl.ds(pl.multiple_of(i * GROUP, GROUP), 80), :]
            raw = dot(anch, patch)
            value = jnp.exp(raw * scale[pl.ds(i, 1), :] - 4.0) * tissue[pl.ds(i, 1), :]
            masked[i] = value.astype(bf16)
            lifted.append((value * norm[pl.ds(i, 1), :]).astype(bf16))
        result = dot(jnp.concatenate(lifted, axis=0), pool[...])
        columned[pl.ds(t * STEP, STEP)] = result.reshape(STEP, 128, HALF)

    for a in range(ROWS // 2):
        acc = None
        for i in range(max(0, 2 * a - 4), min(ROWS, 2 * a + 5)):
            term = tap(2 * a - i) * columned[i]
            acc = term if acc is None else acc + term
        whitened[:, a * HALF : (a + 1) * HALF] = (acc * inv_density[a : a + 1, :]).astype(bf16)

    blocks = [pl.ds(pl.multiple_of(block_of(p) * OWN, OWN), OWN) for p in range(16)]
    for at, weights in ((0, w_own), (OWN, w_partner)):
        ordered = jnp.concatenate([weights[block, :] for block in blocks], axis=0)
        wturned[at : at + OWN, :] = ordered.astype(f32).T.astype(bf16)


def fold(block, rows):
    top, low = block[:rows], block[rows:]
    left = lax.broadcasted_iota(jnp.int32, top.shape, 1) < OWN
    own = jnp.where(left, top, pltpu.roll(low, OWN, 1))
    partner = jnp.where(left, pltpu.roll(top, OWN, 1), low)
    return own.astype(bf16), partner.astype(bf16)


def backward_kernel(*refs):
    blocks = refs[:16]
    (
        wturned, whitened, inv_density, masked, patches, inv_square, anch_t, pool_t, folder,
        own, partner, image,
        rowed, spread_grad, anchor_grad,
    ) = refs[16:]
    grad_w = None
    pooled = []
    for n in range(8):
        cols = pl.ds(n * 256, 256)
        stack = jnp.concatenate([block[:, cols] for block in blocks], axis=0)
        pooled.append(dot(wturned[...], stack))
        term = dot_nt(stack, whitened[:, cols])
        grad_w = term if grad_w is None else grad_w + term
    for p in range(16):
        mine, theirs = fold(grad_w[p * OWN : (p + 1) * OWN], OWN // 2)
        rows = pl.ds(pl.multiple_of(block_of(p) * 32, 32), 32)
        own[rows, :] = mine
        partner[rows, :] = theirs
    scaled = []
    for a in range(ROWS // 2):
        part = pooled[a // 2][:, (a % 2) * HALF : (a % 2 + 1) * HALF]
        scaled.append(part.astype(bf16).astype(f32) * inv_density[a : a + 1, :])
    for i in range(ROWS):
        acc = None
        for a in range(ROWS // 2):
            if abs(2 * a - i) <= 4:
                term = (4.0 * tap(2 * a - i)) * scaled[a]
                acc = term if acc is None else acc + term
        rowed[i * 128 : (i + 1) * 128, :] = acc.astype(bf16)
    spread_grad[...] = jnp.zeros_like(spread_grad)
    anchor_grad[...] = jnp.zeros_like(anchor_grad)

    @pl.loop(0, ROWS // STEP)
    def _(t):
        start = pl.multiple_of(t * (STEP * 128), STEP * 128)
        spread = dot(rowed[pl.ds(start, STEP * 128), :], pool_t[...])
        grads, wides, units = [], [], []
        for r in range(STEP):
            i = t * STEP + r
            patch = patches[pl.ds(pl.multiple_of(i * GROUP, GROUP), 80), :]
            grad = (spread[r * 128 : (r + 1) * 128] * masked[i].astype(f32)).astype(bf16)
            unit = dot(anch_t[...], grad)
            wide = patch.astype(f32)
            along = jnp.sum(wide * unit, axis=0, keepdims=True) * inv_square[pl.ds(i, 1), :]
            units.append(unit - wide * along)
            grads.append(grad)
            wides.append(patch)
        anchor_grad[...] += dot_nt(jnp.concatenate(wides, axis=1), jnp.concatenate(grads, axis=1))
        sums = []
        for g in range(STEP + 4):
            acc = None
            for r in range(STEP):
                if 0 <= g - r < 5:
                    term = units[r][(g - r) * GROUP : (g - r + 1) * GROUP]
                    acc = term if acc is None else acc + term
            sums.append(acc)
        here = pl.ds(pl.multiple_of(t * (STEP * GROUP), STEP * GROUP), (STEP + 4) * GROUP)
        spread_grad[here, :] += jnp.concatenate(sums, axis=0)

    mine, theirs = fold(anchor_grad[...], 40)
    own[512:552, :] = mine
    partner[512:552, :] = theirs
    own[552:560, :] = jnp.zeros((8, 128), bf16)
    partner[552:560, :] = jnp.zeros((8, 128), bf16)
    t = spread_grad[...]
    offset = (lax.broadcasted_iota(jnp.int32, t.shape, 0) % GROUP) % 5
    moved = t
    for b in range(1, 5):
        moved = jnp.where(offset == b, pltpu.roll(t, b, 1), moved)
    high = moved.astype(bf16)
    low = (moved - high.astype(f32)).astype(bf16)
    image[...] = (dot(folder[...], high) + dot(folder[...], low)).astype(bf16)


def pack_kernel(own, partner, parts, packed, middle):
    space = lax.axis_index("space")
    total = (own[...].astype(f32) + partner[...].astype(f32)).astype(bf16)
    halves = []
    for k in range(2):
        acc = parts[k].astype(f32)
        for chip in range(1, 8):
            acc = acc + parts[2 * chip + k].astype(f32)
        halves.append(acc)
    gap = jnp.zeros((8, 256), f32)
    whole = jnp.concatenate([halves[0], gap], axis=1) + jnp.concatenate([gap, halves[1]], axis=1)
    turned = pltpu.roll(whole, 640 - 6, 1)
    middle[...] = turned[:, :512]
    rims = turned[:, 512:]
    lane = lax.broadcasted_iota(jnp.int32, rims.shape, 1)
    for strip in range(16):
        to_next = jnp.where(space + 1 == strip, jnp.where(lane < 6, rims, 0.0), 0.0)
        to_last = jnp.where(space - 1 == strip, jnp.where(lane >= 122, rims, 0.0), 0.0)
        tail = jnp.concatenate([total[512:552].astype(f32), to_next + to_last], axis=0)
        packed[strip, 0:32, :] = total[strip * 32 : (strip + 1) * 32]
        packed[strip, 32:80, :] = tail.astype(bf16)


def unpack_kernel(received, middle, order, grad_anchors, grad_whiten, grad_image):
    total = received[0].astype(f32)
    for strip in range(1, 16):
        total = total + received[strip].astype(f32)
    other = pltpu.roll(total, OWN, 1)
    grad_whiten[0:32, :] = total[0:32, :OWN]
    grad_whiten[32:64, :] = other[0:32, :OWN]
    turned = jnp.concatenate([total[32:72], other[32:72]], axis=0).T[:OWN]
    grad_anchors[...] = lax.dot_general(
        turned, order[...], (((1,), (1,)), ((), ())),
        precision=lax.Precision.HIGHEST, preferred_element_type=f32,
    )
    rims = total[72:80]
    lane = lax.broadcasted_iota(jnp.int32, rims.shape, 1)
    first = jnp.where(lane < 6, rims, 0.0)
    last = jnp.where(lane >= 122, rims, 0.0)
    gap = jnp.zeros((8, 256), f32)
    image = middle[...] + jnp.concatenate([first, gap, last], axis=1)
    for colour in range(3):
        grad_image[colour] = image[2 * colour : 2 * colour + 2]


def call(kernel, outs, scratch, flops, *args):
    size = lambda shape, dtype: math.prod(shape) * jnp.dtype(dtype).itemsize
    moved = sum(size(a.shape, a.dtype) for a in args) + sum(size(*out) for out in outs)
    return pl.pallas_call(
        kernel,
        out_shape=[jax.ShapeDtypeStruct(shape, dtype) for shape, dtype in outs],
        in_specs=[pl.BlockSpec(memory_space=pltpu.VMEM)] * len(args),
        out_specs=[pl.BlockSpec(memory_space=pltpu.VMEM)] * len(outs),
        scratch_shapes=[pltpu.VMEM(shape, dtype) for shape, dtype in scratch],
        compiler_params=pltpu.CompilerParams(vmem_limit_bytes=VMEM),
        cost_estimate=pl.CostEstimate(flops=flops, bytes_accessed=moved, transcendentals=0),
    )(*args)


def shards(image, mask, anchors, whiten, cotangent):
    core = lax.axis_index("chan") % 2

    def send(value, dx, dz, other):
        return lax.ppermute(value, "chan", route(dx, dz, other))

    left, right = cotangent[:, :, :HALF], cotangent[:, :, HALF:]
    own = jnp.where(core == 0, left, right).reshape(OWN, -1)
    away = jnp.where(core == 0, right, left).reshape(OWN, -1)
    held = {(0, 0): (own, send(away, 0, 0, 1))}
    for dx, dz in ((1, 0), (3, 0), (0, 1)):
        held[(4 - dx) % 4, dz] = (send(own, dx, dz, 0), send(away, dx, dz, 1))
    far_own = send(held[0, 1][0], 1, 0, 0)
    far_partner = send(held[0, 1][1], 3, 0, 0)
    held[3, 1] = (far_own, send(held[3, 0][1], 0, 1, 0))
    held[1, 1] = (send(held[1, 0][0], 0, 1, 0), far_partner)
    held[2, 0] = (send(held[3, 0][0], 1, 0, 0), send(held[1, 0][1], 3, 0, 0))
    held[2, 1] = (send(far_own, 1, 0, 0), send(far_partner, 3, 0, 0))
    blocks = [block for chip in CHIPS for block in held[chip]]

    width = mask.shape[1]
    tiles = [
        jnp.concatenate([image[:, :, part], mask[None, :, part].astype(bf16)], axis=0)
        for part in (slice(0, 128), slice(width - 128, width))
    ]
    count = lax.axis_size("space")
    before = lax.ppermute(tiles[1], "space", [(i, i + 1) for i in range(count - 1)])
    after = lax.ppermute(tiles[0], "space", [(i + 1, i) for i in range(count - 1)])

    pool = as_bf16(column_pool())
    order = entry_order()
    patches, masked, whitened, inv_density, inv_square, wturned, anch_t = call(
        forward_kernel,
        [
            ((36 * GROUP, LANES), bf16),
            ((ROWS, 128, LANES), bf16),
            ((128, 16 * HALF), bf16),
            ((16, HALF), f32),
            ((ROWS, LANES), f32),
            ((128, 1024), bf16),
            ((80, 128), bf16),
        ],
        [
            ((ROWS, LANES), f32),
            ((ROWS, LANES), f32),
            ((ROWS, LANES), f32),
            ((ROWS, 128, HALF), f32),
        ],
        6_000_000_000,
        image, mask, before, after, anchors, send(anchors, 0, 0, 1), whiten, send(whiten, 0, 0, 1),
        jnp.asarray(pool), jnp.asarray(row_pool()),
        jnp.asarray(as_bf16(replicate_rows())), jnp.asarray(as_bf16(order)),
    )
    mine, theirs, image_part = call(
        backward_kernel,
        [((560, 128), bf16), ((560, 128), bf16), ((128, LANES), bf16)],
        [((ROWS * 128, HALF), bf16), ((36 * GROUP, LANES), f32), ((80, 128), f32)],
        6_000_000_000,
        *blocks,
        wturned, whitened, inv_density, masked, patches, inv_square, anch_t,
        jnp.asarray(pool.T.copy()), jnp.asarray(as_bf16(fold_rows())),
    )

    parts = lax.all_to_all(image_part.reshape(16, 8, LANES), "chan", 0, 0)
    packed, middle = call(
        pack_kernel,
        [((16, 80, 128), bf16), ((8, 512), f32)],
        [],
        1_000_000,
        mine, send(theirs, 0, 0, 1), parts,
    )
    received = lax.all_to_all(packed, "space", 0, 0)
    return call(
        unpack_kernel,
        [((OWN, 75), f32), ((OWN, OWN), f32), ((3, 2, 512), f32)],
        [],
        1_000_000,
        received, middle, jnp.asarray(order),
    )


def solution(mesh):
    placed = (
        P(None, None, "space"),
        P(None, "space"),
        P("chan", None),
        P(None, "chan"),
        P("chan", None, "space"),
    )
    return jax.shard_map(
        lambda *args: tuple(shards(*args)),
        mesh=mesh,
        in_specs=placed,
        out_specs=(P("chan", None), P("space", "chan"), P(None, "chan", "space")),
        check_vma=False,
    )
```

```python
import math

import jax
import jax.numpy as jnp
import ml_dtypes
import numpy as np
from jax import lax
from jax.experimental import pallas as pl
from jax.experimental.pallas import tpu as pltpu
from jax.sharding import Mesh
from jax.sharding import PartitionSpec as P

EPS = 1e-05
LANES = 384
HALF = 128
ROWS = 32
GROUP = 16
OWN = 64
STEP = 4
MIB = 1024 * 1024

CHIPS = ((0, 0), (0, 1), (1, 0), (3, 0), (1, 1), (3, 1), (2, 0), (2, 1))


STRIPS = ("z_hi", "y")
CHAN = ("x", "z_lo", "core")


def route(dx, dz, core):
    return [(i, ((i // 4 + dx) % 4) * 4 + ((i // 2) % 2 ^ dz) * 2 + (i % 2 ^ core)) for i in range(16)]


def seams():
    pairs = [(16 * s + 2 * q, 16 * s - 16 + 2 * q + 1) for s in range(1, 16) for q in range(8)]
    return pairs + [(b, a) for a, b in pairs]


f32 = jnp.float32
bf16 = jnp.bfloat16


def tap(distance):
    return math.exp(-distance * distance / 8.0) if abs(distance) <= 4 else 0.0


def as_bf16(array):
    return array.astype(ml_dtypes.bfloat16)


def column_pool():
    return np.array([[tap(2 * b - l + 4) for b in range(HALF)] for l in range(LANES)], np.float32)


def row_pool():
    return np.array([[tap(2 * a - i) for i in range(ROWS)] for a in range(ROWS // 2)], np.float32)


def replicate_rows():
    out = np.zeros((36, GROUP, 3, ROWS), np.float32)
    for i in range(ROWS):
        for q in range(15):
            out[i + 2, q, q // 5, i] = 1.0
    return out.reshape(36 * GROUP, 96)


def fold_rows():
    out = np.zeros((128, 36, GROUP), np.float32)
    for i in range(ROWS):
        for q in range(15):
            out[8 * (i // 2) + 2 * (q // 5) + i % 2, i + 2, q] = 1.0
    return out.reshape(128, 36 * GROUP)


def entry_order():
    out = np.zeros((75, 80), np.float32)
    for c in range(3):
        for a in range(5):
            for b in range(5):
                out[25 * c + 5 * a + b, GROUP * a + 5 * c + b] = 1.0
    return out


def on_second():
    return lax.axis_index("core") == 1


def block_of(p):
    dx, dz = CHIPS[p // 2]
    ex = lax.rem(lax.axis_index("x") + dx, 4)
    zed = lax.rem(lax.axis_index("z_lo") + dz, 2)
    core = lax.rem(lax.axis_index("core") + p % 2, 2)
    return ex * 4 + zed * 2 + core


def dot(a, b):
    return jnp.dot(a, b, preferred_element_type=f32)


def dot_nt(a, b):
    return lax.dot_general(a, b, (((1,), (1,)), ((), ())), preferred_element_type=f32)


def rim_kernel(image, mask, after, tile):
    del after
    second = on_second()
    for c in range(4):
        value = (image[c] if c < 3 else mask[...]).astype(f32)
        tile[c] = jnp.where(second, value[:, 384:], value[:, :128]).astype(bf16)


def patch_kernel(
    image, mask, beyond, anch_own, anch_partner, w_own, w_partner, pool, rows, repeat, order,
    patches, tissue, scale, norm, inv_square, inv_density, anch, anch_t, wturned,
):
    second = on_second()

    def half(middle, rim, shift):
        wide = jnp.concatenate([rim, middle, rim], axis=1)
        part = jnp.where(second, wide[:, 256:], wide[:, :512])
        return pltpu.roll(part, 512 - shift, 1)[:, :LANES]

    colours = [half(image[c].astype(f32), beyond[c].astype(f32), 122) for c in range(3)]
    here = half(mask[...].astype(f32), beyond[3].astype(f32), 124)
    lane = lax.broadcasted_iota(jnp.int32, here.shape, 1)
    here = jnp.where(lane < 263, here, 0.0)
    tissue[...] = here
    x = dot(repeat[...], jnp.concatenate(colours, axis=0).astype(bf16))
    offset = (lax.broadcasted_iota(jnp.int32, x.shape, 0) % GROUP) % 5
    s = x
    for b in range(1, 5):
        s = jnp.where(offset == b, pltpu.roll(x, LANES - b, 1), s)
    patches[...] = s.astype(bf16)
    square = jnp.sum((s * s).reshape(36, GROUP, LANES), axis=1)
    total = square[0:ROWS]
    for a in range(1, 5):
        total = total + square[a : a + ROWS]
    total = total + EPS
    root = lax.rsqrt(total)
    scale[...] = 4.0 * root
    norm[...] = total * root
    inv_square[...] = 1.0 / total
    counted = dot(here.astype(bf16), pool[...])
    density = jnp.dot(rows[...], counted, precision=lax.Precision.HIGHEST, preferred_element_type=f32)
    inv_density[...] = 1.0 / jnp.maximum(density, 1.0)
    both = jnp.concatenate([anch_own[...], anch_partner[...]], axis=0)
    ordered = dot(both, order[...])
    anch[...] = ordered.astype(bf16)
    anch_t[...] = ordered.T.astype(bf16)
    blocks = [pl.ds(pl.multiple_of(block_of(p) * OWN, OWN), OWN) for p in range(16)]
    for at, weights in ((0, w_own), (OWN, w_partner)):
        ordered = jnp.concatenate([weights[block, :] for block in blocks], axis=0)
        wturned[at : at + OWN, :] = ordered.astype(f32).T.astype(bf16)


def forward_kernel(
    patches, tissue, scale, norm, inv_density, anch, pool,
    masked, whitened,
    columned,
):
    @pl.loop(0, ROWS // STEP)
    def _(t):
        lifted = []
        for r in range(STEP):
            i = t * STEP + r
            patch = patches[pl.ds(pl.multiple_of(i * GROUP, GROUP), 80), :]
            raw = dot(anch[...], patch)
            value = jnp.exp(raw * scale[pl.ds(i, 1), :] - 4.0) * tissue[pl.ds(i, 1), :]
            masked[i] = value.astype(bf16)
            lifted.append((value * norm[pl.ds(i, 1), :]).astype(bf16))
        result = dot(jnp.concatenate(lifted, axis=0), pool[...])
        columned[pl.ds(t * STEP, STEP)] = result.reshape(STEP, 128, HALF)

    for a in range(ROWS // 2):
        acc = None
        for i in range(max(0, 2 * a - 4), min(ROWS, 2 * a + 5)):
            term = tap(2 * a - i) * columned[i]
            acc = term if acc is None else acc + term
        whitened[:, a * HALF : (a + 1) * HALF] = (acc * inv_density[a : a + 1, :]).astype(bf16)


def fold(block, rows):
    top, low = block[:rows], block[rows:]
    left = lax.broadcasted_iota(jnp.int32, top.shape, 1) < OWN
    own = jnp.where(left, top, pltpu.roll(low, OWN, 1))
    partner = jnp.where(left, pltpu.roll(top, OWN, 1), low)
    return own.astype(bf16), partner.astype(bf16)


def backward_kernel(*refs):
    blocks = refs[:16]
    (
        wturned, inv_density, masked, patches, inv_square, anch_t, pool_t, folder,
        anchor_grad, image, rim,
        rowed, spread_grad,
    ) = refs[16:]
    pooled = []
    for n in range(8):
        cols = pl.ds(n * 256, 256)
        stack = jnp.concatenate([block[:, cols] for block in blocks], axis=0)
        pooled.append(dot(wturned[...], stack))
    scaled = []
    for a in range(ROWS // 2):
        part = pooled[a // 2][:, (a % 2) * HALF : (a % 2 + 1) * HALF]
        scaled.append(part.astype(bf16).astype(f32) * inv_density[a : a + 1, :])
    for i in range(ROWS):
        acc = None
        for a in range(ROWS // 2):
            if abs(2 * a - i) <= 4:
                term = (4.0 * tap(2 * a - i)) * scaled[a]
                acc = term if acc is None else acc + term
        rowed[i * 128 : (i + 1) * 128, :] = acc.astype(bf16)
    spread_grad[...] = jnp.zeros_like(spread_grad)
    anchor_grad[...] = jnp.zeros_like(anchor_grad)

    @pl.loop(0, ROWS // STEP)
    def _(t):
        start = pl.multiple_of(t * (STEP * 128), STEP * 128)
        spread = dot(rowed[pl.ds(start, STEP * 128), :], pool_t[...])
        grads, wides, units = [], [], []
        for r in range(STEP):
            i = t * STEP + r
            patch = patches[pl.ds(pl.multiple_of(i * GROUP, GROUP), 80), :]
            grad = (spread[r * 128 : (r + 1) * 128] * masked[i].astype(f32)).astype(bf16)
            unit = dot(anch_t[...], grad)
            wide = patch.astype(f32)
            along = jnp.sum(wide * unit, axis=0, keepdims=True) * inv_square[pl.ds(i, 1), :]
            units.append(unit - wide * along)
            grads.append(grad)
            wides.append(patch)
        anchor_grad[...] += dot_nt(jnp.concatenate(wides, axis=1), jnp.concatenate(grads, axis=1))
        sums = []
        for g in range(STEP + 4):
            acc = None
            for r in range(STEP):
                if 0 <= g - r < 5:
                    term = units[r][(g - r) * GROUP : (g - r + 1) * GROUP]
                    acc = term if acc is None else acc + term
            sums.append(acc)
        here = pl.ds(pl.multiple_of(t * (STEP * GROUP), STEP * GROUP), (STEP + 4) * GROUP)
        spread_grad[here, :] += jnp.concatenate(sums, axis=0)

    t = spread_grad[...]
    offset = (lax.broadcasted_iota(jnp.int32, t.shape, 0) % GROUP) % 5
    moved = t
    for b in range(1, 5):
        moved = jnp.where(offset == b, pltpu.roll(t, b, 1), moved)
    high = moved.astype(bf16)
    low = (moved - high.astype(f32)).astype(bf16)
    summed = dot(folder[...], high) + dot(folder[...], low)
    image[...] = summed.astype(bf16)
    first, last = summed[:, :128], summed[:, 256:]
    lane = lax.broadcasted_iota(jnp.int32, first.shape, 1)
    first, last = jnp.where(lane < 6, first, 0.0), jnp.where(lane < 6, 0.0, last)
    rim[...] = jnp.where(on_second(), last, first).astype(bf16)


def whiten_kernel(*refs):
    blocks = refs[:16]
    whitened, anchor_grad, packed = refs[16:]
    grad_w = None
    for n in range(8):
        cols = pl.ds(n * 256, 256)
        stack = jnp.concatenate([block[:, cols] for block in blocks], axis=0)
        term = dot_nt(stack, whitened[:, cols])
        grad_w = term if grad_w is None else grad_w + term
    core = lax.axis_index("core")
    for p in range(16):
        strip = block_of(p)
        rows = pl.ds(pl.multiple_of((strip // 4) * 32, 32), 32)
        y = lax.rem(strip, 4)
        mine, theirs = fold(grad_w[p * OWN : (p + 1) * OWN], OWN // 2)
        packed[y * 2 + core, rows, :] = mine
        packed[y * 2 + 1 - core, rows, :] = theirs
    mine, theirs = fold(anchor_grad[...], 40)
    pad = jnp.zeros((8, 128), bf16)
    mine = jnp.concatenate([mine, pad], axis=0)
    theirs = jnp.concatenate([theirs, pad], axis=0)
    for y in range(4):
        packed[y * 2 + core, 128:176, :] = mine
        packed[y * 2 + 1 - core, 128:176, :] = theirs


def seam_kernel(image, rim, joined):
    second = on_second()
    value = rim[...].astype(f32)
    first = image[:, :128].astype(f32) + jnp.where(second, 0.0, value)
    last = image[:, 256:].astype(f32) + jnp.where(second, value, 0.0)
    joined[:, :128] = first.astype(bf16)
    joined[:, 128:256] = image[:, 128:256]
    joined[:, 256:] = last.astype(bf16)


def add_up(ref, count):
    total = ref[0].astype(f32)
    for source in range(1, count):
        total = total + ref[source].astype(f32)
    return total


def pack_kernel(received, packed):
    total = add_up(received, 8).astype(bf16)
    for z in range(4):
        packed[z, 0:32, :] = total[z * 32 : (z + 1) * 32]
        packed[z, 32:80, :] = total[128:176]


def unpack_kernel(received, parts, order, grad_anchors, grad_whiten, grad_image):
    total = add_up(received, 4)
    other = pltpu.roll(total, OWN, 1)
    grad_whiten[0:32, :] = total[0:32, :OWN]
    grad_whiten[32:64, :] = other[0:32, :OWN]
    turned = jnp.concatenate([total[32:72], other[32:72]], axis=0).T[:OWN]
    grad_anchors[...] = lax.dot_general(
        turned, order[...], (((1,), (1,)), ((), ())),
        precision=lax.Precision.HIGHEST, preferred_element_type=f32,
    )
    halves = []
    for k in range(2):
        acc = parts[k].astype(f32)
        for chip in range(1, 8):
            acc = acc + parts[2 * chip + k].astype(f32)
        halves.append(acc)
    gap = jnp.zeros((8, 256), f32)
    whole = jnp.concatenate([halves[0], gap], axis=1) + jnp.concatenate([gap, halves[1]], axis=1)
    image = pltpu.roll(whole, 640 - 6, 1)[:, :512]
    for colour in range(3):
        grad_image[colour] = image[2 * colour : 2 * colour + 2]


def call(kernel, outs, scratch, flops, limit, *args, loose=()):
    size = lambda shape, dtype: math.prod(shape) * jnp.dtype(dtype).itemsize
    moved = sum(size(a.shape, a.dtype) for a in args) + sum(size(*out) for out in outs)
    return pl.pallas_call(
        kernel,
        out_shape=[jax.ShapeDtypeStruct(shape, dtype) for shape, dtype in outs],
        in_specs=[
            pl.BlockSpec(memory_space=pl.ANY if n in loose else pltpu.VMEM) for n in range(len(args))
        ],
        out_specs=[pl.BlockSpec(memory_space=pltpu.VMEM)] * len(outs),
        scratch_shapes=[pltpu.VMEM(shape, dtype) for shape, dtype in scratch],
        compiler_params=pltpu.CompilerParams(vmem_limit_bytes=limit * MIB),
        cost_estimate=pl.CostEstimate(flops=flops, bytes_accessed=moved, transcendentals=0),
    )(*args)


def shards(image, mask, anchors, whiten, cotangent):
    second = on_second()

    def send(value, dx, dz, other):
        return lax.ppermute(value, CHAN, route(dx, dz, other))

    def cross(value):
        return lax.ppermute(value, STRIPS + CHAN, seams())

    left, right = cotangent[:, :, :HALF], cotangent[:, :, HALF:]
    own = jnp.where(second, right, left).reshape(OWN, -1)
    away = jnp.where(second, left, right).reshape(OWN, -1)
    held = {(0, 0): (own, send(away, 0, 0, 1))}
    for dx, dz in ((1, 0), (3, 0), (0, 1)):
        held[(4 - dx) % 4, dz] = (send(own, dx, dz, 0), send(away, dx, dz, 1))
    far_own = send(held[0, 1][0], 1, 0, 0)
    far_partner = send(held[0, 1][1], 3, 0, 0)
    held[3, 1] = (far_own, send(held[3, 0][1], 0, 1, 0))
    held[1, 1] = (send(held[1, 0][0], 0, 1, 0), far_partner)
    held[2, 0] = (send(held[3, 0][0], 1, 0, 0), send(held[1, 0][1], 3, 0, 0))
    held[2, 1] = (send(far_own, 1, 0, 0), send(far_partner, 3, 0, 0))
    blocks = [block for chip in CHIPS for block in held[chip]]

    (tile,) = call(
        rim_kernel, [((4, ROWS, 128), bf16)], [], 1_000_000, 4, image, mask, held[0, 0][1], loose=(2,)
    )
    pool = as_bf16(column_pool())
    order = entry_order()
    plane = ((ROWS, LANES), f32)
    patches, tissue, scale, norm, inv_square, inv_density, anch, anch_t, wturned = call(
        patch_kernel,
        [
            ((36 * GROUP, LANES), bf16),
            plane,
            plane,
            plane,
            plane,
            ((16, HALF), f32),
            ((128, 80), bf16),
            ((80, 128), bf16),
            ((128, 1024), bf16),
        ],
        [],
        1_000_000_000,
        12,
        image, mask, cross(tile), anchors, send(anchors, 0, 0, 1), whiten, send(whiten, 0, 0, 1),
        jnp.asarray(pool), jnp.asarray(row_pool()),
        jnp.asarray(as_bf16(replicate_rows())), jnp.asarray(as_bf16(order)),
    )
    masked, whitened = call(
        forward_kernel,
        [((ROWS, 128, LANES), bf16), ((128, 16 * HALF), bf16)],
        [((ROWS, 128, HALF), f32)],
        3_000_000_000,
        14,
        patches, tissue, scale, norm, inv_density, anch, jnp.asarray(pool),
    )
    anchor_grad, image_part, rim = call(
        backward_kernel,
        [((80, 128), f32), ((128, LANES), bf16), ((128, 128), bf16)],
        [((ROWS * 128, HALF), bf16), ((36 * GROUP, LANES), f32)],
        5_000_000_000,
        20,
        *blocks,
        wturned, inv_density, masked, patches, inv_square, anch_t,
        jnp.asarray(pool.T.copy()), jnp.asarray(as_bf16(fold_rows())),
    )
    rim = cross(rim)
    (packed,) = call(
        whiten_kernel, [((8, 176, 128), bf16)], [], 2_000_000_000, 12, *blocks, whitened, anchor_grad
    )
    (joined,) = call(seam_kernel, [((128, LANES), bf16)], [], 1_000_000, 4, image_part, rim)

    received = lax.all_to_all(packed, ("y", "core"), 0, 0)
    parts = lax.all_to_all(joined.reshape(16, 8, LANES), CHAN, 0, 0)
    (packed,) = call(pack_kernel, [((4, 80, 128), bf16)], [], 1_000_000, 4, received)
    received = lax.all_to_all(packed, "z_hi", 0, 0)
    return call(
        unpack_kernel,
        [((OWN, 75), f32), ((OWN, OWN), f32), ((3, 2, 512), f32)],
        [],
        1_000_000,
        8,
        received, parts, jnp.asarray(order),
    )


def solution(mesh):
    fine = Mesh(mesh.devices.reshape(4, 4, 4, 2, 2), STRIPS + CHAN)
    placed = (
        P(None, None, STRIPS),
        P(None, STRIPS),
        P(CHAN, None),
        P(None, CHAN),
        P(CHAN, None, STRIPS),
    )
    return jax.shard_map(
        lambda *args: tuple(shards(*args)),
        mesh=fine,
        in_specs=placed,
        out_specs=(P(CHAN, None), P(STRIPS, CHAN), P(None, CHAN, STRIPS)),
        check_vma=False,
    )
```

```python
import math

import jax
import jax.numpy as jnp
from jax import lax
from jax.experimental import pallas as pl
from jax.experimental.pallas import tpu as pltpu
from jax.sharding import Mesh
from jax.sharding import PartitionSpec as P

EPS = 1e-05
LANES = 384
HALF = 128
ROWS = 32
GROUP = 16
OWN = 64
STEP = 4
EARLY = 14
MIB = 1024 * 1024

CHIPS = ((0, 0), (0, 1), (1, 0), (3, 0), (1, 1), (3, 1), (2, 0), (2, 1))


STRIPS = ("z_hi", "y")
CHAN = ("x", "z_lo", "core")


def route(dx, dz, core):
    return [(i, ((i // 4 + dx) % 4) * 4 + ((i // 2) % 2 ^ dz) * 2 + (i % 2 ^ core)) for i in range(16)]


def seams():
    pairs = [(16 * s + 2 * q, 16 * s - 16 + 2 * q + 1) for s in range(1, 16) for q in range(8)]
    return pairs + [(b, a) for a, b in pairs]


f32 = jnp.float32
bf16 = jnp.bfloat16


def tap(distance):
    return math.exp(-distance * distance / 8.0) if abs(distance) <= 4 else 0.0


def taps(distance):
    far = jnp.abs(distance) > 4
    distance = distance.astype(f32)
    return jnp.where(far, 0.0, jnp.exp(distance * distance * (-1.0 / 8.0)))


def places(shape):
    return tuple(lax.broadcasted_iota(jnp.int32, shape, dim) for dim in (0, 1))


def column_pool():
    lane, target = places((LANES, HALF))
    return taps(2 * target - lane + 4).astype(bf16)


def column_spread():
    target, lane = places((HALF, LANES))
    return taps(2 * target - lane + 4).astype(bf16)


def row_pool():
    a, i = places((ROWS // 2, ROWS))
    return taps(2 * a - i)


def split_group(row):
    q = row & (GROUP - 1)
    colour = jnp.where(q < 5, 0, jnp.where(q < 10, 1, jnp.where(q < 15, 2, 3)))
    return row >> 4, colour, q - 5 * colour


def ones(hit, dtype=bf16):
    return jnp.where(hit, 1.0, 0.0).astype(dtype)


def replicate_rows():
    out, src = places((36 * GROUP, 3 * ROWS))
    r, colour, _ = split_group(out)
    return ones(((src & 31) == r - 2) & ((src >> 5) == colour))


def fold_rows():
    out, src = places((128, 36 * GROUP))
    r, colour, _ = split_group(src)
    i = 2 * (out >> 3) + (out & 1)
    return ones((r == i + 2) & (colour == ((out & 7) >> 1)) & (colour < 3))


def entry_order(dtype, rows=75):
    entry, out = places((rows, 80))
    a, colour, b = split_group(out)
    return ones((entry == 25 * colour + 5 * a + b) & (colour < 3), dtype)


def on_second():
    return lax.axis_index("core") == 1


def block_of(p):
    dx, dz = CHIPS[p // 2]
    ex = lax.rem(lax.axis_index("x") + dx, 4)
    zed = lax.rem(lax.axis_index("z_lo") + dz, 2)
    core = lax.rem(lax.axis_index("core") + p % 2, 2)
    return ex * 4 + zed * 2 + core


def dot(a, b):
    return jnp.dot(a, b, preferred_element_type=f32)


def dot_nt(a, b):
    return lax.dot_general(a, b, (((1,), (1,)), ((), ())), preferred_element_type=f32)


def rim_kernel(stacked, *refs):
    tile = refs[-1]
    second = on_second()
    for c in range(4):
        value = stacked[c].astype(f32)
        tile[c] = jnp.where(second, value[:, 384:], value[:, :128]).astype(bf16)


def patch_kernel(
    stacked, beyond, own_both, partner_both,
    patches, tissue, scale, norm, inv_square, inv_density, anch, anch_t, wturned,
):
    second = on_second()

    def half(c, shift):
        middle, rim = stacked[c].astype(f32), beyond[c].astype(f32)
        wide = jnp.concatenate([rim, middle, rim], axis=1)
        part = jnp.where(second, wide[:, 256:], wide[:, :512])
        return pltpu.roll(part, 512 - shift, 1)[:, :LANES]

    colours = [half(c, 122) for c in range(3)]
    here = half(3, 124)
    lane = lax.broadcasted_iota(jnp.int32, here.shape, 1)
    here = jnp.where(lane < 263, here, 0.0)
    tissue[...] = here
    x = dot(replicate_rows(), jnp.concatenate(colours, axis=0).astype(bf16))
    offset = (lax.broadcasted_iota(jnp.int32, x.shape, 0) % GROUP) % 5
    s = x
    for b in range(1, 5):
        s = jnp.where(offset == b, pltpu.roll(x, LANES - b, 1), s)
    patches[...] = s.astype(bf16)
    square = jnp.sum((s * s).reshape(36, GROUP, LANES), axis=1)
    total = square[0:ROWS]
    for a in range(1, 5):
        total = total + square[a : a + ROWS]
    total = total + EPS
    root = lax.rsqrt(total)
    scale[...] = 4.0 * root
    norm[...] = total * root
    inv_square[...] = 1.0 / total
    counted = dot(here.astype(bf16), column_pool())
    density = jnp.dot(row_pool(), counted, precision=lax.Precision.HIGHEST, preferred_element_type=f32)
    inv_density[...] = 1.0 / jnp.maximum(density, 1.0)
    both = jnp.concatenate([own_both[1024:1088, :], partner_both[1024:1088, :]], axis=0)
    ordered = dot(both, entry_order(bf16, 128))
    anch[...] = ordered.astype(bf16)
    anch_t[...] = ordered.T.astype(bf16)
    blocks = [pl.ds(pl.multiple_of(block_of(p) * OWN, OWN), OWN) for p in range(16)]
    for at, both in ((0, own_both), (OWN, partner_both)):
        ordered = jnp.concatenate([both[block, :] for block in blocks], axis=0)
        wturned[at : at + OWN, :] = ordered.astype(f32).T[:OWN].astype(bf16)


def forward_kernel(
    patches, tissue, scale, norm, inv_density, anch,
    masked, whitened,
    columned, pool,
):
    pool[...] = column_pool()

    @pl.loop(0, ROWS // STEP)
    def _(t):
        lifted = []
        for r in range(STEP):
            i = t * STEP + r
            patch = patches[pl.ds(pl.multiple_of(i * GROUP, GROUP), 80), :]
            raw = dot(anch[...], patch)
            value = jnp.exp(raw * scale[pl.ds(i, 1), :] - 4.0) * tissue[pl.ds(i, 1), :]
            masked[i] = value.astype(bf16)
            lifted.append((value * norm[pl.ds(i, 1), :]).astype(bf16))
        result = dot(jnp.concatenate(lifted, axis=0), pool[...])
        columned[pl.ds(t * STEP, STEP)] = result.reshape(STEP, 128, HALF)

    for a in range(ROWS // 2):
        acc = None
        for i in range(max(0, 2 * a - 4), min(ROWS, 2 * a + 5)):
            term = tap(2 * a - i) * columned[i]
            acc = term if acc is None else acc + term
        whitened[:, a * HALF : (a + 1) * HALF] = (acc * inv_density[a : a + 1, :]).astype(bf16)


def fold(block, rows):
    top, low = block[:rows], block[rows:]
    left = lax.broadcasted_iota(jnp.int32, top.shape, 1) < OWN
    own = jnp.where(left, top, pltpu.roll(low, OWN, 1))
    partner = jnp.where(left, pltpu.roll(top, OWN, 1), low)
    return own.astype(bf16), partner.astype(bf16)


def gather_products(blocks, first, wturned, whitened, partial):
    grad_w, pooled = None, []
    weights = wturned[:, first * OWN : (first + len(blocks)) * OWN]
    for n in range(8):
        cols = pl.ds(n * 256, 256)
        stack = jnp.concatenate([block[:, cols] for block in blocks], axis=0)
        term = dot(weights, stack)
        pooled.append(term if partial is None else term + partial[:, cols])
        term = dot_nt(stack, whitened[:, cols])
        grad_w = term if grad_w is None else grad_w + term
    return pooled, grad_w


def place_rows(packed, grad_w, first):
    core = lax.axis_index("core")
    for n in range(grad_w.shape[0] // OWN):
        strip = block_of(first + n)
        rows = pl.ds(pl.multiple_of((strip // 4) * 32, 32), 32)
        y = lax.rem(strip, 4)
        mine, theirs = fold(grad_w[n * OWN : (n + 1) * OWN], OWN // 2)
        packed[y * 2 + core, rows, :] = mine
        packed[y * 2 + 1 - core, rows, :] = theirs


def early_kernel(*refs):
    blocks = refs[:EARLY]
    wturned, whitened, partial, packed = refs[EARLY:]
    packed[...] = jnp.zeros_like(packed)
    pooled, grad_w = gather_products(blocks, 0, wturned, whitened, None)
    for n in range(8):
        partial[:, n * 256 : (n + 1) * 256] = pooled[n]
    place_rows(packed, grad_w, 0)


def backward_kernel(*refs):
    blocks = refs[: 16 - EARLY]
    (
        partial, early, wturned, whitened, inv_density, masked, patches, inv_square, anch_t,
        packed, image, rim,
        rowed, spread_grad, anchor_grad, pool_t,
    ) = refs[16 - EARLY :]
    pool_t[...] = column_spread()
    packed[:, 0:128, :] = early[...]
    pooled, grad_w = gather_products(blocks, EARLY, wturned, whitened, partial)
    place_rows(packed, grad_w, EARLY)
    scaled = []
    for a in range(ROWS // 2):
        part = pooled[a // 2][:, (a % 2) * HALF : (a % 2 + 1) * HALF]
        scaled.append(part.astype(bf16).astype(f32) * inv_density[a : a + 1, :])
    for i in range(ROWS):
        acc = None
        for a in range(ROWS // 2):
            if abs(2 * a - i) <= 4:
                term = (4.0 * tap(2 * a - i)) * scaled[a]
                acc = term if acc is None else acc + term
        rowed[i * 128 : (i + 1) * 128, :] = acc.astype(bf16)
    spread_grad[...] = jnp.zeros_like(spread_grad)
    anchor_grad[...] = jnp.zeros_like(anchor_grad)

    @pl.loop(0, ROWS // STEP)
    def _(t):
        start = pl.multiple_of(t * (STEP * 128), STEP * 128)
        spread = dot(rowed[pl.ds(start, STEP * 128), :], pool_t[...])
        grads, wides, units = [], [], []
        for r in range(STEP):
            i = t * STEP + r
            patch = patches[pl.ds(pl.multiple_of(i * GROUP, GROUP), 80), :]
            grad = (spread[r * 128 : (r + 1) * 128] * masked[i].astype(f32)).astype(bf16)
            unit = dot(anch_t[...], grad)
            wide = patch.astype(f32)
            along = jnp.sum(wide * unit, axis=0, keepdims=True) * inv_square[pl.ds(i, 1), :]
            units.append(unit - wide * along)
            grads.append(grad)
            wides.append(patch)
        anchor_grad[...] += dot_nt(jnp.concatenate(wides, axis=1), jnp.concatenate(grads, axis=1))
        sums = []
        for g in range(STEP + 4):
            acc = None
            for r in range(STEP):
                if 0 <= g - r < 5:
                    term = units[r][(g - r) * GROUP : (g - r + 1) * GROUP]
                    acc = term if acc is None else acc + term
            sums.append(acc)
        here = pl.ds(pl.multiple_of(t * (STEP * GROUP), STEP * GROUP), (STEP + 4) * GROUP)
        spread_grad[here, :] += jnp.concatenate(sums, axis=0)

    core = lax.axis_index("core")
    mine, theirs = fold(anchor_grad[...], 40)
    pad = jnp.zeros((8, 128), bf16)
    mine = jnp.concatenate([mine, pad], axis=0)
    theirs = jnp.concatenate([theirs, pad], axis=0)
    for y in range(4):
        packed[y * 2 + core, 128:176, :] = mine
        packed[y * 2 + 1 - core, 128:176, :] = theirs

    t = spread_grad[...]
    offset = (lax.broadcasted_iota(jnp.int32, t.shape, 0) % GROUP) % 5
    moved = t
    for b in range(1, 5):
        moved = jnp.where(offset == b, pltpu.roll(t, b, 1), moved)
    high = moved.astype(bf16)
    low = (moved - high.astype(f32)).astype(bf16)
    folder = fold_rows()
    summed = dot(folder, high) + dot(folder, low)
    image[...] = summed.astype(bf16)
    first, last = summed[:, :128], summed[:, 256:]
    lane = lax.broadcasted_iota(jnp.int32, first.shape, 1)
    first, last = jnp.where(lane < 6, first, 0.0), jnp.where(lane < 6, 0.0, last)
    rim[...] = jnp.where(on_second(), last, first).astype(bf16)


def seam_kernel(image, rim, joined):
    second = on_second()
    value = rim[...].astype(f32)
    first = image[:, :128].astype(f32) + jnp.where(second, 0.0, value)
    last = image[:, 256:].astype(f32) + jnp.where(second, value, 0.0)
    joined[:, :128] = first.astype(bf16)
    joined[:, 128:256] = image[:, 128:256]
    joined[:, 256:] = last.astype(bf16)


def pack_kernel(received, kept, next_one, next_two, next_three, sums):
    total = received[0].astype(f32)
    for source in range(1, 8):
        total = total + received[source].astype(f32)
    sums[...] = total[0:128]
    anchor = total[128:176].astype(bf16)
    for step, packed in enumerate((kept, next_one, next_two, next_three)):
        z = lax.rem(lax.axis_index("z_hi") + step, 4)
        packed[0:32, :] = sums[pl.ds(pl.multiple_of(z * 32, 32), 32), :].astype(bf16)
        packed[32:80, :] = anchor


def unpack_kernel(kept, one, two, three, grad_anchors, grad_whiten):
    total = sum(ref[...].astype(f32) for ref in (one, two, three)) + kept[...].astype(f32)
    other = pltpu.roll(total, OWN, 1)
    grad_whiten[0:32, :] = total[0:32, :OWN]
    grad_whiten[32:64, :] = other[0:32, :OWN]
    turned = jnp.concatenate([total[32:72], other[32:72]], axis=0).T[:OWN]
    grad_anchors[...] = lax.dot_general(
        turned, entry_order(f32), (((1,), (1,)), ((), ())),
        precision=lax.Precision.HIGHEST, preferred_element_type=f32,
    )


def image_kernel(parts, grad_image):
    halves = []
    for k in range(2):
        acc = parts[k].astype(f32)
        for chip in range(1, 8):
            acc = acc + parts[2 * chip + k].astype(f32)
        halves.append(acc)
    gap = jnp.zeros((8, 256), f32)
    whole = jnp.concatenate([halves[0], gap], axis=1) + jnp.concatenate([gap, halves[1]], axis=1)
    image = pltpu.roll(whole, 640 - 6, 1)[:, :512]
    for colour in range(3):
        grad_image[colour] = image[2 * colour : 2 * colour + 2]


def call(kernel, outs, scratch, flops, limit, *args, loose=0):
    size = lambda shape, dtype: math.prod(shape) * jnp.dtype(dtype).itemsize
    tight = len(args) - loose
    moved = sum(size(a.shape, a.dtype) for a in args[:tight]) + sum(size(*out) for out in outs)
    return pl.pallas_call(
        kernel,
        out_shape=[jax.ShapeDtypeStruct(shape, dtype) for shape, dtype in outs],
        in_specs=[pl.BlockSpec(memory_space=pltpu.VMEM)] * tight
        + [pl.BlockSpec(memory_space=pl.ANY)] * loose,
        out_specs=[pl.BlockSpec(memory_space=pltpu.VMEM)] * len(outs),
        scratch_shapes=[pltpu.VMEM(shape, dtype) for shape, dtype in scratch],
        compiler_params=pltpu.CompilerParams(vmem_limit_bytes=limit * MIB),
        cost_estimate=pl.CostEstimate(flops=flops, bytes_accessed=moved, transcendentals=0),
    )(*args)


def shards(image, mask, anchors, whiten, cotangent):
    second = on_second()

    def send(value, dx, dz, other):
        return lax.ppermute(value, CHAN, route(dx, dz, other))

    def cross(value):
        return lax.ppermute(value, STRIPS + CHAN, seams())

    left, right = cotangent[:, :, :HALF], cotangent[:, :, HALF:]
    own = jnp.where(second, right, left).reshape(OWN, -1)
    away = jnp.where(second, left, right).reshape(OWN, -1)
    held = {(0, 0): (own, send(away, 0, 0, 1))}
    for dx, dz in ((1, 0), (3, 0), (0, 1)):
        held[(4 - dx) % 4, dz] = (send(own, dx, dz, 0), send(away, dx, dz, 1))
    far_own = send(held[0, 1][0], 1, 0, 0)
    far_partner = send(held[0, 1][1], 3, 0, 0)
    held[3, 1] = (far_own, send(held[3, 0][1], 0, 1, 0))
    held[1, 1] = (send(held[1, 0][0], 0, 1, 0), far_partner)
    held[2, 0] = (send(held[3, 0][0], 1, 0, 0), send(held[1, 0][1], 3, 0, 0))
    held[2, 1] = (send(far_own, 1, 0, 0), send(far_partner, 3, 0, 0))
    blocks = [block for chip in CHIPS for block in held[chip]]

    stacked = jnp.concatenate([image, mask.astype(bf16)[None]], axis=0)
    (tile,) = call(
        rim_kernel,
        [((4, ROWS, 128), bf16)],
        [],
        1_000_000,
        4,
        stacked, held[0, 0][1], *(block for chip in ((0, 1), (1, 0), (3, 0)) for block in held[chip]),
        loose=7,
    )
    both = jnp.concatenate(
        [jnp.pad(whiten, ((0, 0), (0, OWN))), jnp.pad(anchors, ((0, 0), (0, 53)))], axis=0
    )
    plane = ((ROWS, LANES), f32)
    patches, tissue, scale, norm, inv_square, inv_density, anch, anch_t, wturned = call(
        patch_kernel,
        [
            ((36 * GROUP, LANES), bf16),
            plane,
            plane,
            plane,
            plane,
            ((16, HALF), f32),
            ((128, 80), bf16),
            ((80, 128), bf16),
            ((128, 1024), bf16),
        ],
        [],
        1_000_000_000,
        12,
        stacked, cross(tile), both, send(both, 0, 0, 1),
    )
    masked, whitened = call(
        forward_kernel,
        [((ROWS, 128, LANES), bf16), ((128, 16 * HALF), bf16)],
        [((ROWS, 128, HALF), f32), ((LANES, HALF), bf16)],
        3_000_000_000,
        14,
        patches, tissue, scale, norm, inv_density, anch,
    )
    partial, early = call(
        early_kernel,
        [((128, 16 * HALF), f32), ((8, 128, 128), bf16)],
        [],
        2_000_000_000,
        14,
        *blocks[:EARLY], wturned, whitened,
    )
    packed, image_part, rim = call(
        backward_kernel,
        [((8, 176, 128), bf16), ((128, LANES), bf16), ((128, 128), bf16)],
        [
            ((ROWS * 128, HALF), bf16),
            ((36 * GROUP, LANES), f32),
            ((80, 128), f32),
            ((HALF, LANES), bf16),
        ],
        5_000_000_000,
        20,
        *blocks[EARLY:],
        partial, early, wturned, whitened, inv_density, masked, patches, inv_square, anch_t,
    )
    (joined,) = call(seam_kernel, [((128, LANES), bf16)], [], 1_000_000, 4, image_part, cross(rim))

    received = lax.all_to_all(packed, ("y", "core"), 0, 0)
    parts = lax.all_to_all(joined.reshape(16, 8, LANES), CHAN, 0, 0)
    quarter = ((80, 128), bf16)
    kept, *away = call(pack_kernel, [quarter] * 4, [((128, 128), f32)], 1_000_000, 4, received)
    others = [
        lax.ppermute(value, "z_hi", [(z, (z + step) % 4) for z in range(4)])
        for step, value in enumerate(away, 1)
    ]
    (grad_image,) = call(image_kernel, [((3, 2, 512), f32)], [], 1_000_000, 4, parts)
    grad_anchors, grad_whiten = call(
        unpack_kernel, [((OWN, 75), f32), ((OWN, OWN), f32)], [], 1_000_000, 4, kept, *others
    )
    return grad_anchors, grad_whiten, grad_image


def solution(mesh):
    fine = Mesh(mesh.devices.reshape(4, 4, 4, 2, 2), STRIPS + CHAN)
    placed = (
        P(None, None, STRIPS),
        P(None, STRIPS),
        P(CHAN, None),
        P(None, CHAN),
        P(CHAN, None, STRIPS),
    )
    return jax.shard_map(
        shards,
        mesh=fine,
        in_specs=placed,
        out_specs=(P(CHAN, None), P(STRIPS, CHAN), P(None, CHAN, STRIPS)),
        check_vma=False,
    )
```

```python
import math

import jax
import jax.numpy as jnp
from jax import lax
from jax.experimental import pallas as pl
from jax.experimental.pallas import tpu as pltpu
from jax.sharding import Mesh
from jax.sharding import PartitionSpec as P

EPS = 1e-05
LANES = 384
HALF = 128
ROWS = 32
GROUP = 16
OWN = 64
STEP = 4
EARLY = 10
MIB = 1024 * 1024

CHIPS = ((0, 0), (0, 1), (1, 0), (3, 0), (2, 0), (1, 1), (3, 1), (2, 1))


STRIPS = ("z_hi", "y")
CHAN = ("x", "z_lo", "core")


def route(dx, dz, core):
    return [(i, ((i // 4 + dx) % 4) * 4 + ((i // 2) % 2 ^ dz) * 2 + (i % 2 ^ core)) for i in range(16)]


def seams():
    pairs = [(16 * s + 2 * q, 16 * s - 16 + 2 * q + 1) for s in range(1, 16) for q in range(8)]
    return pairs + [(b, a) for a, b in pairs]


f32 = jnp.float32
bf16 = jnp.bfloat16


def tap(distance):
    return math.exp(-distance * distance / 8.0) if abs(distance) <= 4 else 0.0


def taps(distance):
    far = jnp.abs(distance) > 4
    distance = distance.astype(f32)
    return jnp.where(far, 0.0, jnp.exp(distance * distance * (-1.0 / 8.0)))


def places(shape):
    return tuple(lax.broadcasted_iota(jnp.int32, shape, dim) for dim in (0, 1))


def column_pool():
    lane, target = places((LANES, HALF))
    return taps(2 * target - lane + 4).astype(bf16)


def column_spread():
    target, lane = places((HALF, LANES))
    return taps(2 * target - lane + 4).astype(bf16)


def row_pool():
    a, i = places((ROWS // 2, ROWS))
    return taps(2 * a - i)


def split_group(row):
    q = row & (GROUP - 1)
    colour = jnp.where(q < 5, 0, jnp.where(q < 10, 1, jnp.where(q < 15, 2, 3)))
    return row >> 4, colour, q - 5 * colour


def ones(hit, dtype=bf16):
    return jnp.where(hit, 1.0, 0.0).astype(dtype)


def replicate_rows():
    out, src = places((36 * GROUP, 3 * ROWS))
    r, colour, _ = split_group(out)
    return ones(((src & 31) == r - 2) & ((src >> 5) == colour))


def fold_rows():
    out, src = places((128, 36 * GROUP))
    r, colour, _ = split_group(src)
    i = 2 * (out >> 3) + (out & 1)
    return ones((r == i + 2) & (colour == ((out & 7) >> 1)) & (colour < 3))


def entry_order(dtype, rows=75):
    entry, out = places((rows, 80))
    a, colour, b = split_group(out)
    return ones((entry == 25 * colour + 5 * a + b) & (colour < 3), dtype)


def on_second():
    return lax.axis_index("core") == 1


def block_of(p):
    dx, dz = CHIPS[p // 2]
    ex = lax.rem(lax.axis_index("x") + dx, 4)
    zed = lax.rem(lax.axis_index("z_lo") + dz, 2)
    core = lax.rem(lax.axis_index("core") + p % 2, 2)
    return ex * 4 + zed * 2 + core


def dot(a, b):
    return jnp.dot(a, b, preferred_element_type=f32)


def dot_nt(a, b):
    return lax.dot_general(a, b, (((1,), (1,)), ((), ())), preferred_element_type=f32)


def rim_kernel(stacked, *refs):
    tile = refs[-1]
    second = on_second()
    for c in range(4):
        value = stacked[c].astype(f32)
        tile[c] = jnp.where(second, value[:, 384:], value[:, :128]).astype(bf16)


def patch_kernel(
    stacked, beyond, own_both, partner_both,
    patches, tissue, scale, norm, inv_square, inv_density, anch, anch_t, wturned,
):
    second = on_second()

    def half(c, shift):
        middle, rim = stacked[c].astype(f32), beyond[c].astype(f32)
        wide = jnp.concatenate([rim, middle, rim], axis=1)
        part = jnp.where(second, wide[:, 256:], wide[:, :512])
        return pltpu.roll(part, 512 - shift, 1)[:, :LANES]

    colours = [half(c, 122) for c in range(3)]
    here = half(3, 124)
    lane = lax.broadcasted_iota(jnp.int32, here.shape, 1)
    here = jnp.where(lane < 263, here, 0.0)
    tissue[...] = here
    x = dot(replicate_rows(), jnp.concatenate(colours, axis=0).astype(bf16))
    offset = (lax.broadcasted_iota(jnp.int32, x.shape, 0) % GROUP) % 5
    s = x
    for b in range(1, 5):
        s = jnp.where(offset == b, pltpu.roll(x, LANES - b, 1), s)
    patches[...] = s.astype(bf16)
    square = jnp.sum((s * s).reshape(36, GROUP, LANES), axis=1)
    total = square[0:ROWS]
    for a in range(1, 5):
        total = total + square[a : a + ROWS]
    total = total + EPS
    root = lax.rsqrt(total)
    scale[...] = 4.0 * root
    norm[...] = total * root
    inv_square[...] = 1.0 / total
    counted = dot(here.astype(bf16), column_pool())
    density = jnp.dot(row_pool(), counted, precision=lax.Precision.HIGHEST, preferred_element_type=f32)
    inv_density[...] = 1.0 / jnp.maximum(density, 1.0)
    both = jnp.concatenate([own_both[1024:1088, :], partner_both[1024:1088, :]], axis=0)
    ordered = dot(both, entry_order(bf16, 128))
    anch[...] = ordered.astype(bf16)
    anch_t[...] = ordered.T.astype(bf16)
    blocks = [pl.ds(pl.multiple_of(block_of(p) * OWN, OWN), OWN) for p in range(16)]
    for at, both in ((0, own_both), (OWN, partner_both)):
        ordered = jnp.concatenate([both[block, :] for block in blocks], axis=0)
        wturned[at : at + OWN, :] = ordered.astype(f32).T[:OWN].astype(bf16)


def forward_kernel(
    patches, tissue, scale, norm, inv_density, anch,
    masked, whitened,
    columned, pool,
):
    pool[...] = column_pool()

    @pl.loop(0, ROWS // STEP)
    def _(t):
        lifted = []
        for r in range(STEP):
            i = t * STEP + r
            patch = patches[pl.ds(pl.multiple_of(i * GROUP, GROUP), 80), :]
            raw = dot(anch[...], patch)
            value = jnp.exp(raw * scale[pl.ds(i, 1), :] - 4.0) * tissue[pl.ds(i, 1), :]
            masked[i] = value.astype(bf16)
            lifted.append((value * norm[pl.ds(i, 1), :]).astype(bf16))
        result = dot(jnp.concatenate(lifted, axis=0), pool[...])
        columned[pl.ds(t * STEP, STEP)] = result.reshape(STEP, 128, HALF)

    for a in range(ROWS // 2):
        acc = None
        for i in range(max(0, 2 * a - 4), min(ROWS, 2 * a + 5)):
            term = tap(2 * a - i) * columned[i]
            acc = term if acc is None else acc + term
        whitened[:, a * HALF : (a + 1) * HALF] = (acc * inv_density[a : a + 1, :]).astype(bf16)


def fold(block, rows):
    top, low = block[:rows], block[rows:]
    left = lax.broadcasted_iota(jnp.int32, top.shape, 1) < OWN
    own = jnp.where(left, top, pltpu.roll(low, OWN, 1))
    partner = jnp.where(left, pltpu.roll(top, OWN, 1), low)
    return own.astype(bf16), partner.astype(bf16)


def gather_products(blocks, first, wturned, whitened, partial):
    grad_w, pooled = None, []
    weights = wturned[:, first * OWN : first * OWN + sum(block.shape[0] for block in blocks)]
    for n in range(8):
        cols = pl.ds(n * 256, 256)
        stack = jnp.concatenate([block[:, cols] for block in blocks], axis=0)
        term = dot(weights, stack)
        pooled.append(term if partial is None else term + partial[:, cols])
        term = dot_nt(stack, whitened[:, cols])
        grad_w = term if grad_w is None else grad_w + term
    return pooled, grad_w


def place_rows(packed, grad_w, first):
    core = lax.axis_index("core")
    for n in range(grad_w.shape[0] // OWN):
        strip = block_of(first + n)
        rows = pl.ds(pl.multiple_of((strip // 4) * 32, 32), 32)
        y = lax.rem(strip, 4)
        mine, theirs = fold(grad_w[n * OWN : (n + 1) * OWN], OWN // 2)
        packed[y * 2 + core, rows, :] = mine
        packed[y * 2 + 1 - core, rows, :] = theirs


def early_kernel(*refs):
    blocks, (wturned, whitened, partial, packed) = refs[:6], refs[6:]
    packed[...] = jnp.zeros_like(packed)
    pooled, grad_w = gather_products(blocks, 0, wturned, whitened, None)
    for n in range(8):
        partial[:, n * 256 : (n + 1) * 256] = pooled[n]
    place_rows(packed, grad_w, 0)


def backward_kernel(*refs):
    blocks = refs[:4]
    (
        partial, early, wturned, whitened, inv_density, masked, patches, inv_square, anch_t,
        packed, image,
        rowed, spread_grad, anchor_grad, pool_t,
    ) = refs[4:]
    pool_t[...] = column_spread()
    packed[:, 0:128, :] = early[...]
    pooled, grad_w = gather_products(blocks, EARLY, wturned, whitened, partial)
    place_rows(packed, grad_w, EARLY)
    scaled = []
    for a in range(ROWS // 2):
        part = pooled[a // 2][:, (a % 2) * HALF : (a % 2 + 1) * HALF]
        scaled.append(part.astype(bf16).astype(f32) * inv_density[a : a + 1, :])
    for i in range(ROWS):
        acc = None
        for a in range(ROWS // 2):
            if abs(2 * a - i) <= 4:
                term = (4.0 * tap(2 * a - i)) * scaled[a]
                acc = term if acc is None else acc + term
        rowed[i * 128 : (i + 1) * 128, :] = acc.astype(bf16)
    spread_grad[...] = jnp.zeros_like(spread_grad)
    anchor_grad[...] = jnp.zeros_like(anchor_grad)

    @pl.loop(0, ROWS // STEP)
    def _(t):
        start = pl.multiple_of(t * (STEP * 128), STEP * 128)
        spread = dot(rowed[pl.ds(start, STEP * 128), :], pool_t[...])
        grads, wides, units = [], [], []
        for r in range(STEP):
            i = t * STEP + r
            patch = patches[pl.ds(pl.multiple_of(i * GROUP, GROUP), 80), :]
            grad = (spread[r * 128 : (r + 1) * 128] * masked[i].astype(f32)).astype(bf16)
            unit = dot(anch_t[...], grad)
            wide = patch.astype(f32)
            along = jnp.sum(wide * unit, axis=0, keepdims=True) * inv_square[pl.ds(i, 1), :]
            units.append(unit - wide * along)
            grads.append(grad)
            wides.append(patch)
        anchor_grad[...] += dot_nt(jnp.concatenate(wides, axis=1), jnp.concatenate(grads, axis=1))
        sums = []
        for g in range(STEP + 4):
            acc = None
            for r in range(STEP):
                if 0 <= g - r < 5:
                    term = units[r][(g - r) * GROUP : (g - r + 1) * GROUP]
                    acc = term if acc is None else acc + term
            sums.append(acc)
        here = pl.ds(pl.multiple_of(t * (STEP * GROUP), STEP * GROUP), (STEP + 4) * GROUP)
        spread_grad[here, :] += jnp.concatenate(sums, axis=0)

    core = lax.axis_index("core")
    mine, theirs = fold(anchor_grad[...], 40)
    pad = jnp.zeros((8, 128), bf16)
    mine = jnp.concatenate([mine, pad], axis=0)
    theirs = jnp.concatenate([theirs, pad], axis=0)
    for y in range(4):
        packed[y * 2 + core, 128:176, :] = mine
        packed[y * 2 + 1 - core, 128:176, :] = theirs

    t = spread_grad[...]
    offset = (lax.broadcasted_iota(jnp.int32, t.shape, 0) % GROUP) % 5
    moved = t
    for b in range(1, 5):
        moved = jnp.where(offset == b, pltpu.roll(t, b, 1), moved)
    high = moved.astype(bf16)
    low = (moved - high.astype(f32)).astype(bf16)
    folder = fold_rows()
    image[...] = (dot(folder, high) + dot(folder, low)).astype(bf16)


def pack_kernel(received, kept, next_one, next_two, next_three, sums):
    total = received[0].astype(f32)
    for source in range(1, 8):
        total = total + received[source].astype(f32)
    sums[...] = total[0:128]
    anchor = total[128:176].astype(bf16)
    for step, packed in enumerate((kept, next_one, next_two, next_three)):
        z = lax.rem(lax.axis_index("z_hi") + step, 4)
        packed[0:32, :] = sums[pl.ds(pl.multiple_of(z * 32, 32), 32), :].astype(bf16)
        packed[32:80, :] = anchor


def image_kernel(parts, middle, rims):
    halves = []
    for k in range(2):
        acc = parts[k].astype(f32)
        for chip in range(1, 8):
            acc = acc + parts[2 * chip + k].astype(f32)
        halves.append(acc)
    gap = jnp.zeros((8, 256), f32)
    whole = jnp.concatenate([halves[0], gap], axis=1) + jnp.concatenate([gap, halves[1]], axis=1)
    turned = pltpu.roll(whole, 640 - 6, 1)
    middle[...] = turned[:, :512]
    rims[...] = turned[:, 512:]


def unpack_kernel(
    kept, one, two, three, middle, before, after,
    grad_anchors, grad_whiten, grad_image,
):
    total = sum(ref[...].astype(f32) for ref in (one, two, three)) + kept[...].astype(f32)
    other = pltpu.roll(total, OWN, 1)
    grad_whiten[0:32, :] = total[0:32, :OWN]
    grad_whiten[32:64, :] = other[0:32, :OWN]
    turned = jnp.concatenate([total[32:72], other[32:72]], axis=0).T[:OWN]
    grad_anchors[...] = lax.dot_general(
        turned, entry_order(f32), (((1,), (1,)), ((), ())),
        precision=lax.Precision.HIGHEST, preferred_element_type=f32,
    )
    lane = lax.broadcasted_iota(jnp.int32, before.shape, 1)
    first = jnp.where(lane < 6, before[...], 0.0)
    last = jnp.where(lane >= 122, after[...], 0.0)
    gap = jnp.zeros((8, 256), f32)
    image = middle[...] + jnp.concatenate([first, gap, last], axis=1)
    for colour in range(3):
        grad_image[colour] = image[2 * colour : 2 * colour + 2]


def hold(value, *after):
    def kernel(*refs):
        del refs

    return pl.pallas_call(
        kernel,
        out_shape=jax.ShapeDtypeStruct(value.shape, value.dtype),
        in_specs=[pl.BlockSpec(memory_space=pl.ANY)] * (1 + len(after)),
        out_specs=pl.BlockSpec(memory_space=pl.ANY),
        input_output_aliases={0: 0},
        compiler_params=pltpu.CompilerParams(vmem_limit_bytes=MIB),
        cost_estimate=pl.CostEstimate(flops=1000, bytes_accessed=1000, transcendentals=0),
    )(value, *after)


def call(kernel, outs, scratch, flops, limit, *args, loose=0):
    size = lambda shape, dtype: math.prod(shape) * jnp.dtype(dtype).itemsize
    tight = len(args) - loose
    moved = sum(size(a.shape, a.dtype) for a in args[:tight]) + sum(size(*out) for out in outs)
    return pl.pallas_call(
        kernel,
        out_shape=[jax.ShapeDtypeStruct(shape, dtype) for shape, dtype in outs],
        in_specs=[pl.BlockSpec(memory_space=pltpu.VMEM)] * tight
        + [pl.BlockSpec(memory_space=pl.ANY)] * loose,
        out_specs=[pl.BlockSpec(memory_space=pltpu.VMEM)] * len(outs),
        scratch_shapes=[pltpu.VMEM(shape, dtype) for shape, dtype in scratch],
        compiler_params=pltpu.CompilerParams(vmem_limit_bytes=limit * MIB),
        cost_estimate=pl.CostEstimate(flops=flops, bytes_accessed=moved, transcendentals=0),
    )(*args)


def shards(image, mask, anchors, whiten, cotangent):
    second = on_second()

    def send(value, dx, dz, other):
        return lax.ppermute(value, CHAN, route(dx, dz, other))

    def cross(value):
        return lax.ppermute(value, STRIPS + CHAN, seams())

    left, right = cotangent[:, :, :HALF], cotangent[:, :, HALF:]
    own = jnp.where(second, right, left).reshape(OWN, -1)
    away = jnp.where(second, left, right).reshape(OWN, -1)
    block = jnp.concatenate([own, send(away, 0, 0, 1)], axis=0)
    held = {(0, 0): [block]}
    for dx, dz in ((1, 0), (3, 0), (0, 1)):
        held[(4 - dx) % 4, dz] = [send(block, dx, dz, 0)]
    far = [send(held[3, 0][0][:OWN], 1, 0, 0), send(held[1, 0][0][OWN:], 3, 0, 0)]
    beside = hold(held[0, 1][0], *far)
    held[2, 0] = far
    held[3, 1] = [send(beside, 1, 0, 0)]
    held[1, 1] = [send(beside, 3, 0, 0)]
    held[2, 1] = [send(half, 0, 1, 0) for half in far]
    held[0, 1] = [beside]
    blocks = [part for chip in CHIPS for part in held[chip]]

    stacked = jnp.concatenate([image, mask.astype(bf16)[None]], axis=0)
    (tile,) = call(
        rim_kernel,
        [((4, ROWS, 128), bf16)],
        [],
        1_000_000,
        4,
        stacked, held[3, 0][0],
        loose=1,
    )
    both = jnp.concatenate(
        [jnp.pad(whiten, ((0, 0), (0, OWN))), jnp.pad(anchors, ((0, 0), (0, 53)))], axis=0
    )
    plane = ((ROWS, LANES), f32)
    patches, tissue, scale, norm, inv_square, inv_density, anch, anch_t, wturned = call(
        patch_kernel,
        [
            ((36 * GROUP, LANES), bf16),
            plane,
            plane,
            plane,
            plane,
            ((16, HALF), f32),
            ((128, 80), bf16),
            ((80, 128), bf16),
            ((128, 1024), bf16),
        ],
        [],
        1_000_000_000,
        12,
        stacked, cross(tile), both, send(both, 0, 0, 1),
    )
    masked, whitened = call(
        forward_kernel,
        [((ROWS, 128, LANES), bf16), ((128, 16 * HALF), bf16)],
        [((ROWS, 128, HALF), f32), ((LANES, HALF), bf16)],
        3_000_000_000,
        14,
        patches, tissue, scale, norm, inv_density, anch,
    )
    partial, early = call(
        early_kernel,
        [((128, 16 * HALF), f32), ((8, 128, 128), bf16)],
        [],
        2_000_000_000,
        14,
        *blocks[:6], wturned, whitened,
    )
    packed, image_part = call(
        backward_kernel,
        [((8, 176, 128), bf16), ((128, LANES), bf16)],
        [
            ((ROWS * 128, HALF), bf16),
            ((36 * GROUP, LANES), f32),
            ((80, 128), f32),
            ((HALF, LANES), bf16),
        ],
        5_000_000_000,
        20,
        *blocks[6:],
        partial, early, wturned, whitened, inv_density, masked, patches, inv_square, anch_t,
    )

    received = lax.all_to_all(packed, ("y", "core"), 0, 0)
    parts = lax.all_to_all(image_part.reshape(16, 8, LANES), CHAN, 0, 0)
    quarter = ((80, 128), bf16)
    kept, *away = call(pack_kernel, [quarter] * 4, [((128, 128), f32)], 1_000_000, 4, received)
    others = [
        lax.ppermute(value, "z_hi", [(z, (z + step) % 4) for z in range(4)])
        for step, value in enumerate(away, 1)
    ]
    middle, rims = call(image_kernel, [((8, 512), f32), ((8, 128), f32)], [], 1_000_000, 4, parts)
    before = lax.ppermute(rims, STRIPS, [(i, i + 1) for i in range(15)])
    after = lax.ppermute(rims, STRIPS, [(i + 1, i) for i in range(15)])
    return tuple(
        call(
            unpack_kernel,
            [((OWN, 75), f32), ((OWN, OWN), f32), ((3, 2, 512), f32)],
            [],
            1_000_000,
            4,
            kept, *others, middle, before, after,
        )
    )


def solution(mesh):
    fine = Mesh(mesh.devices.reshape(4, 4, 4, 2, 2), STRIPS + CHAN)
    placed = (
        P(None, None, STRIPS),
        P(None, STRIPS),
        P(CHAN, None),
        P(None, CHAN),
        P(CHAN, None, STRIPS),
    )
    return jax.shard_map(
        shards,
        mesh=fine,
        in_specs=placed,
        out_specs=(P(CHAN, None), P(STRIPS, CHAN), P(None, CHAN, STRIPS)),
        check_vma=False,
    )
```

```python
import math

import jax
import jax.numpy as jnp
from jax import lax
from jax.experimental import pallas as pl
from jax.experimental.pallas import tpu as pltpu
from jax.sharding import Mesh
from jax.sharding import PartitionSpec as P

EPS = 1e-05
LANES = 384
HALF = 128
ROWS = 32
GROUP = 16
OWN = 64
STEP = 4
EARLY = 10
MIB = 1024 * 1024

CHIPS = ((0, 0), (0, 1), (1, 0), (3, 0), (2, 0), (1, 1), (3, 1), (2, 1))


STRIPS = ("z_hi", "y")
CHAN = ("x", "z_lo", "core")


def route(dx, dz, core):
    return [(i, ((i // 4 + dx) % 4) * 4 + ((i // 2) % 2 ^ dz) * 2 + (i % 2 ^ core)) for i in range(16)]


def seams():
    pairs = [(16 * s + 2 * q, 16 * s - 16 + 2 * q + 1) for s in range(1, 16) for q in range(8)]
    return pairs + [(b, a) for a, b in pairs]


f32 = jnp.float32
bf16 = jnp.bfloat16


def tap(distance):
    return math.exp(-distance * distance / 8.0) if abs(distance) <= 4 else 0.0


def taps(distance):
    far = jnp.abs(distance) > 4
    distance = distance.astype(f32)
    return jnp.where(far, 0.0, jnp.exp(distance * distance * (-1.0 / 8.0)))


def places(shape):
    return tuple(lax.broadcasted_iota(jnp.int32, shape, dim) for dim in (0, 1))


def column_pool():
    lane, target = places((LANES, HALF))
    return taps(2 * target - lane + 4).astype(bf16)


def column_spread():
    target, lane = places((HALF, LANES))
    return taps(2 * target - lane + 4).astype(bf16)


def row_pool():
    a, i = places((ROWS // 2, ROWS))
    return taps(2 * a - i)


def split_group(row):
    q = row & (GROUP - 1)
    colour = jnp.where(q < 5, 0, jnp.where(q < 10, 1, jnp.where(q < 15, 2, 3)))
    return row >> 4, colour, q - 5 * colour


def ones(hit, dtype=bf16):
    return jnp.where(hit, 1.0, 0.0).astype(dtype)


def replicate_rows():
    out, src = places((36 * GROUP, 3 * ROWS))
    r, colour, _ = split_group(out)
    return ones(((src & 31) == r - 2) & ((src >> 5) == colour))


def fold_rows():
    out, src = places((128, 36 * GROUP))
    r, colour, _ = split_group(src)
    i = 2 * (out >> 3) + (out & 1)
    return ones((r == i + 2) & (colour == ((out & 7) >> 1)) & (colour < 3))


def entry_order(dtype, rows=75):
    entry, out = places((rows, 80))
    a, colour, b = split_group(out)
    return ones((entry == 25 * colour + 5 * a + b) & (colour < 3), dtype)


def on_second():
    return lax.axis_index("core") == 1


def block_of(p):
    dx, dz = CHIPS[p // 2]
    ex = lax.rem(lax.axis_index("x") + dx, 4)
    zed = lax.rem(lax.axis_index("z_lo") + dz, 2)
    core = lax.rem(lax.axis_index("core") + p % 2, 2)
    return ex * 4 + zed * 2 + core


def dot(a, b):
    return jnp.dot(a, b, preferred_element_type=f32)


def dot_nt(a, b):
    return lax.dot_general(a, b, (((1,), (1,)), ((), ())), preferred_element_type=f32)


def rim_kernel(stacked, *refs):
    tile = refs[-1]
    second = on_second()
    for c in range(4):
        value = stacked[c].astype(f32)
        tile[c] = jnp.where(second, value[:, 384:], value[:, :128]).astype(bf16)


def patch_kernel(
    stacked, beyond, own_both, partner_both,
    patches, tissue, scale, norm, inv_square, inv_density, anch, anch_t, wturned,
):
    second = on_second()

    def half(c, shift):
        middle, rim = stacked[c].astype(f32), beyond[c].astype(f32)
        wide = jnp.concatenate([rim, middle, rim], axis=1)
        part = jnp.where(second, wide[:, 256:], wide[:, :512])
        return pltpu.roll(part, 512 - shift, 1)[:, :LANES]

    colours = [half(c, 122) for c in range(3)]
    here = half(3, 124)
    lane = lax.broadcasted_iota(jnp.int32, here.shape, 1)
    here = jnp.where(lane < 263, here, 0.0)
    tissue[...] = here
    x = dot(replicate_rows(), jnp.concatenate(colours, axis=0).astype(bf16))
    offset = (lax.broadcasted_iota(jnp.int32, x.shape, 0) % GROUP) % 5
    s = x
    for b in range(1, 5):
        s = jnp.where(offset == b, pltpu.roll(x, LANES - b, 1), s)
    patches[...] = s.astype(bf16)
    square = jnp.sum((s * s).reshape(36, GROUP, LANES), axis=1)
    total = square[0:ROWS]
    for a in range(1, 5):
        total = total + square[a : a + ROWS]
    total = total + EPS
    root = lax.rsqrt(total)
    scale[...] = 4.0 * root
    norm[...] = total * root
    inv_square[...] = 1.0 / total
    counted = dot(here.astype(bf16), column_pool())
    density = jnp.dot(row_pool(), counted, precision=lax.Precision.HIGHEST, preferred_element_type=f32)
    inv_density[...] = 1.0 / jnp.maximum(density, 1.0)
    both = jnp.concatenate([own_both[1024:1088, :], partner_both[1024:1088, :]], axis=0)
    ordered = dot(both, entry_order(bf16, 128))
    anch[...] = ordered.astype(bf16)
    anch_t[...] = ordered.T.astype(bf16)
    blocks = [pl.ds(pl.multiple_of(block_of(p) * OWN, OWN), OWN) for p in range(16)]
    for at, both in ((0, own_both), (OWN, partner_both)):
        ordered = jnp.concatenate([both[block, :] for block in blocks], axis=0)
        wturned[at : at + OWN, :] = ordered.astype(f32).T[:OWN].astype(bf16)


def forward_kernel(
    patches, tissue, scale, norm, inv_density, anch,
    masked, whitened,
    columned, pool,
):
    pool[...] = column_pool()

    @pl.loop(0, ROWS // STEP)
    def _(t):
        lifted = []
        for r in range(STEP):
            i = t * STEP + r
            patch = patches[pl.ds(pl.multiple_of(i * GROUP, GROUP), 80), :]
            raw = dot(anch[...], patch)
            value = jnp.exp(raw * scale[pl.ds(i, 1), :] - 4.0) * tissue[pl.ds(i, 1), :]
            masked[i] = value.astype(bf16)
            lifted.append((value * norm[pl.ds(i, 1), :]).astype(bf16))
        result = dot(jnp.concatenate(lifted, axis=0), pool[...])
        columned[pl.ds(t * STEP, STEP)] = result.reshape(STEP, 128, HALF)

    for a in range(ROWS // 2):
        acc = None
        for i in range(max(0, 2 * a - 4), min(ROWS, 2 * a + 5)):
            term = tap(2 * a - i) * columned[i]
            acc = term if acc is None else acc + term
        whitened[:, a * HALF : (a + 1) * HALF] = (acc * inv_density[a : a + 1, :]).astype(bf16)


def fold(block, rows):
    top, low = block[:rows], block[rows:]
    left = lax.broadcasted_iota(jnp.int32, top.shape, 1) < OWN
    own = jnp.where(left, top, pltpu.roll(low, OWN, 1))
    partner = jnp.where(left, pltpu.roll(top, OWN, 1), low)
    return own.astype(bf16), partner.astype(bf16)


def gather_products(blocks, first, wturned, whitened, partial):
    grad_w, pooled = None, []
    weights = wturned[:, first * OWN : first * OWN + sum(block.shape[0] for block in blocks)]
    for n in range(8):
        cols = pl.ds(n * 256, 256)
        stack = jnp.concatenate([block[:, cols] for block in blocks], axis=0)
        term = dot(weights, stack)
        pooled.append(term if partial is None else term + partial[:, cols])
        term = dot_nt(stack, whitened[:, cols])
        grad_w = term if grad_w is None else grad_w + term
    return pooled, grad_w


def place_rows(packed, grad_w, first):
    core = lax.axis_index("core")
    for n in range(grad_w.shape[0] // OWN):
        strip = block_of(first + n)
        rows = pl.ds(pl.multiple_of((strip // 4) * 32, 32), 32)
        y = lax.rem(strip, 4)
        mine, theirs = fold(grad_w[n * OWN : (n + 1) * OWN], OWN // 2)
        packed[y * 2 + core, rows, :] = mine
        packed[y * 2 + 1 - core, rows, :] = theirs


def early_kernel(*refs):
    blocks, (wturned, whitened, partial, packed) = refs[:6], refs[6:]
    packed[...] = jnp.zeros_like(packed)
    pooled, grad_w = gather_products(blocks, 0, wturned, whitened, None)
    for n in range(8):
        partial[:, n * 256 : (n + 1) * 256] = pooled[n]
    place_rows(packed, grad_w, 0)


def backward_kernel(*refs):
    blocks = refs[:4]
    (
        partial, early, wturned, whitened, inv_density, masked, patches, inv_square, anch_t,
        packed, image, rim,
        rowed, spread_grad, anchor_grad, pool_t,
    ) = refs[4:]
    pool_t[...] = column_spread()
    packed[:, 0:128, :] = early[...]
    pooled, grad_w = gather_products(blocks, EARLY, wturned, whitened, partial)
    place_rows(packed, grad_w, EARLY)
    scaled = []
    for a in range(ROWS // 2):
        part = pooled[a // 2][:, (a % 2) * HALF : (a % 2 + 1) * HALF]
        scaled.append(part.astype(bf16).astype(f32) * inv_density[a : a + 1, :])
    for i in range(ROWS):
        acc = None
        for a in range(ROWS // 2):
            if abs(2 * a - i) <= 4:
                term = (4.0 * tap(2 * a - i)) * scaled[a]
                acc = term if acc is None else acc + term
        rowed[i * 128 : (i + 1) * 128, :] = acc.astype(bf16)
    spread_grad[...] = jnp.zeros_like(spread_grad)
    anchor_grad[...] = jnp.zeros_like(anchor_grad)

    @pl.loop(0, ROWS // STEP)
    def _(t):
        start = pl.multiple_of(t * (STEP * 128), STEP * 128)
        spread = dot(rowed[pl.ds(start, STEP * 128), :], pool_t[...])
        grads, wides, units = [], [], []
        for r in range(STEP):
            i = t * STEP + r
            patch = patches[pl.ds(pl.multiple_of(i * GROUP, GROUP), 80), :]
            grad = (spread[r * 128 : (r + 1) * 128] * masked[i].astype(f32)).astype(bf16)
            unit = dot(anch_t[...], grad)
            wide = patch.astype(f32)
            along = jnp.sum(wide * unit, axis=0, keepdims=True) * inv_square[pl.ds(i, 1), :]
            units.append(unit - wide * along)
            grads.append(grad)
            wides.append(patch)
        anchor_grad[...] += dot_nt(jnp.concatenate(wides, axis=1), jnp.concatenate(grads, axis=1))
        sums = []
        for g in range(STEP + 4):
            acc = None
            for r in range(STEP):
                if 0 <= g - r < 5:
                    term = units[r][(g - r) * GROUP : (g - r + 1) * GROUP]
                    acc = term if acc is None else acc + term
            sums.append(acc)
        here = pl.ds(pl.multiple_of(t * (STEP * GROUP), STEP * GROUP), (STEP + 4) * GROUP)
        spread_grad[here, :] += jnp.concatenate(sums, axis=0)

    core = lax.axis_index("core")
    mine, theirs = fold(anchor_grad[...], 40)
    pad = jnp.zeros((8, 128), bf16)
    mine = jnp.concatenate([mine, pad], axis=0)
    theirs = jnp.concatenate([theirs, pad], axis=0)
    for y in range(4):
        packed[y * 2 + core, 128:176, :] = mine
        packed[y * 2 + 1 - core, 128:176, :] = theirs

    t = spread_grad[...]
    offset = (lax.broadcasted_iota(jnp.int32, t.shape, 0) % GROUP) % 5
    moved = t
    for b in range(1, 5):
        moved = jnp.where(offset == b, pltpu.roll(t, b, 1), moved)
    high = moved.astype(bf16)
    low = (moved - high.astype(f32)).astype(bf16)
    folder = fold_rows()
    summed = dot(folder, high) + dot(folder, low)
    image[...] = summed.astype(bf16)
    first, last = summed[:, :128], summed[:, 256:]
    lane = lax.broadcasted_iota(jnp.int32, first.shape, 1)
    first, last = jnp.where(lane < 6, first, 0.0), jnp.where(lane < 6, 0.0, last)
    rim[...] = jnp.where(on_second(), last, first).astype(bf16)


def seam_kernel(image, rim, joined):
    second = on_second()
    value = rim[...].astype(f32)
    first = image[:, :128].astype(f32) + jnp.where(second, 0.0, value)
    last = image[:, 256:].astype(f32) + jnp.where(second, value, 0.0)
    joined[:, :128] = first.astype(bf16)
    joined[:, 128:256] = image[:, 128:256]
    joined[:, 256:] = last.astype(bf16)


def pack_kernel(received, kept, next_one, next_two, next_three, sums):
    total = received[0].astype(f32)
    for source in range(1, 8):
        total = total + received[source].astype(f32)
    sums[...] = total[0:128]
    anchor = total[128:176].astype(bf16)
    for step, packed in enumerate((kept, next_one, next_two, next_three)):
        z = lax.rem(lax.axis_index("z_hi") + step, 4)
        packed[0:32, :] = sums[pl.ds(pl.multiple_of(z * 32, 32), 32), :].astype(bf16)
        packed[32:80, :] = anchor


def unpack_kernel(kept, one, two, three, grad_anchors, grad_whiten):
    total = sum(ref[...].astype(f32) for ref in (one, two, three)) + kept[...].astype(f32)
    other = pltpu.roll(total, OWN, 1)
    grad_whiten[0:32, :] = total[0:32, :OWN]
    grad_whiten[32:64, :] = other[0:32, :OWN]
    turned = jnp.concatenate([total[32:72], other[32:72]], axis=0).T[:OWN]
    grad_anchors[...] = lax.dot_general(
        turned, entry_order(f32), (((1,), (1,)), ((), ())),
        precision=lax.Precision.HIGHEST, preferred_element_type=f32,
    )


def image_kernel(parts, grad_image):
    halves = []
    for k in range(2):
        acc = parts[k].astype(f32)
        for chip in range(1, 8):
            acc = acc + parts[2 * chip + k].astype(f32)
        halves.append(acc)
    gap = jnp.zeros((8, 256), f32)
    whole = jnp.concatenate([halves[0], gap], axis=1) + jnp.concatenate([gap, halves[1]], axis=1)
    image = pltpu.roll(whole, 640 - 6, 1)[:, :512]
    for colour in range(3):
        grad_image[colour] = image[2 * colour : 2 * colour + 2]


def halve_kernel(first, second, after, upper, lower):
    del after
    upper[...] = first[:OWN]
    lower[...] = second[OWN:]


def hold(value, *after):
    def kernel(*refs):
        del refs

    return pl.pallas_call(
        kernel,
        out_shape=jax.ShapeDtypeStruct(value.shape, value.dtype),
        in_specs=[pl.BlockSpec(memory_space=pl.ANY)] * (1 + len(after)),
        out_specs=pl.BlockSpec(memory_space=pl.ANY),
        input_output_aliases={0: 0},
        compiler_params=pltpu.CompilerParams(vmem_limit_bytes=MIB),
        cost_estimate=pl.CostEstimate(flops=1000, bytes_accessed=1000, transcendentals=0),
    )(value, *after)


def call(kernel, outs, scratch, flops, limit, *args, loose=0):
    size = lambda shape, dtype: math.prod(shape) * jnp.dtype(dtype).itemsize
    tight = len(args) - loose
    moved = sum(size(a.shape, a.dtype) for a in args[:tight]) + sum(size(*out) for out in outs)
    return pl.pallas_call(
        kernel,
        out_shape=[jax.ShapeDtypeStruct(shape, dtype) for shape, dtype in outs],
        in_specs=[pl.BlockSpec(memory_space=pltpu.VMEM)] * tight
        + [pl.BlockSpec(memory_space=pl.ANY)] * loose,
        out_specs=[pl.BlockSpec(memory_space=pltpu.VMEM)] * len(outs),
        scratch_shapes=[pltpu.VMEM(shape, dtype) for shape, dtype in scratch],
        compiler_params=pltpu.CompilerParams(vmem_limit_bytes=limit * MIB),
        cost_estimate=pl.CostEstimate(flops=flops, bytes_accessed=moved, transcendentals=0),
    )(*args)


def shards(image, mask, anchors, whiten, cotangent):
    second = on_second()

    def send(value, dx, dz, other):
        return lax.ppermute(value, CHAN, route(dx, dz, other))

    def cross(value):
        return lax.ppermute(value, STRIPS + CHAN, seams())

    left, right = cotangent[:, :, :HALF], cotangent[:, :, HALF:]
    own = jnp.where(second, right, left).reshape(OWN, -1)
    away = jnp.where(second, left, right).reshape(OWN, -1)
    block = jnp.concatenate([own, send(away, 0, 0, 1)], axis=0)
    held = {(0, 0): [block]}
    for dx, dz in ((1, 0), (3, 0), (0, 1)):
        held[(4 - dx) % 4, dz] = [send(block, dx, dz, 0)]
    both = jnp.concatenate(
        [jnp.pad(whiten, ((0, 0), (0, OWN))), jnp.pad(anchors, ((0, 0), (0, 53)))], axis=0
    )
    partner_both = send(both, 0, 0, 1)

    stacked = jnp.concatenate([image, mask.astype(bf16)[None]], axis=0)
    (tile,) = call(
        rim_kernel,
        [((4, ROWS, 128), bf16)],
        [],
        1_000_000,
        4,
        stacked, partner_both,
        loose=1,
    )
    plane = ((ROWS, LANES), f32)
    patches, tissue, scale, norm, inv_square, inv_density, anch, anch_t, wturned = call(
        patch_kernel,
        [
            ((36 * GROUP, LANES), bf16),
            plane,
            plane,
            plane,
            plane,
            ((16, HALF), f32),
            ((128, 80), bf16),
            ((80, 128), bf16),
            ((128, 1024), bf16),
        ],
        [],
        1_000_000_000,
        12,
        stacked, cross(tile), both, partner_both,
    )
    half = ((OWN, 16 * HALF), bf16)
    upper, lower = call(
        halve_kernel, [half, half], [], 1_000_000, 4, held[3, 0][0], held[1, 0][0], inv_density, loose=1
    )
    far = [send(upper, 1, 0, 0), send(lower, 3, 0, 0)]
    beside = hold(held[0, 1][0], *far)
    held[2, 0] = far
    held[3, 1] = [send(beside, 1, 0, 0)]
    held[1, 1] = [send(beside, 3, 0, 0)]
    held[2, 1] = [send(half, 0, 1, 0) for half in far]
    held[0, 1] = [beside]
    blocks = [part for chip in CHIPS for part in held[chip]]

    masked, whitened = call(
        forward_kernel,
        [((ROWS, 128, LANES), bf16), ((128, 16 * HALF), bf16)],
        [((ROWS, 128, HALF), f32), ((LANES, HALF), bf16)],
        3_000_000_000,
        14,
        patches, tissue, scale, norm, inv_density, anch,
    )
    partial, early = call(
        early_kernel,
        [((128, 16 * HALF), f32), ((8, 128, 128), bf16)],
        [],
        2_000_000_000,
        14,
        *blocks[:6], wturned, whitened,
    )
    packed, image_part, rim = call(
        backward_kernel,
        [((8, 176, 128), bf16), ((128, LANES), bf16), ((128, 128), bf16)],
        [
            ((ROWS * 128, HALF), bf16),
            ((36 * GROUP, LANES), f32),
            ((80, 128), f32),
            ((HALF, LANES), bf16),
        ],
        5_000_000_000,
        20,
        *blocks[6:],
        partial, early, wturned, whitened, inv_density, masked, patches, inv_square, anch_t,
    )

    (joined,) = call(seam_kernel, [((128, LANES), bf16)], [], 1_000_000, 4, image_part, cross(rim))

    received = lax.all_to_all(packed, ("y", "core"), 0, 0)
    parts = lax.all_to_all(joined.reshape(16, 8, LANES), CHAN, 0, 0)
    quarter = ((80, 128), bf16)
    kept, *away = call(pack_kernel, [quarter] * 4, [((128, 128), f32)], 1_000_000, 4, received)
    others = [
        lax.ppermute(value, "z_hi", [(z, (z + step) % 4) for z in range(4)])
        for step, value in enumerate(away, 1)
    ]
    (grad_image,) = call(image_kernel, [((3, 2, 512), f32)], [], 1_000_000, 4, parts)
    grad_anchors, grad_whiten = call(
        unpack_kernel, [((OWN, 75), f32), ((OWN, OWN), f32)], [], 1_000_000, 4, kept, *others
    )
    return grad_anchors, grad_whiten, grad_image


def solution(mesh):
    fine = Mesh(mesh.devices.reshape(4, 4, 4, 2, 2), STRIPS + CHAN)
    placed = (
        P(None, None, STRIPS),
        P(None, STRIPS),
        P(CHAN, None),
        P(None, CHAN),
        P(CHAN, None, STRIPS),
    )
    return jax.shard_map(
        shards,
        mesh=fine,
        in_specs=placed,
        out_specs=(P(CHAN, None), P(STRIPS, CHAN), P(None, CHAN, STRIPS)),
        check_vma=False,
    )
```

```python
import math

import jax
import jax.numpy as jnp
from jax import lax
from jax.experimental import pallas as pl
from jax.experimental.pallas import tpu as pltpu
from jax.sharding import Mesh
from jax.sharding import PartitionSpec as P

EPS = 1e-05
LANES = 384
HALF = 128
ROWS = 32
GROUP = 16
OWN = 64
STEP = 4
EARLY = 10
MIB = 1024 * 1024

CHIPS = ((0, 0), (0, 1), (1, 0), (3, 0), (2, 0), (1, 1), (3, 1), (2, 1))


STRIPS = ("z_hi", "y")
CHAN = ("x", "z_lo", "core")


def route(dx, dz, core):
    return [(i, ((i // 4 + dx) % 4) * 4 + ((i // 2) % 2 ^ dz) * 2 + (i % 2 ^ core)) for i in range(16)]


def seams():
    pairs = [(16 * s + 2 * q, 16 * s - 16 + 2 * q + 1) for s in range(1, 16) for q in range(8)]
    return pairs + [(b, a) for a, b in pairs]


f32 = jnp.float32
bf16 = jnp.bfloat16


def tap(distance):
    return math.exp(-distance * distance / 8.0) if abs(distance) <= 4 else 0.0


def taps(distance):
    far = jnp.abs(distance) > 4
    distance = distance.astype(f32)
    return jnp.where(far, 0.0, jnp.exp(distance * distance * (-1.0 / 8.0)))


def places(shape):
    return tuple(lax.broadcasted_iota(jnp.int32, shape, dim) for dim in (0, 1))


def column_pool():
    lane, target = places((LANES, HALF))
    return taps(2 * target - lane + 4).astype(bf16)


def column_spread():
    target, lane = places((HALF, LANES))
    return taps(2 * target - lane + 4).astype(bf16)


def row_pool():
    a, i = places((ROWS // 2, ROWS))
    return taps(2 * a - i)


def split_group(row):
    q = row & (GROUP - 1)
    colour = jnp.where(q < 5, 0, jnp.where(q < 10, 1, jnp.where(q < 15, 2, 3)))
    return row >> 4, colour, q - 5 * colour


def ones(hit, dtype=bf16):
    return jnp.where(hit, 1.0, 0.0).astype(dtype)


def replicate_rows():
    out, src = places((36 * GROUP, 3 * ROWS))
    r, colour, _ = split_group(out)
    return ones(((src & 31) == r - 2) & ((src >> 5) == colour))


def fold_rows():
    out, src = places((128, 36 * GROUP))
    r, colour, _ = split_group(src)
    i = 2 * (out >> 3) + (out & 1)
    return ones((r == i + 2) & (colour == ((out & 7) >> 1)) & (colour < 3))


def entry_order(dtype, rows=75):
    entry, out = places((rows, 80))
    a, colour, b = split_group(out)
    return ones((entry == 25 * colour + 5 * a + b) & (colour < 3), dtype)


def on_second():
    return lax.axis_index("core") == 1


def block_of(p):
    dx, dz = CHIPS[p // 2]
    ex = lax.rem(lax.axis_index("x") + dx, 4)
    zed = lax.rem(lax.axis_index("z_lo") + dz, 2)
    core = lax.rem(lax.axis_index("core") + p % 2, 2)
    return ex * 4 + zed * 2 + core


def dot(a, b):
    return jnp.dot(a, b, preferred_element_type=f32)


def dot_nt(a, b):
    return lax.dot_general(a, b, (((1,), (1,)), ((), ())), preferred_element_type=f32)


def rim_kernel(stacked, *refs):
    tile = refs[-1]
    second = on_second()
    for c in range(4):
        value = stacked[c].astype(f32)
        tile[c] = jnp.where(second, value[:, 384:], value[:, :128]).astype(bf16)


def patch_kernel(
    stacked, beyond, own_both, partner_both, after,
    patches, tissue, scale, norm, inv_square, inv_density, anch, anch_t, wturned,
):
    del after
    second = on_second()

    def half(c, shift):
        middle, rim = stacked[c].astype(f32), beyond[c].astype(f32)
        wide = jnp.concatenate([rim, middle, rim], axis=1)
        part = jnp.where(second, wide[:, 256:], wide[:, :512])
        return pltpu.roll(part, 512 - shift, 1)[:, :LANES]

    colours = [half(c, 122) for c in range(3)]
    here = half(3, 124)
    lane = lax.broadcasted_iota(jnp.int32, here.shape, 1)
    here = jnp.where(lane < 263, here, 0.0)
    tissue[...] = here
    x = dot(replicate_rows(), jnp.concatenate(colours, axis=0).astype(bf16))
    offset = (lax.broadcasted_iota(jnp.int32, x.shape, 0) % GROUP) % 5
    s = x
    for b in range(1, 5):
        s = jnp.where(offset == b, pltpu.roll(x, LANES - b, 1), s)
    patches[...] = s.astype(bf16)
    square = jnp.sum((s * s).reshape(36, GROUP, LANES), axis=1)
    total = square[0:ROWS]
    for a in range(1, 5):
        total = total + square[a : a + ROWS]
    total = total + EPS
    root = lax.rsqrt(total)
    scale[...] = 4.0 * root
    norm[...] = total * root
    inv_square[...] = 1.0 / total
    counted = dot(here.astype(bf16), column_pool())
    density = jnp.dot(row_pool(), counted, precision=lax.Precision.HIGHEST, preferred_element_type=f32)
    inv_density[...] = 1.0 / jnp.maximum(density, 1.0)
    both = jnp.concatenate([own_both[1024:1088, :], partner_both[1024:1088, :]], axis=0)
    ordered = dot(both, entry_order(bf16, 128))
    anch[...] = ordered.astype(bf16)
    anch_t[...] = ordered.T.astype(bf16)
    blocks = [pl.ds(pl.multiple_of(block_of(p) * OWN, OWN), OWN) for p in range(16)]
    for at, both in ((0, own_both), (OWN, partner_both)):
        ordered = jnp.concatenate([both[block, :] for block in blocks], axis=0)
        wturned[at : at + OWN, :] = ordered.astype(f32).T[:OWN].astype(bf16)


def forward_kernel(
    patches, tissue, scale, norm, inv_density, anch,
    masked, whitened,
    columned, pool,
):
    pool[...] = column_pool()

    @pl.loop(0, ROWS // STEP)
    def _(t):
        lifted = []
        for r in range(STEP):
            i = t * STEP + r
            patch = patches[pl.ds(pl.multiple_of(i * GROUP, GROUP), 80), :]
            raw = dot(anch[...], patch)
            value = jnp.exp(raw * scale[pl.ds(i, 1), :] - 4.0) * tissue[pl.ds(i, 1), :]
            masked[i] = value.astype(bf16)
            lifted.append((value * norm[pl.ds(i, 1), :]).astype(bf16))
        result = dot(jnp.concatenate(lifted, axis=0), pool[...])
        columned[pl.ds(t * STEP, STEP)] = result.reshape(STEP, 128, HALF)

    for a in range(ROWS // 2):
        acc = None
        for i in range(max(0, 2 * a - 4), min(ROWS, 2 * a + 5)):
            term = tap(2 * a - i) * columned[i]
            acc = term if acc is None else acc + term
        whitened[:, a * HALF : (a + 1) * HALF] = (acc * inv_density[a : a + 1, :]).astype(bf16)


def fold(block, rows):
    top, low = block[:rows], block[rows:]
    left = lax.broadcasted_iota(jnp.int32, top.shape, 1) < OWN
    own = jnp.where(left, top, pltpu.roll(low, OWN, 1))
    partner = jnp.where(left, pltpu.roll(top, OWN, 1), low)
    return own.astype(bf16), partner.astype(bf16)


def stacks(blocks):
    for n in range(8):
        cols = slice(n * 256, (n + 1) * 256)
        yield cols, jnp.concatenate([block[:, cols] for block in blocks], axis=0)


def whiten_rows(blocks, whitened):
    return sum(dot_nt(stack, whitened[:, cols]) for cols, stack in stacks(blocks))


def place_rows(packed, grad_w, first):
    core = lax.axis_index("core")
    for n in range(grad_w.shape[0] // OWN):
        strip = block_of(first + n)
        rows = pl.ds(pl.multiple_of((strip // 4) * 32, 32), 32)
        y = lax.rem(strip, 4)
        mine, theirs = fold(grad_w[n * OWN : (n + 1) * OWN], OWN // 2)
        packed[y * 2 + core, rows, :] = mine
        packed[y * 2 + 1 - core, rows, :] = theirs


def early_kernel(*refs):
    blocks, (wturned, whitened, partial, packed) = refs[:5], refs[5:]
    packed[...] = jnp.zeros_like(packed)
    for cols, stack in stacks(blocks):
        partial[:, cols] = dot(wturned[:, : EARLY * OWN], stack)
    place_rows(packed, whiten_rows(blocks, whitened), 0)


def backward_kernel(*refs):
    blocks = refs[:3]
    (
        partial, wturned, inv_density, masked, patches, inv_square, anch_t,
        anchor_grad, image,
        rowed, spread_grad, pool_t,
    ) = refs[3:]
    pool_t[...] = column_spread()
    pooled = [
        partial[:, cols] + dot(wturned[:, EARLY * OWN :], stack) for cols, stack in stacks(blocks)
    ]
    scaled = []
    for a in range(ROWS // 2):
        part = pooled[a // 2][:, (a % 2) * HALF : (a % 2 + 1) * HALF]
        scaled.append(part.astype(bf16).astype(f32) * inv_density[a : a + 1, :])
    for i in range(ROWS):
        acc = None
        for a in range(ROWS // 2):
            if abs(2 * a - i) <= 4:
                term = (4.0 * tap(2 * a - i)) * scaled[a]
                acc = term if acc is None else acc + term
        rowed[i * 128 : (i + 1) * 128, :] = acc.astype(bf16)
    spread_grad[...] = jnp.zeros_like(spread_grad)
    anchor_grad[...] = jnp.zeros_like(anchor_grad)

    @pl.loop(0, ROWS // STEP)
    def _(t):
        start = pl.multiple_of(t * (STEP * 128), STEP * 128)
        spread = dot(rowed[pl.ds(start, STEP * 128), :], pool_t[...])
        grads, wides, units = [], [], []
        for r in range(STEP):
            i = t * STEP + r
            patch = patches[pl.ds(pl.multiple_of(i * GROUP, GROUP), 80), :]
            grad = (spread[r * 128 : (r + 1) * 128] * masked[i].astype(f32)).astype(bf16)
            unit = dot(anch_t[...], grad)
            wide = patch.astype(f32)
            along = jnp.sum(wide * unit, axis=0, keepdims=True) * inv_square[pl.ds(i, 1), :]
            units.append(unit - wide * along)
            grads.append(grad)
            wides.append(patch)
        anchor_grad[...] += dot_nt(jnp.concatenate(wides, axis=1), jnp.concatenate(grads, axis=1))
        sums = []
        for g in range(STEP + 4):
            acc = None
            for r in range(STEP):
                if 0 <= g - r < 5:
                    term = units[r][(g - r) * GROUP : (g - r + 1) * GROUP]
                    acc = term if acc is None else acc + term
            sums.append(acc)
        here = pl.ds(pl.multiple_of(t * (STEP * GROUP), STEP * GROUP), (STEP + 4) * GROUP)
        spread_grad[here, :] += jnp.concatenate(sums, axis=0)

    t = spread_grad[...]
    offset = (lax.broadcasted_iota(jnp.int32, t.shape, 0) % GROUP) % 5
    moved = t
    for b in range(1, 5):
        moved = jnp.where(offset == b, pltpu.roll(t, b, 1), moved)
    high = moved.astype(bf16)
    low = (moved - high.astype(f32)).astype(bf16)
    folder = fold_rows()
    image[...] = (dot(folder, high) + dot(folder, low)).astype(bf16)


def finish_kernel(first, second, third, whitened, early, anchor_grad, packed):
    packed[:, 0:128, :] = early[...]
    place_rows(packed, whiten_rows((first, second, third), whitened), EARLY)
    core = lax.axis_index("core")
    pad = jnp.zeros((8, 128), bf16)
    mine, theirs = (jnp.concatenate([part, pad], axis=0) for part in fold(anchor_grad[...], 40))
    for y in range(4):
        packed[y * 2 + core, 128:176, :] = mine
        packed[y * 2 + 1 - core, 128:176, :] = theirs


def rim_lanes(rims):
    lane = lax.broadcasted_iota(jnp.int32, rims.shape, 1)
    return jnp.where(lane < 6, rims, 0.0), jnp.where(lane >= 122, rims, 0.0)


def image_kernel(parts, packed, middle, carried):
    halves = []
    for k in range(2):
        acc = parts[k].astype(f32)
        for chip in range(1, 8):
            acc = acc + parts[2 * chip + k].astype(f32)
        halves.append(acc)
    gap = jnp.zeros((8, 256), f32)
    whole = jnp.concatenate([halves[0], gap], axis=1) + jnp.concatenate([gap, halves[1]], axis=1)
    turned = pltpu.roll(whole, 640 - 6, 1)
    middle[...] = turned[:, :512]
    later, earlier = rim_lanes(turned[:, 512:])
    y, z, core = (lax.axis_index(name) for name in ("y", "z_hi", "core"))
    later = jnp.where((y == 3) & (z == 3), 0.0, later)
    earlier = jnp.where((y == 0) & (z == 0), 0.0, earlier)
    carried[...] = packed[...]
    for target in range(4):
        rims = jnp.where(y + 1 == target, later, 0.0) + jnp.where(y - 1 == target, earlier, 0.0)
        if target == 0:
            rims = rims + jnp.where(y == 3, pltpu.roll(later, 64, 1), 0.0)
        if target == 3:
            rims = rims + jnp.where(y == 0, pltpu.roll(earlier, 64, 1), 0.0)
        slot = target * 2 + core
        anchor = packed[slot, 128:176, :].astype(f32)[:40]
        carried[slot, 128:176, :] = jnp.concatenate([anchor, rims], axis=0).astype(bf16)


def pack_kernel(received, kept, next_one, next_two, next_three, sums):
    total = received[0].astype(f32)
    for source in range(1, 8):
        total = total + received[source].astype(f32)
    sums[...] = total[0:128]
    straight = rim_lanes(total[168:176])
    onward = rim_lanes(pltpu.roll(total[168:176], 64, 1))
    rims = (straight[0] + straight[1], onward[0], jnp.zeros((8, 128), f32), onward[1])
    for step, packed in enumerate((kept, next_one, next_two, next_three)):
        z = lax.rem(lax.axis_index("z_hi") + step, 4)
        packed[0:32, :] = sums[pl.ds(pl.multiple_of(z * 32, 32), 32), :].astype(bf16)
        packed[32:80, :] = jnp.concatenate([total[128:168], rims[step]], axis=0).astype(bf16)


def unpack_kernel(kept, one, two, three, middle, grad_anchors, grad_whiten, grad_image):
    total = sum(ref[...].astype(f32) for ref in (one, two, three)) + kept[...].astype(f32)
    other = pltpu.roll(total, OWN, 1)
    grad_whiten[0:32, :] = total[0:32, :OWN]
    grad_whiten[32:64, :] = other[0:32, :OWN]
    turned = jnp.concatenate([total[32:72], other[32:72]], axis=0).T[:OWN]
    grad_anchors[...] = lax.dot_general(
        turned, entry_order(f32), (((1,), (1,)), ((), ())),
        precision=lax.Precision.HIGHEST, preferred_element_type=f32,
    )
    first, last = rim_lanes(total[72:80])
    image = middle[...] + jnp.concatenate([first, jnp.zeros((8, 256), f32), last], axis=1)
    for colour in range(3):
        grad_image[colour] = image[2 * colour : 2 * colour + 2]


def halve_kernel(first, second, after, upper, lower):
    del after
    upper[...] = first[:OWN]
    lower[...] = second[OWN:]


def join_kernel(upper, lower, joined):
    joined[:OWN] = upper[...]
    joined[OWN:] = lower[...]


def hold(value, *after):
    def kernel(*refs):
        del refs

    return pl.pallas_call(
        kernel,
        out_shape=jax.ShapeDtypeStruct(value.shape, value.dtype),
        in_specs=[pl.BlockSpec(memory_space=pl.ANY)] * (1 + len(after)),
        out_specs=pl.BlockSpec(memory_space=pl.ANY),
        input_output_aliases={0: 0},
        compiler_params=pltpu.CompilerParams(vmem_limit_bytes=MIB),
        cost_estimate=pl.CostEstimate(flops=1000, bytes_accessed=1000, transcendentals=0),
    )(value, *after)


def call(kernel, outs, scratch, flops, limit, *args, loose=0):
    size = lambda shape, dtype: math.prod(shape) * jnp.dtype(dtype).itemsize
    tight = len(args) - loose
    moved = sum(size(a.shape, a.dtype) for a in args[:tight]) + sum(size(*out) for out in outs)
    return pl.pallas_call(
        kernel,
        out_shape=[jax.ShapeDtypeStruct(shape, dtype) for shape, dtype in outs],
        in_specs=[pl.BlockSpec(memory_space=pltpu.VMEM)] * tight
        + [pl.BlockSpec(memory_space=pl.ANY)] * loose,
        out_specs=[pl.BlockSpec(memory_space=pltpu.VMEM)] * len(outs),
        scratch_shapes=[pltpu.VMEM(shape, dtype) for shape, dtype in scratch],
        compiler_params=pltpu.CompilerParams(vmem_limit_bytes=limit * MIB),
        cost_estimate=pl.CostEstimate(flops=flops, bytes_accessed=moved, transcendentals=0),
    )(*args)


def shards(image, mask, anchors, whiten, cotangent):
    second = on_second()

    def send(value, dx, dz, other):
        return lax.ppermute(value, CHAN, route(dx, dz, other))

    def cross(value):
        return lax.ppermute(value, STRIPS + CHAN, seams())

    left, right = cotangent[:, :, :HALF], cotangent[:, :, HALF:]
    own = jnp.where(second, right, left).reshape(OWN, -1)
    away = jnp.where(second, left, right).reshape(OWN, -1)
    block = jnp.concatenate([own, send(away, 0, 0, 1)], axis=0)
    held = {(0, 0): [block]}
    for dx, dz in ((1, 0), (3, 0), (0, 1)):
        held[(4 - dx) % 4, dz] = [send(block, dx, dz, 0)]
    both = jnp.concatenate(
        [jnp.pad(whiten, ((0, 0), (0, OWN))), jnp.pad(anchors, ((0, 0), (0, 53)))], axis=0
    )
    partner_both = send(both, 0, 0, 1)

    stacked = jnp.concatenate([image, mask.astype(bf16)[None]], axis=0)
    (tile,) = call(
        rim_kernel,
        [((4, ROWS, 128), bf16)],
        [],
        1_000_000,
        4,
        stacked, partner_both,
        loose=1,
    )
    half = ((OWN, 16 * HALF), bf16)
    upper, lower = call(
        halve_kernel, [half, half], [], 1_000_000, 4, held[3, 0][0], held[1, 0][0], tile, loose=1
    )
    far = [send(upper, 1, 0, 0), send(lower, 3, 0, 0)]
    (opposite,) = call(join_kernel, [((2 * OWN, 16 * HALF), bf16)], [], 1_000_000, 4, *far)
    beside = hold(held[0, 1][0], opposite)
    held[2, 0] = [opposite]
    held[3, 1] = [send(beside, 1, 0, 0)]
    held[1, 1] = [send(beside, 3, 0, 0)]
    held[2, 1] = [send(opposite, 0, 1, 0)]
    held[0, 1] = [beside]
    blocks = [part for chip in CHIPS for part in held[chip]]

    plane = ((ROWS, LANES), f32)
    patches, tissue, scale, norm, inv_square, inv_density, anch, anch_t, wturned = call(
        patch_kernel,
        [
            ((36 * GROUP, LANES), bf16),
            plane,
            plane,
            plane,
            plane,
            ((16, HALF), f32),
            ((128, 80), bf16),
            ((80, 128), bf16),
            ((128, 1024), bf16),
        ],
        [],
        1_000_000_000,
        12,
        stacked, cross(tile), both, partner_both, beside,
        loose=1,
    )
    masked, whitened = call(
        forward_kernel,
        [((ROWS, 128, LANES), bf16), ((128, 16 * HALF), bf16)],
        [((ROWS, 128, HALF), f32), ((LANES, HALF), bf16)],
        3_000_000_000,
        14,
        patches, tissue, scale, norm, inv_density, anch,
    )
    partial, early = call(
        early_kernel,
        [((128, 16 * HALF), f32), ((8, 128, 128), bf16)],
        [],
        2_000_000_000,
        14,
        *blocks[:5], wturned, whitened,
    )
    anchor_grad, image_part = call(
        backward_kernel,
        [((80, 128), f32), ((128, LANES), bf16)],
        [((ROWS * 128, HALF), bf16), ((36 * GROUP, LANES), f32), ((HALF, LANES), bf16)],
        5_000_000_000,
        20,
        *blocks[5:],
        partial, wturned, inv_density, masked, patches, inv_square, anch_t,
    )

    parts = lax.all_to_all(image_part.reshape(16, 8, LANES), CHAN, 0, 0)
    packed_shape = ((8, 176, 128), bf16)
    (packed,) = call(
        finish_kernel, [packed_shape], [], 1_000_000_000, 12, *blocks[5:], whitened, early, anchor_grad
    )
    middle, packed = call(
        image_kernel, [((8, 512), f32), packed_shape], [], 1_000_000, 6, parts, packed
    )
    received = lax.all_to_all(packed, ("y", "core"), 0, 0)
    quarter = ((80, 128), bf16)
    kept, *away = call(pack_kernel, [quarter] * 4, [((128, 128), f32)], 1_000_000, 4, received)
    others = [
        lax.ppermute(value, "z_hi", [(z, (z + step) % 4) for z in range(4)])
        for step, value in enumerate(away, 1)
    ]
    return tuple(
        call(
            unpack_kernel,
            [((OWN, 75), f32), ((OWN, OWN), f32), ((3, 2, 512), f32)],
            [],
            1_000_000,
            4,
            kept, *others, middle,
        )
    )


def solution(mesh):
    fine = Mesh(mesh.devices.reshape(4, 4, 4, 2, 2), STRIPS + CHAN)
    placed = (
        P(None, None, STRIPS),
        P(None, STRIPS),
        P(CHAN, None),
        P(None, CHAN),
        P(CHAN, None, STRIPS),
    )
    return jax.shard_map(
        shards,
        mesh=fine,
        in_specs=placed,
        out_specs=(P(CHAN, None), P(STRIPS, CHAN), P(None, CHAN, STRIPS)),
        check_vma=False,
    )
```

```python
import math

import jax
import jax.numpy as jnp
from jax import lax
from jax.experimental import pallas as pl
from jax.experimental.pallas import tpu as pltpu
from jax.sharding import Mesh
from jax.sharding import PartitionSpec as P

EPS = 1e-05
LANES = 384
HALF = 128
ROWS = 32
GROUP = 16
OWN = 64
STEP = 4
EARLY = 14
MIB = 1024 * 1024

ORDER = (
    (0, 0, 0), (0, 0, 1), (0, 1, 0), (0, 1, 1), (1, 0, 0), (1, 0, 1), (3, 0, 0), (3, 0, 1),
    (2, 0, 0), (3, 1, 0), (2, 0, 1), (1, 1, 1), (3, 1, 1), (1, 1, 0),
    (2, 1, 0), (2, 1, 1),
)
STRIPS = ("z_hi", "y")
CHAN = ("x", "z_lo", "core")


def route(dx, dz, core):
    return [(i, ((i // 4 + dx) % 4) * 4 + ((i // 2) % 2 ^ dz) * 2 + (i % 2 ^ core)) for i in range(16)]


def seams():
    pairs = [(16 * s + 2 * q, 16 * s - 16 + 2 * q + 1) for s in range(1, 16) for q in range(8)]
    return pairs + [(b, a) for a, b in pairs]


f32 = jnp.float32
bf16 = jnp.bfloat16


def tap(distance):
    return math.exp(-distance * distance / 8.0) if abs(distance) <= 4 else 0.0


def taps(distance):
    far = jnp.abs(distance) > 4
    distance = distance.astype(f32)
    return jnp.where(far, 0.0, jnp.exp(distance * distance * (-1.0 / 8.0)))


def places(shape):
    return tuple(lax.broadcasted_iota(jnp.int32, shape, dim) for dim in (0, 1))


def column_pool():
    lane, target = places((LANES, HALF))
    return taps(2 * target - lane + 4).astype(bf16)


def column_spread():
    target, lane = places((HALF, LANES))
    return taps(2 * target - lane + 4).astype(bf16)


def row_pool():
    a, i = places((ROWS // 2, ROWS))
    return taps(2 * a - i)


def split_group(row):
    q = row & (GROUP - 1)
    colour = jnp.where(q < 5, 0, jnp.where(q < 10, 1, jnp.where(q < 15, 2, 3)))
    return row >> 4, colour, q - 5 * colour


def ones(hit, dtype=bf16):
    return jnp.where(hit, 1.0, 0.0).astype(dtype)


def replicate_rows():
    out, src = places((36 * GROUP, 3 * ROWS))
    r, colour, _ = split_group(out)
    return ones(((src & 31) == r - 2) & ((src >> 5) == colour))


def fold_rows():
    out, src = places((128, 36 * GROUP))
    r, colour, _ = split_group(src)
    i = 2 * (out >> 3) + (out & 1)
    return ones((r == i + 2) & (colour == ((out & 7) >> 1)) & (colour < 3))


def entry_order(dtype, rows=75):
    entry, out = places((rows, 80))
    a, colour, b = split_group(out)
    return ones((entry == 25 * colour + 5 * a + b) & (colour < 3), dtype)


def on_second():
    return lax.axis_index("core") == 1


def block_of(p):
    dx, dz, other = ORDER[p]
    ex = lax.rem(lax.axis_index("x") + dx, 4)
    zed = lax.rem(lax.axis_index("z_lo") + dz, 2)
    core = lax.rem(lax.axis_index("core") + other, 2)
    return ex * 4 + zed * 2 + core


def dot(a, b):
    return jnp.dot(a, b, preferred_element_type=f32)


def dot_nt(a, b):
    return lax.dot_general(a, b, (((1,), (1,)), ((), ())), preferred_element_type=f32)


def rim_kernel(stacked, *refs):
    tile = refs[-1]
    second = on_second()
    for c in range(4):
        value = stacked[c].astype(f32)
        tile[c] = jnp.where(second, value[:, 384:], value[:, :128]).astype(bf16)


def patch_kernel(
    stacked, beyond, own_both, partner_both,
    patches, tissue, scale, norm, inv_square, inv_density, anch, anch_t, wturned,
):
    second = on_second()

    def half(c, shift):
        middle, rim = stacked[c].astype(f32), beyond[c].astype(f32)
        wide = jnp.concatenate([rim, middle, rim], axis=1)
        part = jnp.where(second, wide[:, 256:], wide[:, :512])
        return pltpu.roll(part, 512 - shift, 1)[:, :LANES]

    colours = [half(c, 122) for c in range(3)]
    here = half(3, 124)
    lane = lax.broadcasted_iota(jnp.int32, here.shape, 1)
    here = jnp.where(lane < 263, here, 0.0)
    tissue[...] = here
    x = dot(replicate_rows(), jnp.concatenate(colours, axis=0).astype(bf16))
    offset = (lax.broadcasted_iota(jnp.int32, x.shape, 0) % GROUP) % 5
    s = x
    for b in range(1, 5):
        s = jnp.where(offset == b, pltpu.roll(x, LANES - b, 1), s)
    patches[...] = s.astype(bf16)
    square = jnp.sum((s * s).reshape(36, GROUP, LANES), axis=1)
    total = square[0:ROWS]
    for a in range(1, 5):
        total = total + square[a : a + ROWS]
    total = total + EPS
    root = lax.rsqrt(total)
    scale[...] = 4.0 * root
    norm[...] = total * root
    inv_square[...] = 1.0 / total
    counted = dot(here.astype(bf16), column_pool())
    density = jnp.dot(row_pool(), counted, precision=lax.Precision.HIGHEST, preferred_element_type=f32)
    inv_density[...] = 1.0 / jnp.maximum(density, 1.0)
    both = jnp.concatenate([own_both[1024:1088, :], partner_both[1024:1088, :]], axis=0)
    ordered = dot(both, entry_order(bf16, 128))
    anch[...] = ordered.astype(bf16)
    anch_t[...] = ordered.T.astype(bf16)
    blocks = [pl.ds(pl.multiple_of(block_of(p) * OWN, OWN), OWN) for p in range(16)]
    for at, both in ((0, own_both), (OWN, partner_both)):
        ordered = jnp.concatenate([both[block, :] for block in blocks], axis=0)
        wturned[at : at + OWN, :] = ordered.astype(f32).T[:OWN].astype(bf16)


def forward_kernel(
    patches, tissue, scale, norm, inv_density, anch,
    masked, whitened,
    columned, pool,
):
    pool[...] = column_pool()

    @pl.loop(0, ROWS // STEP)
    def _(t):
        lifted = []
        for r in range(STEP):
            i = t * STEP + r
            patch = patches[pl.ds(pl.multiple_of(i * GROUP, GROUP), 80), :]
            raw = dot(anch[...], patch)
            value = jnp.exp(raw * scale[pl.ds(i, 1), :] - 4.0) * tissue[pl.ds(i, 1), :]
            masked[i] = value.astype(bf16)
            lifted.append((value * norm[pl.ds(i, 1), :]).astype(bf16))
        result = dot(jnp.concatenate(lifted, axis=0), pool[...])
        columned[pl.ds(t * STEP, STEP)] = result.reshape(STEP, 128, HALF)

    for a in range(ROWS // 2):
        acc = None
        for i in range(max(0, 2 * a - 4), min(ROWS, 2 * a + 5)):
            term = tap(2 * a - i) * columned[i]
            acc = term if acc is None else acc + term
        whitened[:, a * HALF : (a + 1) * HALF] = (acc * inv_density[a : a + 1, :]).astype(bf16)


def fold(block, rows):
    top, low = block[:rows], block[rows:]
    left = lax.broadcasted_iota(jnp.int32, top.shape, 1) < OWN
    own = jnp.where(left, top, pltpu.roll(low, OWN, 1))
    partner = jnp.where(left, pltpu.roll(top, OWN, 1), low)
    return own.astype(bf16), partner.astype(bf16)


def stacks(blocks):
    for n in range(8):
        cols = slice(n * 256, (n + 1) * 256)
        yield cols, jnp.concatenate([block[:, cols] for block in blocks], axis=0)


def whiten_rows(blocks, whitened):
    return sum(dot_nt(stack, whitened[:, cols]) for cols, stack in stacks(blocks))


def place_rows(own, partner, grad_w, first):
    for n in range(grad_w.shape[0] // OWN):
        strip = block_of(first + n)
        place = lax.rem(strip, 4) * 4 + strip // 4
        rows = pl.ds(pl.multiple_of(place * 32, 32), 32)
        own[rows, :], partner[rows, :] = fold(grad_w[n * OWN : (n + 1) * OWN], OWN // 2)


def early_kernel(*refs):
    blocks, (wturned, whitened, partial, own, partner) = refs[:7], refs[7:]
    own[...] = jnp.zeros_like(own)
    partner[...] = jnp.zeros_like(partner)
    for cols, stack in stacks(blocks):
        partial[:, cols] = dot(wturned[:, : EARLY * OWN], stack)
    place_rows(own, partner, whiten_rows(blocks, whitened), 0)


def backward_kernel(*refs):
    blocks = refs[:2]
    (
        partial, wturned, inv_density, masked, patches, inv_square, anch_t,
        anchor_grad, image,
        rowed, spread_grad, pool_t,
    ) = refs[2:]
    pool_t[...] = column_spread()
    pooled = [
        partial[:, cols] + dot(wturned[:, EARLY * OWN :], stack) for cols, stack in stacks(blocks)
    ]
    scaled = []
    for a in range(ROWS // 2):
        part = pooled[a // 2][:, (a % 2) * HALF : (a % 2 + 1) * HALF]
        scaled.append(part.astype(bf16).astype(f32) * inv_density[a : a + 1, :])
    for i in range(ROWS):
        acc = None
        for a in range(ROWS // 2):
            if abs(2 * a - i) <= 4:
                term = (4.0 * tap(2 * a - i)) * scaled[a]
                acc = term if acc is None else acc + term
        rowed[i * 128 : (i + 1) * 128, :] = acc.astype(bf16)
    spread_grad[...] = jnp.zeros_like(spread_grad)
    anchor_grad[...] = jnp.zeros_like(anchor_grad)

    @pl.loop(0, ROWS // STEP)
    def _(t):
        start = pl.multiple_of(t * (STEP * 128), STEP * 128)
        spread = dot(rowed[pl.ds(start, STEP * 128), :], pool_t[...])
        grads, wides, units = [], [], []
        for r in range(STEP):
            i = t * STEP + r
            patch = patches[pl.ds(pl.multiple_of(i * GROUP, GROUP), 80), :]
            grad = (spread[r * 128 : (r + 1) * 128] * masked[i].astype(f32)).astype(bf16)
            unit = dot(anch_t[...], grad)
            wide = patch.astype(f32)
            along = jnp.sum(wide * unit, axis=0, keepdims=True) * inv_square[pl.ds(i, 1), :]
            units.append(unit - wide * along)
            grads.append(grad)
            wides.append(patch)
        anchor_grad[...] += dot_nt(jnp.concatenate(wides, axis=1), jnp.concatenate(grads, axis=1))
        sums = []
        for g in range(STEP + 4):
            acc = None
            for r in range(STEP):
                if 0 <= g - r < 5:
                    term = units[r][(g - r) * GROUP : (g - r + 1) * GROUP]
                    acc = term if acc is None else acc + term
            sums.append(acc)
        here = pl.ds(pl.multiple_of(t * (STEP * GROUP), STEP * GROUP), (STEP + 4) * GROUP)
        spread_grad[here, :] += jnp.concatenate(sums, axis=0)

    t = spread_grad[...]
    offset = (lax.broadcasted_iota(jnp.int32, t.shape, 0) % GROUP) % 5
    moved = t
    for b in range(1, 5):
        moved = jnp.where(offset == b, pltpu.roll(t, b, 1), moved)
    high = moved.astype(bf16)
    low = (moved - high.astype(f32)).astype(bf16)
    folder = fold_rows()
    image[...] = (dot(folder, high) + dot(folder, low)).astype(bf16)


def finish_kernel(first, second, whitened, early_own, early_partner, anchor_grad, own, partner):
    own[0:512, :] = early_own[...]
    partner[0:512, :] = early_partner[...]
    place_rows(own, partner, whiten_rows((first, second), whitened), EARLY)
    pad = jnp.zeros((8, 128), bf16)
    mine, theirs = fold(anchor_grad[...], 40)
    own[512:560, :] = jnp.concatenate([mine, pad], axis=0)
    partner[512:560, :] = jnp.concatenate([theirs, pad], axis=0)


def chip_kernel(own, partner, kept, next_one, next_two, next_three, sums):
    sums[...] = own[...].astype(f32) + partner[...].astype(f32)
    for step, part in enumerate((kept, next_one, next_two, next_three)):
        y = lax.rem(lax.axis_index("y") + step, 4)
        part[0:128, :] = sums[pl.ds(pl.multiple_of(y * 128, 128), 128), :].astype(bf16)
        part[128:176, :] = sums[512:560, :].astype(bf16)


def add_four(refs):
    first, *others = refs
    total = first[...].astype(f32)
    for ref in others:
        total = total + ref[...].astype(f32)
    return total


def pack_kernel(kept, one, two, three, packed):
    total = add_four((kept, one, two, three)).astype(bf16)
    for z in range(4):
        packed[z, 0:32, :] = total[z * 32 : (z + 1) * 32]
        packed[z, 32:80, :] = total[128:176]


def image_kernel(parts, middle, rims):
    halves = []
    for k in range(2):
        acc = parts[k].astype(f32)
        for chip in range(1, 8):
            acc = acc + parts[2 * chip + k].astype(f32)
        halves.append(acc)
    gap = jnp.zeros((8, 256), f32)
    whole = jnp.concatenate([halves[0], gap], axis=1) + jnp.concatenate([gap, halves[1]], axis=1)
    turned = pltpu.roll(whole, 640 - 6, 1)
    middle[...] = turned[:, :512]
    rims[...] = turned[:, 512:]


def unpack_kernel(
    received, middle, before, after,
    grad_anchors, grad_whiten, grad_image,
):
    total = add_four([received.at[z] for z in range(4)])
    other = pltpu.roll(total, OWN, 1)
    grad_whiten[0:32, :] = total[0:32, :OWN]
    grad_whiten[32:64, :] = other[0:32, :OWN]
    turned = jnp.concatenate([total[32:72], other[32:72]], axis=0).T[:OWN]
    grad_anchors[...] = lax.dot_general(
        turned, entry_order(f32), (((1,), (1,)), ((), ())),
        precision=lax.Precision.HIGHEST, preferred_element_type=f32,
    )
    lane = lax.broadcasted_iota(jnp.int32, before.shape, 1)
    first = jnp.where(lane < 6, before[...], 0.0)
    last = jnp.where(lane >= 122, after[...], 0.0)
    gap = jnp.zeros((8, 256), f32)
    image = middle[...] + jnp.concatenate([first, gap, last], axis=1)
    for colour in range(3):
        grad_image[colour] = image[2 * colour : 2 * colour + 2]


def mix_kernel(last, following, beside, right, left, across):
    right[:OWN], right[OWN:] = last[:OWN], beside[:OWN]
    left[:OWN], left[OWN:] = following[OWN:], beside[OWN:]
    across[:OWN], across[OWN:] = last[OWN:], following[:OWN]


def cut_kernel(right, left, across, after, onward, over):
    del across, after
    onward[...] = right[OWN:]
    over[...] = left[:OWN]


def call(kernel, outs, scratch, flops, limit, *args, loose=0):
    size = lambda shape, dtype: math.prod(shape) * jnp.dtype(dtype).itemsize
    tight = len(args) - loose
    moved = sum(size(a.shape, a.dtype) for a in args[:tight]) + sum(size(*out) for out in outs)
    return pl.pallas_call(
        kernel,
        out_shape=[jax.ShapeDtypeStruct(shape, dtype) for shape, dtype in outs],
        in_specs=[pl.BlockSpec(memory_space=pltpu.VMEM)] * tight
        + [pl.BlockSpec(memory_space=pl.ANY)] * loose,
        out_specs=[pl.BlockSpec(memory_space=pltpu.VMEM)] * len(outs),
        scratch_shapes=[pltpu.VMEM(shape, dtype) for shape, dtype in scratch],
        compiler_params=pltpu.CompilerParams(vmem_limit_bytes=limit * MIB),
        cost_estimate=pl.CostEstimate(flops=flops, bytes_accessed=moved, transcendentals=0),
    )(*args)


def shards(image, mask, anchors, whiten, cotangent):
    second = on_second()

    def send(value, dx, dz, other):
        return lax.ppermute(value, CHAN, route(dx, dz, other))

    def cross(value):
        return lax.ppermute(value, STRIPS + CHAN, seams())

    left, right = cotangent[:, :, :HALF], cotangent[:, :, HALF:]
    own = jnp.where(second, right, left).reshape(OWN, -1)
    away = jnp.where(second, left, right).reshape(OWN, -1)
    block = jnp.concatenate([own, send(away, 0, 0, 1)], axis=0)
    last, following, beside = send(block, 1, 0, 0), send(block, 3, 0, 0), send(block, 0, 1, 0)
    pair = ((2 * OWN, 16 * HALF), bf16)
    right, left, across = call(mix_kernel, [pair] * 3, [], 1_000_000, 6, last, following, beside)
    right, left, across = send(right, 1, 0, 0), send(left, 3, 0, 0), send(across, 0, 1, 0)
    both = jnp.concatenate(
        [jnp.pad(whiten, ((0, 0), (0, OWN))), jnp.pad(anchors, ((0, 0), (0, 53)))], axis=0
    )
    partner_both = send(both, 0, 0, 1)

    stacked = jnp.concatenate([image, mask.astype(bf16)[None]], axis=0)
    (tile,) = call(
        rim_kernel,
        [((4, ROWS, 128), bf16)],
        [],
        1_000_000,
        4,
        stacked, partner_both,
        loose=1,
    )
    plane = ((ROWS, LANES), f32)
    patches, tissue, scale, norm, inv_square, inv_density, anch, anch_t, wturned = call(
        patch_kernel,
        [
            ((36 * GROUP, LANES), bf16),
            plane,
            plane,
            plane,
            plane,
            ((16, HALF), f32),
            ((128, 80), bf16),
            ((80, 128), bf16),
            ((128, 1024), bf16),
        ],
        [],
        10_000_000_000,
        12,
        stacked, cross(tile), both, partner_both,
    )
    masked, whitened = call(
        forward_kernel,
        [((ROWS, 128, LANES), bf16), ((128, 16 * HALF), bf16)],
        [((ROWS, 128, HALF), f32), ((LANES, HALF), bf16)],
        30_000_000_000,
        14,
        patches, tissue, scale, norm, inv_density, anch,
    )
    onward, over = call(
        cut_kernel, [((OWN, 16 * HALF), bf16)] * 2, [], 1_000_000, 6, right, left, across, whitened, loose=2
    )
    first_blocks = (block, beside, following, last, right, left, across)
    last_blocks = (send(onward, 1, 0, 0), send(over, 0, 1, 0))
    rows = ((512, 128), bf16)
    partial, early_own, early_partner = call(
        early_kernel,
        [((128, 16 * HALF), f32), rows, rows],
        [],
        2_000_000_000,
        14,
        *first_blocks, wturned, whitened,
    )
    anchor_grad, image_part = call(
        backward_kernel,
        [((80, 128), f32), ((128, LANES), bf16)],
        [((ROWS * 128, HALF), bf16), ((36 * GROUP, LANES), f32), ((HALF, LANES), bf16)],
        5_000_000_000,
        20,
        *last_blocks, partial, wturned, inv_density, masked, patches, inv_square, anch_t,
    )

    parts = lax.all_to_all(image_part.reshape(16, 8, LANES), CHAN, 0, 0)
    rows = ((560, 128), bf16)
    mine, theirs = call(
        finish_kernel,
        [rows, rows],
        [],
        1_000_000_000,
        12,
        *last_blocks, whitened, early_own, early_partner, anchor_grad,
    )

    def exchange(values, axis):
        return [
            lax.ppermute(value, axis, [(i, (i + step) % 4) for i in range(4)])
            for step, value in enumerate(values, 1)
        ]

    kept, *away = call(
        chip_kernel,
        [((176, 128), bf16)] * 4,
        [((560, 128), f32)],
        1_000_000,
        6,
        mine, send(theirs, 0, 0, 1),
    )
    (packed,) = call(
        pack_kernel, [((4, 80, 128), bf16)], [], 1_000_000, 4, kept, *exchange(away, "y")
    )
    received = lax.all_to_all(packed, "z_hi", 0, 0)
    middle, rims = call(image_kernel, [((8, 512), f32), ((8, 128), f32)], [], 1_000_000, 4, parts)
    before = lax.ppermute(rims, STRIPS, [(i, i + 1) for i in range(15)])
    after = lax.ppermute(rims, STRIPS, [(i + 1, i) for i in range(15)])
    return tuple(
        call(
            unpack_kernel,
            [((OWN, 75), f32), ((OWN, OWN), f32), ((3, 2, 512), f32)],
            [],
            1_000_000,
            4,
            received, middle, before, after,
        )
    )


def solution(mesh):
    fine = Mesh(mesh.devices.reshape(4, 4, 4, 2, 2), STRIPS + CHAN)
    placed = (
        P(None, None, STRIPS),
        P(None, STRIPS),
        P(CHAN, None),
        P(None, CHAN),
        P(CHAN, None, STRIPS),
    )
    return jax.shard_map(
        shards,
        mesh=fine,
        in_specs=placed,
        out_specs=(P(CHAN, None), P(STRIPS, CHAN), P(None, CHAN, STRIPS)),
        check_vma=False,
    )
```

```python
import math

import jax
import jax.numpy as jnp
from jax import lax
from jax.experimental import pallas as pl
from jax.experimental.pallas import tpu as pltpu
from jax.sharding import Mesh
from jax.sharding import PartitionSpec as P

EPS = 1e-05
LANES = 256
REACH = 135
QUARTER = 64
FLAT = 16 * QUARTER
ROWS = 32
GROUP = 16
OWN = 64
KEPT = 4 * OWN
STEP = 4
EARLY = 12
MIB = 1024 * 1024

STRIPS = ("z_hi", "y")
CHAN = ("x", "z_lo", "core")


def route(dx, other):
    return [(i, (i // 4 + dx) % 4 * 4 + (i % 4 ^ other)) for i in range(16)]


def seams():
    pairs = [(16 * s + 4 * x, 16 * s - 16 + 4 * x + 3) for s in range(1, 16) for x in range(4)]
    return pairs + [(b, a) for a, b in pairs]


f32 = jnp.float32
bf16 = jnp.bfloat16


def tap(distance):
    return math.exp(-distance * distance / 8.0) if abs(distance) <= 4 else 0.0


def taps(distance):
    far = jnp.abs(distance) > 4
    distance = distance.astype(f32)
    return jnp.where(far, 0.0, jnp.exp(distance * distance * (-1.0 / 8.0)))


def places(shape):
    return tuple(lax.broadcasted_iota(jnp.int32, shape, dim) for dim in (0, 1))


def column_pool():
    lane, target = places((LANES, 128))
    return taps(2 * (target & 63) - lane + 4).astype(bf16)


def column_spread():
    target, lane = places((128, LANES))
    return taps(2 * (target & 63) - lane + 4).astype(bf16)


def row_weights(t, i):
    low, high = tap(4 * t - i), tap(4 * t + 2 - i)
    if low == 0.0 and high == 0.0:
        return None
    return jnp.where(lax.broadcasted_iota(jnp.int32, (1, 128), 1) < QUARTER, low, high)


def row_pool(odd):
    t, i = places((8, ROWS))
    return taps(4 * t + 2 * odd - i)


def split_group(row):
    q = row & (GROUP - 1)
    colour = jnp.where(q < 5, 0, jnp.where(q < 10, 1, jnp.where(q < 15, 2, 3)))
    return row >> 4, colour, q - 5 * colour


def ones(hit, dtype=bf16):
    return jnp.where(hit, 1.0, 0.0).astype(dtype)


def replicate_rows():
    out, src = places((36 * GROUP, 3 * ROWS))
    r, colour, _ = split_group(out)
    return ones(((src & 31) == r - 2) & ((src >> 5) == colour))


def fold_rows():
    out, src = places((128, 36 * GROUP))
    r, colour, _ = split_group(src)
    i = 2 * (out >> 3) + (out & 1)
    return ones((r == i + 2) & (colour == ((out & 7) >> 1)) & (colour < 3))


def entry_order(dtype, rows=75):
    entry, out = places((rows, 80))
    a, colour, b = split_group(out)
    return ones((entry == 25 * colour + 5 * a + b) & (colour < 3), dtype)


def quarter():
    return lax.axis_index("z_lo") * 2 + lax.axis_index("core")


def flipped(axis, bit):
    return lax.rem(lax.axis_index(axis) + bit, 2)


def block_of(p):
    dx, other = (0, 1, 3, 2)[p // 4], p % 4
    ex = lax.rem(lax.axis_index("x") + dx, 4)
    return ex * 4 + flipped("z_lo", other // 2) * 2 + flipped("core", other % 2)


def dot(a, b):
    return jnp.dot(a, b, preferred_element_type=f32)


def dot_nt(a, b):
    return lax.dot_general(a, b, (((1,), (1,)), ((), ())), preferred_element_type=f32)


def quarter_kernel(cotangent, own, core, zed, both, parts):
    lane = lax.broadcasted_iota(jnp.int32, (OWN, 128), 1)
    for t in range(8):
        low, high = (cotangent[:, 2 * t + n, :].astype(f32) for n in (0, 1))
        for side in range(2):
            cols = slice(side * 128, side * 128 + 128)
            even = jnp.where(lane < QUARTER, low[:, cols], pltpu.roll(high[:, cols], QUARTER, 1))
            odd = jnp.where(lane < QUARTER, pltpu.roll(low[:, cols], QUARTER, 1), high[:, cols])
            parts[2 * side, :, t * 128 : (t + 1) * 128] = even.astype(bf16)
            parts[2 * side + 1, :, t * 128 : (t + 1) * 128] = odd.astype(bf16)
    for other, part in enumerate((own, core, zed, both)):
        part[...] = parts[flipped("z_lo", other // 2) * 2 + flipped("core", other % 2)]


def join_kernel(*refs):
    joined = refs[-1]
    start = 0
    for ref in refs[:-1]:
        joined[start : start + ref.shape[0]] = ref[...]
        start += ref.shape[0]


def halve_kernel(first, second, after, upper, lower):
    del after
    upper[...] = first[: KEPT // 2]
    lower[...] = second[KEPT // 2 :]


def rim_kernel(stacked, *refs):
    tile = refs[-1]
    first = quarter() == 0
    for c in range(4):
        value = stacked[c].astype(f32)
        tile[c] = jnp.where(first, value[:, :128], value[:, 384:]).astype(bf16)


def patch_kernel(
    stacked, beyond, *refs,
):
    shared = refs[:4]
    patches, tissue, scale, norm, inv_square, inv_density, anch, anch_t, wturned, wide = refs[4:]
    start = pl.multiple_of(quarter() * 128, 128)

    def part(c, shift):
        rim = beyond[c].astype(f32)
        wide[:, 0:128] = rim
        wide[:, 128:640] = stacked[c].astype(f32)
        wide[:, 640:768] = rim
        return pltpu.roll(wide[:, pl.ds(start, 384)], 384 - shift, 1)[:, :LANES]

    colours = [part(c, 122) for c in range(3)]
    here = part(3, 124)
    lane = lax.broadcasted_iota(jnp.int32, here.shape, 1)
    here = jnp.where(lane < REACH, here, 0.0)
    tissue[...] = here
    x = dot(replicate_rows(), jnp.concatenate(colours, axis=0).astype(bf16))
    offset = (lax.broadcasted_iota(jnp.int32, x.shape, 0) % GROUP) % 5
    s = x
    for b in range(1, 5):
        s = jnp.where(offset == b, pltpu.roll(x, LANES - b, 1), s)
    patches[...] = s.astype(bf16)
    square = jnp.sum((s * s).reshape(36, GROUP, LANES), axis=1)
    total = square[0:ROWS]
    for a in range(1, 5):
        total = total + square[a : a + ROWS]
    total = total + EPS
    root = lax.rsqrt(total)
    scale[...] = 4.0 * root
    norm[...] = total * root
    inv_square[...] = 1.0 / total
    counted = dot(here.astype(bf16), column_pool())
    even, odd = (
        jnp.dot(row_pool(n), counted, precision=lax.Precision.HIGHEST, preferred_element_type=f32)
        for n in (0, 1)
    )
    lane = lax.broadcasted_iota(jnp.int32, even.shape, 1)
    inv_density[...] = 1.0 / jnp.maximum(jnp.where(lane < QUARTER, even, odd), 1.0)
    anchors = jnp.concatenate([both[1024:1088, :] for both in shared], axis=0)
    ordered = dot(anchors, entry_order(bf16, 128))
    anch[...] = ordered.astype(bf16)
    anch_t[...] = ordered.T.astype(bf16)
    blocks = [pl.ds(pl.multiple_of(block_of(p) * OWN, OWN), OWN) for p in range(16)]
    for n, both in enumerate(shared):
        ordered = jnp.concatenate([both[block, :] for block in blocks], axis=0)
        wturned[n * OWN : (n + 1) * OWN, :] = ordered.astype(f32).T[:OWN].astype(bf16)


def forward_kernel(
    patches, tissue, scale, norm, inv_density, anch,
    masked, whitened,
    columned, pool,
):
    pool[...] = column_pool()

    @pl.loop(0, ROWS // STEP)
    def _(t):
        lifted = []
        for r in range(STEP):
            i = t * STEP + r
            patch = patches[pl.ds(pl.multiple_of(i * GROUP, GROUP), 80), :]
            raw = dot(anch[...], patch)
            value = jnp.exp(raw * scale[pl.ds(i, 1), :] - 4.0) * tissue[pl.ds(i, 1), :]
            masked[i] = value.astype(bf16)
            lifted.append((value * norm[pl.ds(i, 1), :]).astype(bf16))
        result = dot(jnp.concatenate(lifted, axis=0), pool[...])
        columned[pl.ds(t * STEP, STEP)] = result.reshape(STEP, KEPT, 128)

    for t in range(8):
        acc = None
        for i in range(ROWS):
            weights = row_weights(t, i)
            if weights is not None:
                term = weights * columned[i]
                acc = term if acc is None else acc + term
        whitened[:, t * 128 : (t + 1) * 128] = (acc * inv_density[t : t + 1, :]).astype(bf16)


def fold(block, rows):
    top, low = block[:rows], block[rows:]
    left = lax.broadcasted_iota(jnp.int32, top.shape, 1) < OWN
    own = jnp.where(left, top, pltpu.roll(low, OWN, 1))
    partner = jnp.where(left, pltpu.roll(top, OWN, 1), low)
    return own.astype(bf16), partner.astype(bf16)


def stacks(blocks):
    for n in range(FLAT // 256):
        cols = slice(n * 256, (n + 1) * 256)
        yield cols, jnp.concatenate([block[:, cols] for block in blocks], axis=0)


def whiten_rows(blocks, whitened):
    return sum(dot_nt(stack, whitened[:, cols]) for cols, stack in stacks(blocks))


def four_folds(block, rows):
    return fold(block[:, :128], rows) + fold(block[:, 128:], rows)


def place_rows(sums, grad_w, first):
    for n in range(grad_w.shape[0] // OWN):
        strip = block_of(first + n)
        place = lax.rem(strip, 4) * 4 + strip // 4
        rows = pl.ds(pl.multiple_of(place * 32, 32), 32)
        for ref, value in zip(sums, four_folds(grad_w[n * OWN : (n + 1) * OWN], OWN // 2)):
            ref[rows, :] = value


def early_kernel(*refs):
    blocks, (wturned, whitened, partial, *sums) = refs[:3], refs[3:]
    for ref in sums:
        ref[...] = jnp.zeros_like(ref)
    for cols, stack in stacks(blocks):
        partial[:, cols] = dot(wturned[:, : EARLY * OWN], stack)
    place_rows(sums, whiten_rows(blocks, whitened), 0)


def backward_kernel(
    first, second, partial, wturned, inv_density, masked, patches, inv_square, anch_t,
    anchor_grad, image,
    rowed, spread_grad, pool_t,
):
    pool_t[...] = column_spread()
    scaled = []
    for cols, stack in stacks((first, second)):
        pooled = partial[:, cols] + dot(wturned[:, EARLY * OWN :], stack)
        for side in range(2):
            t = len(scaled)
            part = pooled[:, side * 128 : (side + 1) * 128]
            scaled.append(part.astype(bf16).astype(f32) * (4.0 * inv_density[t : t + 1, :]))
    for i in range(ROWS):
        acc = None
        for t in range(8):
            weights = row_weights(t, i)
            if weights is not None:
                term = weights * scaled[t]
                acc = term if acc is None else acc + term
        rowed[i * KEPT : (i + 1) * KEPT, :] = acc.astype(bf16)
    spread_grad[...] = jnp.zeros_like(spread_grad)
    anchor_grad[...] = jnp.zeros_like(anchor_grad)

    @pl.loop(0, ROWS // STEP)
    def _(t):
        start = pl.multiple_of(t * (STEP * KEPT), STEP * KEPT)
        spread = dot(rowed[pl.ds(start, STEP * KEPT), :], pool_t[...])
        grads, wides, units = [], [], []
        for r in range(STEP):
            i = t * STEP + r
            patch = patches[pl.ds(pl.multiple_of(i * GROUP, GROUP), 80), :]
            grad = (spread[r * KEPT : (r + 1) * KEPT] * masked[i].astype(f32)).astype(bf16)
            unit = dot(anch_t[...], grad)
            wide = patch.astype(f32)
            along = jnp.sum(wide * unit, axis=0, keepdims=True) * inv_square[pl.ds(i, 1), :]
            units.append(unit - wide * along)
            grads.append(grad)
            wides.append(patch)
        anchor_grad[...] += dot_nt(jnp.concatenate(wides, axis=1), jnp.concatenate(grads, axis=1))
        sums = []
        for g in range(STEP + 4):
            acc = None
            for r in range(STEP):
                if 0 <= g - r < 5:
                    term = units[r][(g - r) * GROUP : (g - r + 1) * GROUP]
                    acc = term if acc is None else acc + term
            sums.append(acc)
        here = pl.ds(pl.multiple_of(t * (STEP * GROUP), STEP * GROUP), (STEP + 4) * GROUP)
        spread_grad[here, :] += jnp.concatenate(sums, axis=0)

    t = spread_grad[...]
    offset = (lax.broadcasted_iota(jnp.int32, t.shape, 0) % GROUP) % 5
    moved = t
    for b in range(1, 5):
        moved = jnp.where(offset == b, pltpu.roll(t, b, 1), moved)
    high = moved.astype(bf16)
    low = (moved - high.astype(f32)).astype(bf16)
    folder = fold_rows()
    image[...] = (dot(folder, high) + dot(folder, low)).astype(bf16)


def finish_kernel(*refs):
    first, second, whitened, *early = refs[:7]
    anchor_grad, *sums = refs[7:]
    pad = jnp.zeros((8, 128), bf16)
    for ref, start, part in zip(sums, early, four_folds(anchor_grad[...], 40)):
        ref[0:512, :] = start[...]
        ref[512:560, :] = jnp.concatenate([part, pad], axis=0)
    place_rows(sums, whiten_rows((first, second), whitened), EARLY)


def add_up(refs):
    total = refs[0][...].astype(f32)
    for ref in refs[1:]:
        total = total + ref[...].astype(f32)
    return total


def rim_lanes(rims):
    lane = lax.broadcasted_iota(jnp.int32, rims.shape, 1)
    return jnp.where(lane < 6, rims, 0.0), jnp.where(lane >= 122, rims, 0.0)


def chip_kernel(parts, own, one, two, three, middle, kept, next_one, next_two, next_three, sums):
    gap = jnp.zeros((8, 128), f32)
    whole = None
    for q in range(4):
        part = add_up([parts.at[4 * x + q] for x in range(4)])
        pieces = [gap] * q + [part] + [gap] * (3 - q)
        placed = jnp.concatenate(pieces, axis=1)
        whole = placed if whole is None else whole + placed
    turned = pltpu.roll(whole, 640 - 6, 1)
    middle[...] = turned[:, :512]
    later, earlier = rim_lanes(turned[:, 512:])
    y, z = lax.axis_index("y"), lax.axis_index("z_hi")
    later = jnp.where((y == 3) & (z == 3), 0.0, later)
    earlier = jnp.where((y == 0) & (z == 0), 0.0, earlier)
    later = jnp.where(y == 3, pltpu.roll(later, 64, 1), later)
    earlier = jnp.where(y == 0, pltpu.roll(earlier, 64, 1), earlier)
    sums[...] = add_up((own, one, two, three))
    for step, part in enumerate((kept, next_one, next_two, next_three)):
        target = lax.rem(y + step, 4)
        part[0:128, :] = sums[pl.ds(pl.multiple_of(target * 128, 128), 128), :].astype(bf16)
        rims = {1: later, 3: earlier}.get(step, gap)
        part[128:176, :] = jnp.concatenate([sums[512:552, :], rims], axis=0).astype(bf16)


def pack_kernel(kept, one, two, three, packed, sums):
    total = add_up((kept, one, two, three))
    sums[...] = total[0:128]
    straight = rim_lanes(total[168:176])
    onward = rim_lanes(pltpu.roll(total[168:176], 64, 1))
    rims = (straight[0] + straight[1], onward[0], jnp.zeros((8, 128), f32), onward[1])
    for step in range(4):
        z = lax.rem(lax.axis_index("z_hi") + step, 4)
        packed[z, 0:32, :] = sums[pl.ds(pl.multiple_of(z * 32, 32), 32), :].astype(bf16)
        packed[z, 32:80, :] = jnp.concatenate([total[128:168], rims[step]], axis=0).astype(bf16)


def unpack_kernel(received, middle, grad_anchors, grad_whiten, grad_image):
    total = add_up([received.at[z] for z in range(4)])
    other = pltpu.roll(total, OWN, 1)
    grad_whiten[0:32, :] = total[0:32, :OWN]
    grad_whiten[32:64, :] = other[0:32, :OWN]
    turned = jnp.concatenate([total[32:72], other[32:72]], axis=0).T[:OWN]
    grad_anchors[...] = lax.dot_general(
        turned, entry_order(f32), (((1,), (1,)), ((), ())),
        precision=lax.Precision.HIGHEST, preferred_element_type=f32,
    )
    first, last = rim_lanes(total[72:80])
    image = middle[...] + jnp.concatenate([first, jnp.zeros((8, 256), f32), last], axis=1)
    for colour in range(3):
        grad_image[colour] = image[2 * colour : 2 * colour + 2]


def call(kernel, outs, scratch, flops, limit, *args, loose=0):
    size = lambda shape, dtype: math.prod(shape) * jnp.dtype(dtype).itemsize
    tight = len(args) - loose
    moved = sum(size(a.shape, a.dtype) for a in args[:tight]) + sum(size(*out) for out in outs)
    return pl.pallas_call(
        kernel,
        out_shape=[jax.ShapeDtypeStruct(shape, dtype) for shape, dtype in outs],
        in_specs=[pl.BlockSpec(memory_space=pltpu.VMEM)] * tight
        + [pl.BlockSpec(memory_space=pl.ANY)] * loose,
        out_specs=[pl.BlockSpec(memory_space=pltpu.VMEM)] * len(outs),
        scratch_shapes=[pltpu.VMEM(shape, dtype) for shape, dtype in scratch],
        compiler_params=pltpu.CompilerParams(vmem_limit_bytes=limit * MIB),
        cost_estimate=pl.CostEstimate(flops=flops, bytes_accessed=moved, transcendentals=0),
    )(*args)


def shards(image, mask, anchors, whiten, cotangent):
    def send(value, dx, other):
        return lax.ppermute(value, CHAN, route(dx, other))

    part = ((OWN, FLAT), bf16)
    own, *away = call(
        quarter_kernel, [part] * 4, [((4, OWN, FLAT), bf16)], 1_000_000, 6, cotangent
    )
    (block,) = call(
        join_kernel,
        [((KEPT, FLAT), bf16)],
        [],
        1_000_000,
        4,
        own, *(send(value, 0, other) for other, value in enumerate(away, 1)),
    )
    last, following = send(block, 1, 0), send(block, 3, 0)

    both = jnp.concatenate(
        [jnp.pad(whiten, ((0, 0), (0, OWN))), jnp.pad(anchors, ((0, 0), (0, 53)))], axis=0
    )
    shared = [both] + [send(both, 0, other) for other in (1, 2, 3)]

    stacked = jnp.concatenate([image, mask.astype(bf16)[None]], axis=0)
    (tile,) = call(
        rim_kernel, [((4, ROWS, 128), bf16)], [], 1_000_000, 4, stacked, block, loose=1
    )
    half = ((KEPT // 2, FLAT), bf16)
    upper, lower = call(
        halve_kernel, [half, half], [], 1_000_000, 4, last, following, tile, loose=1
    )
    first_blocks = (block, following, last)
    last_blocks = (send(upper, 1, 0), send(lower, 3, 0))

    plane = ((ROWS, LANES), f32)
    patches, tissue, scale, norm, inv_square, inv_density, anch, anch_t, wturned = call(
        patch_kernel,
        [
            ((36 * GROUP, LANES), bf16),
            plane,
            plane,
            plane,
            plane,
            ((8, 128), f32),
            ((KEPT, 80), bf16),
            ((80, KEPT), bf16),
            ((KEPT, 1024), bf16),
        ],
        [((ROWS, 768), f32)],
        1_000_000_000,
        12,
        stacked, lax.ppermute(tile, STRIPS + CHAN, seams()), *shared,
    )
    masked, whitened = call(
        forward_kernel,
        [((ROWS, KEPT, LANES), bf16), ((KEPT, FLAT), bf16)],
        [((ROWS, KEPT, 128), f32), ((LANES, 128), bf16)],
        3_000_000_000,
        18,
        patches, tissue, scale, norm, inv_density, anch,
    )
    rows = ((512, 128), bf16)
    partial, *early = call(
        early_kernel,
        [((KEPT, FLAT), f32)] + [rows] * 4,
        [],
        2_000_000_000,
        14,
        *first_blocks, wturned, whitened,
    )
    anchor_grad, image_part = call(
        backward_kernel,
        [((80, KEPT), f32), ((128, LANES), bf16)],
        [((ROWS * KEPT, 128), bf16), ((36 * GROUP, LANES), f32), ((128, LANES), bf16)],
        5_000_000_000,
        24,
        *last_blocks, partial, wturned, inv_density, masked, patches, inv_square, anch_t,
    )

    parts = lax.all_to_all(image_part.reshape(16, 8, LANES), CHAN, 0, 0)
    rows = ((560, 128), bf16)
    own, *away = call(
        finish_kernel,
        [rows] * 4,
        [],
        1_000_000_000,
        12,
        *last_blocks, whitened, *early, anchor_grad,
    )
    middle, kept, *others = call(
        chip_kernel,
        [((8, 512), f32)] + [((176, 128), bf16)] * 4,
        [((560, 128), f32)],
        1_000_000,
        8,
        parts, own, *(send(value, 0, other) for other, value in enumerate(away, 1)),
    )
    others = [
        lax.ppermute(value, "y", [(y, (y + step) % 4) for y in range(4)])
        for step, value in enumerate(others, 1)
    ]
    (packed,) = call(
        pack_kernel, [((4, 80, 128), bf16)], [((128, 128), f32)], 1_000_000, 4, kept, *others
    )
    return tuple(
        call(
            unpack_kernel,
            [((OWN, 75), f32), ((OWN, OWN), f32), ((3, 2, 512), f32)],
            [],
            1_000_000,
            4,
            lax.all_to_all(packed, "z_hi", 0, 0), middle,
        )
    )


def solution(mesh):
    fine = Mesh(mesh.devices.reshape(4, 4, 4, 2, 2), STRIPS + CHAN)
    placed = (
        P(None, None, STRIPS),
        P(None, STRIPS),
        P(CHAN, None),
        P(None, CHAN),
        P(CHAN, None, STRIPS),
    )
    return jax.shard_map(
        shards,
        mesh=fine,
        in_specs=placed,
        out_specs=(P(CHAN, None), P(STRIPS, CHAN), P(None, CHAN, STRIPS)),
        check_vma=False,
    )
```

```python
import math

import jax
import jax.numpy as jnp
from jax import lax
from jax.experimental import pallas as pl
from jax.experimental.pallas import tpu as pltpu
from jax.sharding import Mesh
from jax.sharding import PartitionSpec as P

EPS = 1e-05
LANES = 256
REACH = 135
QUARTER = 64
FLAT = 16 * QUARTER
ROWS = 32
GROUP = 16
OWN = 64
KEPT = 4 * OWN
STEP = 4
EARLY = 12
MIB = 1024 * 1024

STRIPS = ("z_hi", "y")
CHAN = ("x", "z_lo", "core")


def route(dx, other):
    return [(i, (i // 4 + dx) % 4 * 4 + (i % 4 ^ other)) for i in range(16)]


def seams():
    pairs = [(16 * s + 4 * x, 16 * s - 16 + 4 * x + 3) for s in range(1, 16) for x in range(4)]
    return pairs + [(b, a) for a, b in pairs]


f32 = jnp.float32
bf16 = jnp.bfloat16


def tap(distance):
    return math.exp(-distance * distance / 8.0) if abs(distance) <= 4 else 0.0


def taps(distance):
    far = jnp.abs(distance) > 4
    distance = distance.astype(f32)
    return jnp.where(far, 0.0, jnp.exp(distance * distance * (-1.0 / 8.0)))


def places(shape):
    return tuple(lax.broadcasted_iota(jnp.int32, shape, dim) for dim in (0, 1))


def column_pool():
    lane, target = places((LANES, 128))
    return taps(2 * (target & 63) - lane + 4).astype(bf16)


def column_spread():
    target, lane = places((128, LANES))
    return taps(2 * (target & 63) - lane + 4).astype(bf16)


def row_weights(t, i):
    low, high = tap(4 * t - i), tap(4 * t + 2 - i)
    if low == 0.0 and high == 0.0:
        return None
    return jnp.where(lax.broadcasted_iota(jnp.int32, (1, 128), 1) < QUARTER, low, high)


def row_pool(odd):
    t, i = places((8, ROWS))
    return taps(4 * t + 2 * odd - i)


def split_group(row):
    q = row & (GROUP - 1)
    colour = jnp.where(q < 5, 0, jnp.where(q < 10, 1, jnp.where(q < 15, 2, 3)))
    return row >> 4, colour, q - 5 * colour


def ones(hit, dtype=bf16):
    return jnp.where(hit, 1.0, 0.0).astype(dtype)


def replicate_rows():
    out, src = places((36 * GROUP, 3 * ROWS))
    r, colour, _ = split_group(out)
    return ones(((src & 31) == r - 2) & ((src >> 5) == colour))


def fold_rows():
    out, src = places((128, 36 * GROUP))
    r, colour, _ = split_group(src)
    i = 2 * (out >> 3) + (out & 1)
    return ones((r == i + 2) & (colour == ((out & 7) >> 1)) & (colour < 3))


def entry_order(dtype, rows=75):
    entry, out = places((rows, 80))
    a, colour, b = split_group(out)
    return ones((entry == 25 * colour + 5 * a + b) & (colour < 3), dtype)


def quarter():
    return lax.axis_index("z_lo") * 2 + lax.axis_index("core")


def flipped(axis, bit):
    return lax.rem(lax.axis_index(axis) + bit, 2)


def block_of(p):
    dx, other = (0, 1, 3, 2)[p // 4], p % 4
    ex = lax.rem(lax.axis_index("x") + dx, 4)
    return ex * 4 + flipped("z_lo", other // 2) * 2 + flipped("core", other % 2)


def dot(a, b):
    return jnp.dot(a, b, preferred_element_type=f32)


def dot_nt(a, b):
    return lax.dot_general(a, b, (((1,), (1,)), ((), ())), preferred_element_type=f32)


def quarter_kernel(cotangent, own, core, zed, both, parts):
    lane = lax.broadcasted_iota(jnp.int32, (OWN, 128), 1)
    for t in range(8):
        low, high = (cotangent[:, 2 * t + n, :].astype(f32) for n in (0, 1))
        for side in range(2):
            cols = slice(side * 128, side * 128 + 128)
            even = jnp.where(lane < QUARTER, low[:, cols], pltpu.roll(high[:, cols], QUARTER, 1))
            odd = jnp.where(lane < QUARTER, pltpu.roll(low[:, cols], QUARTER, 1), high[:, cols])
            parts[2 * side, :, t * 128 : (t + 1) * 128] = even.astype(bf16)
            parts[2 * side + 1, :, t * 128 : (t + 1) * 128] = odd.astype(bf16)
    for other, part in enumerate((own, core, zed, both)):
        part[...] = parts[flipped("z_lo", other // 2) * 2 + flipped("core", other % 2)]


def join_kernel(*refs):
    *parts, _, _, joined = refs
    start = 0
    for ref in parts:
        joined[start : start + ref.shape[0]] = ref[...]
        start += ref.shape[0]


def bundle_kernel(whiten, anchors, after, bundle):
    del after
    bundle[0:512, :OWN] = whiten[0:512, :]
    bundle[0:512, OWN:] = whiten[512:1024, :]
    bundle[512:576, :] = jnp.zeros((OWN, 128), bf16)
    bundle[512:576, :75] = anchors[...]


def halve_kernel(first, second, after, upper, lower):
    del after
    upper[...] = first[: KEPT // 2]
    lower[...] = second[KEPT // 2 :]


def rim_kernel(stacked, *refs):
    tile = refs[-1]
    first = quarter() == 0
    for c in range(4):
        value = stacked[c].astype(f32)
        tile[c] = jnp.where(first, value[:, :128], value[:, 384:]).astype(bf16)


def patch_kernel(
    stacked, beyond, *refs,
):
    shared = refs[:4]
    patches, tissue, scale, norm, inv_square, inv_density, anch, anch_t, wturned, wide = refs[4:]
    start = pl.multiple_of(quarter() * 128, 128)

    def part(c, shift):
        rim = beyond[c].astype(f32)
        wide[:, 0:128] = rim
        wide[:, 128:640] = stacked[c].astype(f32)
        wide[:, 640:768] = rim
        return pltpu.roll(wide[:, pl.ds(start, 384)], 384 - shift, 1)[:, :LANES]

    colours = [part(c, 122) for c in range(3)]
    here = part(3, 124)
    lane = lax.broadcasted_iota(jnp.int32, here.shape, 1)
    here = jnp.where(lane < REACH, here, 0.0)
    tissue[...] = here
    x = dot(replicate_rows(), jnp.concatenate(colours, axis=0).astype(bf16))
    offset = (lax.broadcasted_iota(jnp.int32, x.shape, 0) % GROUP) % 5
    s = x
    for b in range(1, 5):
        s = jnp.where(offset == b, pltpu.roll(x, LANES - b, 1), s)
    patches[...] = s.astype(bf16)
    square = jnp.sum((s * s).reshape(36, GROUP, LANES), axis=1)
    total = square[0:ROWS]
    for a in range(1, 5):
        total = total + square[a : a + ROWS]
    total = total + EPS
    root = lax.rsqrt(total)
    scale[...] = 4.0 * root
    norm[...] = total * root
    inv_square[...] = 1.0 / total
    counted = dot(here.astype(bf16), column_pool())
    even, odd = (
        jnp.dot(row_pool(n), counted, precision=lax.Precision.HIGHEST, preferred_element_type=f32)
        for n in (0, 1)
    )
    lane = lax.broadcasted_iota(jnp.int32, even.shape, 1)
    inv_density[...] = 1.0 / jnp.maximum(jnp.where(lane < QUARTER, even, odd), 1.0)
    anchors = jnp.concatenate([bundle[512:576, :] for bundle in shared], axis=0)
    ordered = dot(anchors, entry_order(bf16, 128))
    anch[...] = ordered.astype(bf16)
    anch_t[...] = ordered.T.astype(bf16)
    blocks = [block_of(p) for p in range(16)]
    for n, bundle in enumerate(shared):
        ordered = []
        for block in blocks:
            rows = pl.ds(pl.multiple_of(lax.rem(block, 8) * OWN, OWN), OWN)
            value = bundle[rows, :].astype(f32)
            ordered.append(jnp.where(block >= 8, pltpu.roll(value, OWN, 1), value))
        turned = jnp.concatenate(ordered, axis=0).T
        wturned[n * OWN : (n + 1) * OWN, :] = turned[:OWN].astype(bf16)


def forward_kernel(
    patches, tissue, scale, norm, inv_density, anch, after,
    masked, whitened,
    columned, pool,
):
    del after
    pool[...] = column_pool()

    @pl.loop(0, ROWS // STEP)
    def _(t):
        lifted = []
        for r in range(STEP):
            i = t * STEP + r
            patch = patches[pl.ds(pl.multiple_of(i * GROUP, GROUP), 80), :]
            raw = dot(anch[...], patch)
            value = jnp.exp(raw * scale[pl.ds(i, 1), :] - 4.0) * tissue[pl.ds(i, 1), :]
            masked[i] = value.astype(bf16)
            lifted.append((value * norm[pl.ds(i, 1), :]).astype(bf16))
        result = dot(jnp.concatenate(lifted, axis=0), pool[...])
        columned[pl.ds(t * STEP, STEP)] = result.reshape(STEP, KEPT, 128)

    for t in range(8):
        acc = None
        for i in range(ROWS):
            weights = row_weights(t, i)
            if weights is not None:
                term = weights * columned[i]
                acc = term if acc is None else acc + term
        whitened[:, t * 128 : (t + 1) * 128] = (acc * inv_density[t : t + 1, :]).astype(bf16)


def fold(block, rows):
    top, low = block[:rows], block[rows:]
    left = lax.broadcasted_iota(jnp.int32, top.shape, 1) < OWN
    own = jnp.where(left, top, pltpu.roll(low, OWN, 1))
    partner = jnp.where(left, pltpu.roll(top, OWN, 1), low)
    return own.astype(bf16), partner.astype(bf16)


def stacks(blocks):
    for n in range(FLAT // 256):
        cols = slice(n * 256, (n + 1) * 256)
        yield cols, jnp.concatenate([block[:, cols] for block in blocks], axis=0)


def whiten_rows(blocks, whitened):
    return sum(dot_nt(stack, whitened[:, cols]) for cols, stack in stacks(blocks))


def four_folds(block, rows):
    return fold(block[:, :128], rows) + fold(block[:, 128:], rows)


def place_rows(sums, grad_w, first):
    for n in range(grad_w.shape[0] // OWN):
        strip = block_of(first + n)
        place = lax.rem(strip, 4) * 4 + strip // 4
        rows = pl.ds(pl.multiple_of(place * 32, 32), 32)
        for ref, value in zip(sums, four_folds(grad_w[n * OWN : (n + 1) * OWN], OWN // 2)):
            ref[rows, :] = value


def early_kernel(*refs):
    blocks, (wturned, whitened, partial, *sums) = refs[:3], refs[3:]
    for ref in sums:
        ref[...] = jnp.zeros_like(ref)
    for cols, stack in stacks(blocks):
        partial[:, cols] = dot(wturned[:, : EARLY * OWN], stack)
    place_rows(sums, whiten_rows(blocks, whitened), 0)


def backward_kernel(
    first, second, partial, wturned, inv_density, masked, patches, inv_square, anch_t,
    anchor_grad, image,
    rowed, spread_grad, pool_t,
):
    pool_t[...] = column_spread()
    scaled = []
    for cols, stack in stacks((first, second)):
        pooled = partial[:, cols] + dot(wturned[:, EARLY * OWN :], stack)
        for side in range(2):
            t = len(scaled)
            part = pooled[:, side * 128 : (side + 1) * 128]
            scaled.append(part.astype(bf16).astype(f32) * (4.0 * inv_density[t : t + 1, :]))
    for i in range(ROWS):
        acc = None
        for t in range(8):
            weights = row_weights(t, i)
            if weights is not None:
                term = weights * scaled[t]
                acc = term if acc is None else acc + term
        rowed[i * KEPT : (i + 1) * KEPT, :] = acc.astype(bf16)
    spread_grad[...] = jnp.zeros_like(spread_grad)
    anchor_grad[...] = jnp.zeros_like(anchor_grad)

    @pl.loop(0, ROWS // STEP)
    def _(t):
        start = pl.multiple_of(t * (STEP * KEPT), STEP * KEPT)
        spread = dot(rowed[pl.ds(start, STEP * KEPT), :], pool_t[...])
        grads, wides, units = [], [], []
        for r in range(STEP):
            i = t * STEP + r
            patch = patches[pl.ds(pl.multiple_of(i * GROUP, GROUP), 80), :]
            grad = (spread[r * KEPT : (r + 1) * KEPT] * masked[i].astype(f32)).astype(bf16)
            unit = dot(anch_t[...], grad)
            wide = patch.astype(f32)
            along = jnp.sum(wide * unit, axis=0, keepdims=True) * inv_square[pl.ds(i, 1), :]
            units.append(unit - wide * along)
            grads.append(grad)
            wides.append(patch)
        anchor_grad[...] += dot_nt(jnp.concatenate(wides, axis=1), jnp.concatenate(grads, axis=1))
        sums = []
        for g in range(STEP + 4):
            acc = None
            for r in range(STEP):
                if 0 <= g - r < 5:
                    term = units[r][(g - r) * GROUP : (g - r + 1) * GROUP]
                    acc = term if acc is None else acc + term
            sums.append(acc)
        here = pl.ds(pl.multiple_of(t * (STEP * GROUP), STEP * GROUP), (STEP + 4) * GROUP)
        spread_grad[here, :] += jnp.concatenate(sums, axis=0)

    t = spread_grad[...]
    offset = (lax.broadcasted_iota(jnp.int32, t.shape, 0) % GROUP) % 5
    moved = t
    for b in range(1, 5):
        moved = jnp.where(offset == b, pltpu.roll(t, b, 1), moved)
    high = moved.astype(bf16)
    low = (moved - high.astype(f32)).astype(bf16)
    folder = fold_rows()
    image[...] = (dot(folder, high) + dot(folder, low)).astype(bf16)


def finish_kernel(*refs):
    first, second, whitened, *early = refs[:7]
    anchor_grad, *sums = refs[7:]
    pad = jnp.zeros((8, 128), bf16)
    for ref, start, part in zip(sums, early, four_folds(anchor_grad[...], 40)):
        ref[0:512, :] = start[...]
        ref[512:560, :] = jnp.concatenate([part, pad], axis=0)
    place_rows(sums, whiten_rows((first, second), whitened), EARLY)


def add_up(refs):
    total = refs[0][...].astype(f32)
    for ref in refs[1:]:
        total = total + ref[...].astype(f32)
    return total


def rim_lanes(rims):
    lane = lax.broadcasted_iota(jnp.int32, rims.shape, 1)
    return jnp.where(lane < 6, rims, 0.0), jnp.where(lane >= 122, rims, 0.0)


def chip_kernel(parts, own, one, two, three, middle, kept, next_one, next_two, next_three, sums):
    gap = jnp.zeros((8, 128), f32)
    whole = None
    for q in range(4):
        part = add_up([parts.at[4 * x + q] for x in range(4)])
        pieces = [gap] * q + [part] + [gap] * (3 - q)
        placed = jnp.concatenate(pieces, axis=1)
        whole = placed if whole is None else whole + placed
    turned = pltpu.roll(whole, 640 - 6, 1)
    middle[...] = turned[:, :512]
    later, earlier = rim_lanes(turned[:, 512:])
    y, z = lax.axis_index("y"), lax.axis_index("z_hi")
    later = jnp.where((y == 3) & (z == 3), 0.0, later)
    earlier = jnp.where((y == 0) & (z == 0), 0.0, earlier)
    later = jnp.where(y == 3, pltpu.roll(later, 64, 1), later)
    earlier = jnp.where(y == 0, pltpu.roll(earlier, 64, 1), earlier)
    sums[...] = add_up((own, one, two, three))
    for step, part in enumerate((kept, next_one, next_two, next_three)):
        target = lax.rem(y + step, 4)
        part[0:128, :] = sums[pl.ds(pl.multiple_of(target * 128, 128), 128), :].astype(bf16)
        rims = {1: later, 3: earlier}.get(step, gap)
        part[128:176, :] = jnp.concatenate([sums[512:552, :], rims], axis=0).astype(bf16)


def pack_kernel(kept, one, two, three, packed, sums):
    total = add_up((kept, one, two, three))
    sums[...] = total[0:128]
    straight = rim_lanes(total[168:176])
    onward = rim_lanes(pltpu.roll(total[168:176], 64, 1))
    rims = (straight[0] + straight[1], onward[0], jnp.zeros((8, 128), f32), onward[1])
    for step in range(4):
        z = lax.rem(lax.axis_index("z_hi") + step, 4)
        packed[z, 0:32, :] = sums[pl.ds(pl.multiple_of(z * 32, 32), 32), :].astype(bf16)
        packed[z, 32:80, :] = jnp.concatenate([total[128:168], rims[step]], axis=0).astype(bf16)


def unpack_kernel(received, middle, grad_anchors, grad_whiten, grad_image):
    total = add_up([received.at[z] for z in range(4)])
    other = pltpu.roll(total, OWN, 1)
    grad_whiten[0:32, :] = total[0:32, :OWN]
    grad_whiten[32:64, :] = other[0:32, :OWN]
    turned = jnp.concatenate([total[32:72], other[32:72]], axis=0).T[:OWN]
    grad_anchors[...] = lax.dot_general(
        turned, entry_order(f32), (((1,), (1,)), ((), ())),
        precision=lax.Precision.HIGHEST, preferred_element_type=f32,
    )
    first, last = rim_lanes(total[72:80])
    image = middle[...] + jnp.concatenate([first, jnp.zeros((8, 256), f32), last], axis=1)
    for colour in range(3):
        grad_image[colour] = image[2 * colour : 2 * colour + 2]


def hold(value, *after):
    def kernel(*refs):
        del refs

    return pl.pallas_call(
        kernel,
        out_shape=jax.ShapeDtypeStruct(value.shape, value.dtype),
        in_specs=[pl.BlockSpec(memory_space=pl.ANY)] * (1 + len(after)),
        out_specs=pl.BlockSpec(memory_space=pl.ANY),
        input_output_aliases={0: 0},
        compiler_params=pltpu.CompilerParams(vmem_limit_bytes=MIB),
        cost_estimate=pl.CostEstimate(flops=1000, bytes_accessed=1000, transcendentals=0),
    )(value, *after)


def call(kernel, outs, scratch, flops, limit, *args, loose=0):
    size = lambda shape, dtype: math.prod(shape) * jnp.dtype(dtype).itemsize
    tight = len(args) - loose
    moved = sum(size(a.shape, a.dtype) for a in args[:tight]) + sum(size(*out) for out in outs)
    return pl.pallas_call(
        kernel,
        out_shape=[jax.ShapeDtypeStruct(shape, dtype) for shape, dtype in outs],
        in_specs=[pl.BlockSpec(memory_space=pltpu.VMEM)] * tight
        + [pl.BlockSpec(memory_space=pl.ANY)] * loose,
        out_specs=[pl.BlockSpec(memory_space=pltpu.VMEM)] * len(outs),
        scratch_shapes=[pltpu.VMEM(shape, dtype) for shape, dtype in scratch],
        compiler_params=pltpu.CompilerParams(vmem_limit_bytes=limit * MIB),
        cost_estimate=pl.CostEstimate(flops=flops, bytes_accessed=moved, transcendentals=0),
    )(*args)


def shards(image, mask, anchors, whiten, cotangent):
    def send(value, dx, other):
        return lax.ppermute(value, CHAN, route(dx, other))

    part = ((OWN, FLAT), bf16)
    own, *away = call(
        quarter_kernel, [part] * 4, [((4, OWN, FLAT), bf16)], 1_000_000, 6, cotangent
    )
    (bundle,) = call(
        bundle_kernel, [((576, 128), bf16)], [], 1_000_000, 4, whiten, anchors, away[2], loose=1
    )

    stacked = jnp.concatenate([image, mask.astype(bf16)[None]], axis=0)
    (tile,) = call(
        rim_kernel, [((4, ROWS, 128), bf16)], [], 1_000_000, 4, stacked, away[2], loose=1
    )
    (block,) = call(
        join_kernel,
        [((KEPT, FLAT), bf16)],
        [],
        1_000_000,
        4,
        own, *(send(value, 0, other) for other, value in enumerate(away, 1)), tile, bundle,
        loose=2,
    )
    last, following = send(block, 1, 0), send(block, 3, 0)
    bundle = hold(bundle, block)
    shared = [bundle] + [send(bundle, 0, other) for other in (1, 2, 3)]
    half = ((KEPT // 2, FLAT), bf16)
    upper, lower = call(
        halve_kernel, [half, half], [], 1_000_000, 4, last, following, tile, loose=1
    )
    first_blocks = (block, following, last)
    last_blocks = (send(upper, 1, 0), send(lower, 3, 0))

    plane = ((ROWS, LANES), f32)
    patches, tissue, scale, norm, inv_square, inv_density, anch, anch_t, wturned = call(
        patch_kernel,
        [
            ((36 * GROUP, LANES), bf16),
            plane,
            plane,
            plane,
            plane,
            ((8, 128), f32),
            ((KEPT, 80), bf16),
            ((80, KEPT), bf16),
            ((KEPT, 1024), bf16),
        ],
        [((ROWS, 768), f32)],
        1_000_000_000,
        12,
        stacked, lax.ppermute(tile, STRIPS + CHAN, seams()), *shared,
    )
    masked, whitened = call(
        forward_kernel,
        [((ROWS, KEPT, LANES), bf16), ((KEPT, FLAT), bf16)],
        [((ROWS, KEPT, 128), f32), ((LANES, 128), bf16)],
        3_000_000_000,
        18,
        patches, tissue, scale, norm, inv_density, anch, upper,
        loose=1,
    )
    rows = ((512, 128), bf16)
    partial, *early = call(
        early_kernel,
        [((KEPT, FLAT), f32)] + [rows] * 4,
        [],
        2_000_000_000,
        14,
        *first_blocks, wturned, whitened,
    )
    anchor_grad, image_part = call(
        backward_kernel,
        [((80, KEPT), f32), ((128, LANES), bf16)],
        [((ROWS * KEPT, 128), bf16), ((36 * GROUP, LANES), f32), ((128, LANES), bf16)],
        5_000_000_000,
        24,
        *last_blocks, partial, wturned, inv_density, masked, patches, inv_square, anch_t,
    )

    parts = lax.all_to_all(image_part.reshape(16, 8, LANES), CHAN, 0, 0)
    rows = ((560, 128), bf16)
    own, *away = call(
        finish_kernel,
        [rows] * 4,
        [],
        1_000_000_000,
        12,
        *last_blocks, whitened, *early, anchor_grad,
    )
    middle, kept, *others = call(
        chip_kernel,
        [((8, 512), f32)] + [((176, 128), bf16)] * 4,
        [((560, 128), f32)],
        1_000_000,
        8,
        parts, own, *(send(value, 0, other) for other, value in enumerate(away, 1)),
    )
    others = [
        lax.ppermute(value, "y", [(y, (y + step) % 4) for y in range(4)])
        for step, value in enumerate(others, 1)
    ]
    (packed,) = call(
        pack_kernel, [((4, 80, 128), bf16)], [((128, 128), f32)], 1_000_000, 4, kept, *others
    )
    return tuple(
        call(
            unpack_kernel,
            [((OWN, 75), f32), ((OWN, OWN), f32), ((3, 2, 512), f32)],
            [],
            1_000_000,
            4,
            lax.all_to_all(packed, "z_hi", 0, 0), middle,
        )
    )


def solution(mesh):
    fine = Mesh(mesh.devices.reshape(4, 4, 4, 2, 2), STRIPS + CHAN)
    placed = (
        P(None, None, STRIPS),
        P(None, STRIPS),
        P(CHAN, None),
        P(None, CHAN),
        P(CHAN, None, STRIPS),
    )
    return jax.shard_map(
        shards,
        mesh=fine,
        in_specs=placed,
        out_specs=(P(CHAN, None), P(STRIPS, CHAN), P(None, CHAN, STRIPS)),
        check_vma=False,
    )
```

```python
import math

import jax
import jax.numpy as jnp
from jax import lax
from jax.experimental import pallas as pl
from jax.experimental.pallas import tpu as pltpu
from jax.sharding import Mesh
from jax.sharding import PartitionSpec as P

EPS = 1e-05
LANES = 256
REACH = 135
QUARTER = 64
FLAT = 16 * QUARTER
ROWS = 32
GROUP = 16
OWN = 64
KEPT = 4 * OWN
STEP = 4
EARLY = 12
MIB = 1024 * 1024

STRIPS = ("z_hi", "y")
CHAN = ("x", "z_lo", "core")


def route(dx, other):
    return [(i, (i // 4 + dx) % 4 * 4 + (i % 4 ^ other)) for i in range(16)]


def seams():
    pairs = [(16 * s + 4 * x, 16 * s - 16 + 4 * x + 3) for s in range(1, 16) for x in range(4)]
    return pairs + [(b, a) for a, b in pairs]


f32 = jnp.float32
bf16 = jnp.bfloat16


def tap(distance):
    return math.exp(-distance * distance / 8.0) if abs(distance) <= 4 else 0.0


def taps(distance):
    far = jnp.abs(distance) > 4
    distance = distance.astype(f32)
    return jnp.where(far, 0.0, jnp.exp(distance * distance * (-1.0 / 8.0)))


def places(shape):
    return tuple(lax.broadcasted_iota(jnp.int32, shape, dim) for dim in (0, 1))


def column_pool():
    lane, target = places((LANES, 128))
    return taps(2 * (target & 63) - lane + 4).astype(bf16)


def column_spread():
    target, lane = places((128, LANES))
    return taps(2 * (target & 63) - lane + 4).astype(bf16)


def row_weights(t, i):
    low, high = tap(4 * t - i), tap(4 * t + 2 - i)
    if low == 0.0 and high == 0.0:
        return None
    return jnp.where(lax.broadcasted_iota(jnp.int32, (1, 128), 1) < QUARTER, low, high)


def row_pool(odd):
    t, i = places((8, ROWS))
    return taps(4 * t + 2 * odd - i)


def split_group(row):
    q = row & (GROUP - 1)
    colour = jnp.where(q < 5, 0, jnp.where(q < 10, 1, jnp.where(q < 15, 2, 3)))
    return row >> 4, colour, q - 5 * colour


def ones(hit, dtype=bf16):
    return jnp.where(hit, 1.0, 0.0).astype(dtype)


def replicate_rows():
    out, src = places((36 * GROUP, 3 * ROWS))
    r, colour, _ = split_group(out)
    return ones(((src & 31) == r - 2) & ((src >> 5) == colour))


def fold_rows():
    out, src = places((128, 36 * GROUP))
    r, colour, _ = split_group(src)
    i = 2 * (out >> 3) + (out & 1)
    return ones((r == i + 2) & (colour == ((out & 7) >> 1)) & (colour < 3))


def entry_order(dtype, rows=75):
    entry, out = places((rows, 80))
    a, colour, b = split_group(out)
    return ones((entry == 25 * colour + 5 * a + b) & (colour < 3), dtype)


def quarter():
    return lax.axis_index("z_lo") * 2 + lax.axis_index("core")


def flipped(axis, bit):
    return lax.rem(lax.axis_index(axis) + bit, 2)


def block_of(p):
    dx, other = (0, 1, 3, 2)[p // 4], p % 4
    ex = lax.rem(lax.axis_index("x") + dx, 4)
    return ex * 4 + flipped("z_lo", other // 2) * 2 + flipped("core", other % 2)


def dot(a, b):
    return jnp.dot(a, b, preferred_element_type=f32)


def dot_nt(a, b):
    return lax.dot_general(a, b, (((1,), (1,)), ((), ())), preferred_element_type=f32)


def quarter_kernel(cotangent, anchors, own, core, zed, both, parts):
    lane = lax.broadcasted_iota(jnp.int32, (OWN, 128), 1)
    for t in range(8):
        low, high = (cotangent[:, 2 * t + n, :].astype(f32) for n in (0, 1))
        for side in range(2):
            cols = slice(side * 128, side * 128 + 128)
            even = jnp.where(lane < QUARTER, low[:, cols], pltpu.roll(high[:, cols], QUARTER, 1))
            odd = jnp.where(lane < QUARTER, pltpu.roll(low[:, cols], QUARTER, 1), high[:, cols])
            parts[2 * side, :, t * 128 : (t + 1) * 128] = even.astype(bf16)
            parts[2 * side + 1, :, t * 128 : (t + 1) * 128] = odd.astype(bf16)
    for other, part in enumerate((own, core, zed, both)):
        part[:, :FLAT] = parts[flipped("z_lo", other // 2) * 2 + flipped("core", other % 2)]
        part[:, FLAT:] = jnp.zeros((OWN, 128), bf16)
        part[:, FLAT : FLAT + 75] = anchors[...]


def join_kernel(*refs):
    *parts, _, _, joined = refs
    start = 0
    for ref in parts:
        joined[start : start + ref.shape[0]] = ref[:, :FLAT]
        start += ref.shape[0]


def bundle_kernel(whiten, after, bundle):
    del after
    bundle[:, :OWN] = whiten[0:512, :]
    bundle[:, OWN:] = whiten[512:1024, :]


def halve_kernel(first, second, after, upper, lower):
    del after
    upper[...] = first[: KEPT // 2]
    lower[...] = second[KEPT // 2 :]


def rim_kernel(stacked, *refs):
    tile = refs[-1]
    first = quarter() == 0
    for c in range(4):
        value = stacked[c].astype(f32)
        tile[c] = jnp.where(first, value[:, :128], value[:, 384:]).astype(bf16)


def patch_kernel(
    stacked, beyond, *refs,
):
    quarters = refs[:4]
    patches, tissue, scale, norm, inv_square, inv_density, anch, anch_t, wide = refs[4:]
    start = pl.multiple_of(quarter() * 128, 128)

    def part(c, shift):
        rim = beyond[c].astype(f32)
        wide[:, 0:128] = rim
        wide[:, 128:640] = stacked[c].astype(f32)
        wide[:, 640:768] = rim
        return pltpu.roll(wide[:, pl.ds(start, 384)], 384 - shift, 1)[:, :LANES]

    colours = [part(c, 122) for c in range(3)]
    here = part(3, 124)
    lane = lax.broadcasted_iota(jnp.int32, here.shape, 1)
    here = jnp.where(lane < REACH, here, 0.0)
    tissue[...] = here
    x = dot(replicate_rows(), jnp.concatenate(colours, axis=0).astype(bf16))
    offset = (lax.broadcasted_iota(jnp.int32, x.shape, 0) % GROUP) % 5
    s = x
    for b in range(1, 5):
        s = jnp.where(offset == b, pltpu.roll(x, LANES - b, 1), s)
    patches[...] = s.astype(bf16)
    square = jnp.sum((s * s).reshape(36, GROUP, LANES), axis=1)
    total = square[0:ROWS]
    for a in range(1, 5):
        total = total + square[a : a + ROWS]
    total = total + EPS
    root = lax.rsqrt(total)
    scale[...] = 4.0 * root
    norm[...] = total * root
    inv_square[...] = 1.0 / total
    counted = dot(here.astype(bf16), column_pool())
    even, odd = (
        jnp.dot(row_pool(n), counted, precision=lax.Precision.HIGHEST, preferred_element_type=f32)
        for n in (0, 1)
    )
    lane = lax.broadcasted_iota(jnp.int32, even.shape, 1)
    inv_density[...] = 1.0 / jnp.maximum(jnp.where(lane < QUARTER, even, odd), 1.0)
    anchors = jnp.concatenate([part[:, FLAT:] for part in quarters], axis=0)
    ordered = dot(anchors, entry_order(bf16, 128))
    anch[...] = ordered.astype(bf16)
    anch_t[...] = ordered.T.astype(bf16)

def turn_kernel(*refs):
    *shared, wturned = refs
    blocks = [block_of(p) for p in range(16)]
    for n, bundle in enumerate(shared):
        ordered = []
        for block in blocks:
            rows = pl.ds(pl.multiple_of(lax.rem(block, 8) * OWN, OWN), OWN)
            value = bundle[rows, :].astype(f32)
            ordered.append(jnp.where(block >= 8, pltpu.roll(value, OWN, 1), value))
        turned = jnp.concatenate(ordered, axis=0).T
        wturned[n * OWN : (n + 1) * OWN, :] = turned[:OWN].astype(bf16)


def forward_kernel(
    patches, tissue, scale, norm, inv_density, anch,
    masked, whitened,
    columned, pool,
):
    pool[...] = column_pool()

    @pl.loop(0, ROWS // STEP)
    def _(t):
        lifted = []
        for r in range(STEP):
            i = t * STEP + r
            patch = patches[pl.ds(pl.multiple_of(i * GROUP, GROUP), 80), :]
            raw = dot(anch[...], patch)
            value = jnp.exp(raw * scale[pl.ds(i, 1), :] - 4.0) * tissue[pl.ds(i, 1), :]
            masked[i] = value.astype(bf16)
            lifted.append((value * norm[pl.ds(i, 1), :]).astype(bf16))
        result = dot(jnp.concatenate(lifted, axis=0), pool[...])
        columned[pl.ds(t * STEP, STEP)] = result.reshape(STEP, KEPT, 128)

    for t in range(8):
        acc = None
        for i in range(ROWS):
            weights = row_weights(t, i)
            if weights is not None:
                term = weights * columned[i]
                acc = term if acc is None else acc + term
        whitened[:, t * 128 : (t + 1) * 128] = (acc * inv_density[t : t + 1, :]).astype(bf16)


def fold(block, rows):
    top, low = block[:rows], block[rows:]
    left = lax.broadcasted_iota(jnp.int32, top.shape, 1) < OWN
    own = jnp.where(left, top, pltpu.roll(low, OWN, 1))
    partner = jnp.where(left, pltpu.roll(top, OWN, 1), low)
    return own.astype(bf16), partner.astype(bf16)


def stacks(blocks):
    for n in range(FLAT // 256):
        cols = slice(n * 256, (n + 1) * 256)
        yield cols, jnp.concatenate([block[:, cols] for block in blocks], axis=0)


def whiten_rows(blocks, whitened):
    return sum(dot_nt(stack, whitened[:, cols]) for cols, stack in stacks(blocks))


def four_folds(block, rows):
    return fold(block[:, :128], rows) + fold(block[:, 128:], rows)


def place_rows(sums, grad_w, first):
    for n in range(grad_w.shape[0] // OWN):
        strip = block_of(first + n)
        place = lax.rem(strip, 4) * 4 + strip // 4
        rows = pl.ds(pl.multiple_of(place * 32, 32), 32)
        for ref, value in zip(sums, four_folds(grad_w[n * OWN : (n + 1) * OWN], OWN // 2)):
            ref[rows, :] = value


def early_kernel(*refs):
    blocks, (wturned, whitened, partial, *sums) = refs[:3], refs[3:]
    for ref in sums:
        ref[...] = jnp.zeros_like(ref)
    for cols, stack in stacks(blocks):
        partial[:, cols] = dot(wturned[:, : EARLY * OWN], stack)
    place_rows(sums, whiten_rows(blocks, whitened), 0)


def backward_kernel(
    first, second, partial, wturned, inv_density, masked, patches, inv_square, anch_t,
    anchor_grad, image,
    rowed, spread_grad, pool_t,
):
    pool_t[...] = column_spread()
    scaled = []
    for cols, stack in stacks((first, second)):
        pooled = partial[:, cols] + dot(wturned[:, EARLY * OWN :], stack)
        for side in range(2):
            t = len(scaled)
            part = pooled[:, side * 128 : (side + 1) * 128]
            scaled.append(part.astype(bf16).astype(f32) * (4.0 * inv_density[t : t + 1, :]))
    for i in range(ROWS):
        acc = None
        for t in range(8):
            weights = row_weights(t, i)
            if weights is not None:
                term = weights * scaled[t]
                acc = term if acc is None else acc + term
        rowed[i * KEPT : (i + 1) * KEPT, :] = acc.astype(bf16)
    spread_grad[...] = jnp.zeros_like(spread_grad)
    anchor_grad[...] = jnp.zeros_like(anchor_grad)

    @pl.loop(0, ROWS // STEP)
    def _(t):
        start = pl.multiple_of(t * (STEP * KEPT), STEP * KEPT)
        spread = dot(rowed[pl.ds(start, STEP * KEPT), :], pool_t[...])
        grads, wides, units = [], [], []
        for r in range(STEP):
            i = t * STEP + r
            patch = patches[pl.ds(pl.multiple_of(i * GROUP, GROUP), 80), :]
            grad = (spread[r * KEPT : (r + 1) * KEPT] * masked[i].astype(f32)).astype(bf16)
            unit = dot(anch_t[...], grad)
            wide = patch.astype(f32)
            along = jnp.sum(wide * unit, axis=0, keepdims=True) * inv_square[pl.ds(i, 1), :]
            units.append(unit - wide * along)
            grads.append(grad)
            wides.append(patch)
        anchor_grad[...] += dot_nt(jnp.concatenate(wides, axis=1), jnp.concatenate(grads, axis=1))
        sums = []
        for g in range(STEP + 4):
            acc = None
            for r in range(STEP):
                if 0 <= g - r < 5:
                    term = units[r][(g - r) * GROUP : (g - r + 1) * GROUP]
                    acc = term if acc is None else acc + term
            sums.append(acc)
        here = pl.ds(pl.multiple_of(t * (STEP * GROUP), STEP * GROUP), (STEP + 4) * GROUP)
        spread_grad[here, :] += jnp.concatenate(sums, axis=0)

    t = spread_grad[...]
    offset = (lax.broadcasted_iota(jnp.int32, t.shape, 0) % GROUP) % 5
    moved = t
    for b in range(1, 5):
        moved = jnp.where(offset == b, pltpu.roll(t, b, 1), moved)
    high = moved.astype(bf16)
    low = (moved - high.astype(f32)).astype(bf16)
    folder = fold_rows()
    image[...] = (dot(folder, high) + dot(folder, low)).astype(bf16)


def finish_kernel(*refs):
    first, second, whitened, *early = refs[:7]
    anchor_grad, *sums = refs[7:]
    pad = jnp.zeros((8, 128), bf16)
    for ref, start, part in zip(sums, early, four_folds(anchor_grad[...], 40)):
        ref[0:512, :] = start[...]
        ref[512:560, :] = jnp.concatenate([part, pad], axis=0)
    place_rows(sums, whiten_rows((first, second), whitened), EARLY)


def add_up(refs):
    total = refs[0][...].astype(f32)
    for ref in refs[1:]:
        total = total + ref[...].astype(f32)
    return total


def rim_lanes(rims):
    lane = lax.broadcasted_iota(jnp.int32, rims.shape, 1)
    return jnp.where(lane < 6, rims, 0.0), jnp.where(lane >= 122, rims, 0.0)


def chip_kernel(parts, own, one, two, three, middle, kept, next_one, next_two, next_three, sums):
    gap = jnp.zeros((8, 128), f32)
    whole = None
    for q in range(4):
        part = add_up([parts.at[4 * x + q] for x in range(4)])
        pieces = [gap] * q + [part] + [gap] * (3 - q)
        placed = jnp.concatenate(pieces, axis=1)
        whole = placed if whole is None else whole + placed
    turned = pltpu.roll(whole, 640 - 6, 1)
    middle[...] = turned[:, :512]
    later, earlier = rim_lanes(turned[:, 512:])
    y, z = lax.axis_index("y"), lax.axis_index("z_hi")
    later = jnp.where((y == 3) & (z == 3), 0.0, later)
    earlier = jnp.where((y == 0) & (z == 0), 0.0, earlier)
    later = jnp.where(y == 3, pltpu.roll(later, 64, 1), later)
    earlier = jnp.where(y == 0, pltpu.roll(earlier, 64, 1), earlier)
    sums[...] = add_up((own, one, two, three))
    for step, part in enumerate((kept, next_one, next_two, next_three)):
        target = lax.rem(y + step, 4)
        part[0:128, :] = sums[pl.ds(pl.multiple_of(target * 128, 128), 128), :].astype(bf16)
        rims = {1: later, 3: earlier}.get(step, gap)
        part[128:176, :] = jnp.concatenate([sums[512:552, :], rims], axis=0).astype(bf16)


def pack_kernel(kept, one, two, three, packed, sums):
    total = add_up((kept, one, two, three))
    sums[...] = total[0:128]
    straight = rim_lanes(total[168:176])
    onward = rim_lanes(pltpu.roll(total[168:176], 64, 1))
    rims = (straight[0] + straight[1], onward[0], jnp.zeros((8, 128), f32), onward[1])
    for step in range(4):
        z = lax.rem(lax.axis_index("z_hi") + step, 4)
        packed[z, 0:32, :] = sums[pl.ds(pl.multiple_of(z * 32, 32), 32), :].astype(bf16)
        packed[z, 32:80, :] = jnp.concatenate([total[128:168], rims[step]], axis=0).astype(bf16)


def unpack_kernel(received, middle, grad_anchors, grad_whiten, grad_image):
    total = add_up([received.at[z] for z in range(4)])
    other = pltpu.roll(total, OWN, 1)
    grad_whiten[0:32, :] = total[0:32, :OWN]
    grad_whiten[32:64, :] = other[0:32, :OWN]
    turned = jnp.concatenate([total[32:72], other[32:72]], axis=0).T[:OWN]
    grad_anchors[...] = lax.dot_general(
        turned, entry_order(f32), (((1,), (1,)), ((), ())),
        precision=lax.Precision.HIGHEST, preferred_element_type=f32,
    )
    first, last = rim_lanes(total[72:80])
    image = middle[...] + jnp.concatenate([first, jnp.zeros((8, 256), f32), last], axis=1)
    for colour in range(3):
        grad_image[colour] = image[2 * colour : 2 * colour + 2]


def hold(value, *after):
    def kernel(*refs):
        del refs

    return pl.pallas_call(
        kernel,
        out_shape=jax.ShapeDtypeStruct(value.shape, value.dtype),
        in_specs=[pl.BlockSpec(memory_space=pl.ANY)] * (1 + len(after)),
        out_specs=pl.BlockSpec(memory_space=pl.ANY),
        input_output_aliases={0: 0},
        compiler_params=pltpu.CompilerParams(vmem_limit_bytes=MIB),
        cost_estimate=pl.CostEstimate(flops=1000, bytes_accessed=1000, transcendentals=0),
    )(value, *after)


def call(kernel, outs, scratch, flops, limit, *args, loose=0):
    size = lambda shape, dtype: math.prod(shape) * jnp.dtype(dtype).itemsize
    tight = len(args) - loose
    moved = sum(size(a.shape, a.dtype) for a in args[:tight]) + sum(size(*out) for out in outs)
    return pl.pallas_call(
        kernel,
        out_shape=[jax.ShapeDtypeStruct(shape, dtype) for shape, dtype in outs],
        in_specs=[pl.BlockSpec(memory_space=pltpu.VMEM)] * tight
        + [pl.BlockSpec(memory_space=pl.ANY)] * loose,
        out_specs=[pl.BlockSpec(memory_space=pltpu.VMEM)] * len(outs),
        scratch_shapes=[pltpu.VMEM(shape, dtype) for shape, dtype in scratch],
        compiler_params=pltpu.CompilerParams(vmem_limit_bytes=limit * MIB),
        cost_estimate=pl.CostEstimate(flops=flops, bytes_accessed=moved, transcendentals=0),
    )(*args)


def shards(image, mask, anchors, whiten, cotangent):
    def send(value, dx, other):
        return lax.ppermute(value, CHAN, route(dx, other))

    part = ((OWN, FLAT + 128), bf16)
    own, *away = call(
        quarter_kernel, [part] * 4, [((4, OWN, FLAT), bf16)], 1_000_000, 6, cotangent, anchors
    )
    quarters = [own] + [send(value, 0, other) for other, value in enumerate(away, 1)]
    (bundle,) = call(
        bundle_kernel, [((512, 128), bf16)], [], 1_000_000, 4, whiten, away[2], loose=1
    )

    stacked = jnp.concatenate([image, mask.astype(bf16)[None]], axis=0)
    (tile,) = call(
        rim_kernel, [((4, ROWS, 128), bf16)], [], 1_000_000, 4, stacked, away[2], loose=1
    )
    (block,) = call(
        join_kernel,
        [((KEPT, FLAT), bf16)],
        [],
        1_000_000,
        4,
        *quarters, tile, bundle,
        loose=2,
    )
    last, following = send(block, 1, 0), send(block, 3, 0)
    bundle = hold(bundle, block)
    shared = [bundle] + [send(bundle, 0, other) for other in (1, 2, 3)]
    half = ((KEPT // 2, FLAT), bf16)
    upper, lower = call(
        halve_kernel, [half, half], [], 1_000_000, 4, last, following, tile, loose=1
    )
    first_blocks = (block, following, last)
    last_blocks = (send(upper, 1, 0), send(lower, 3, 0))

    plane = ((ROWS, LANES), f32)
    patches, tissue, scale, norm, inv_square, inv_density, anch, anch_t = call(
        patch_kernel,
        [
            ((36 * GROUP, LANES), bf16),
            plane,
            plane,
            plane,
            plane,
            ((8, 128), f32),
            ((KEPT, 80), bf16),
            ((80, KEPT), bf16),
        ],
        [((ROWS, 768), f32)],
        1_000_000_000,
        12,
        stacked, lax.ppermute(tile, STRIPS + CHAN, seams()), *quarters,
    )
    (wturned,) = call(turn_kernel, [((KEPT, 1024), bf16)], [], 500_000_000, 8, *shared)
    masked, whitened = call(
        forward_kernel,
        [((ROWS, KEPT, LANES), bf16), ((KEPT, FLAT), bf16)],
        [((ROWS, KEPT, 128), f32), ((LANES, 128), bf16)],
        3_000_000_000,
        18,
        patches, tissue, scale, norm, inv_density, anch,
    )
    rows = ((512, 128), bf16)
    partial, *early = call(
        early_kernel,
        [((KEPT, FLAT), f32)] + [rows] * 4,
        [],
        2_000_000_000,
        14,
        *first_blocks, wturned, whitened,
    )
    anchor_grad, image_part = call(
        backward_kernel,
        [((80, KEPT), f32), ((128, LANES), bf16)],
        [((ROWS * KEPT, 128), bf16), ((36 * GROUP, LANES), f32), ((128, LANES), bf16)],
        5_000_000_000,
        24,
        *last_blocks, partial, wturned, inv_density, masked, patches, inv_square, anch_t,
    )

    parts = lax.all_to_all(image_part.reshape(16, 8, LANES), CHAN, 0, 0)
    rows = ((560, 128), bf16)
    own, *away = call(
        finish_kernel,
        [rows] * 4,
        [],
        20_000_000_000,
        12,
        *last_blocks, whitened, *early, anchor_grad,
    )
    middle, kept, *others = call(
        chip_kernel,
        [((8, 512), f32)] + [((176, 128), bf16)] * 4,
        [((560, 128), f32)],
        1_000_000,
        8,
        parts, own, *(send(value, 0, other) for other, value in enumerate(away, 1)),
    )
    others = [
        lax.ppermute(value, "y", [(y, (y + step) % 4) for y in range(4)])
        for step, value in enumerate(others, 1)
    ]
    (packed,) = call(
        pack_kernel, [((4, 80, 128), bf16)], [((128, 128), f32)], 1_000_000, 4, kept, *others
    )
    return tuple(
        call(
            unpack_kernel,
            [((OWN, 75), f32), ((OWN, OWN), f32), ((3, 2, 512), f32)],
            [],
            1_000_000,
            4,
            lax.all_to_all(packed, "z_hi", 0, 0), middle,
        )
    )


def solution(mesh):
    fine = Mesh(mesh.devices.reshape(4, 4, 4, 2, 2), STRIPS + CHAN)
    placed = (
        P(None, None, STRIPS),
        P(None, STRIPS),
        P(CHAN, None),
        P(None, CHAN),
        P(CHAN, None, STRIPS),
    )
    return jax.shard_map(
        shards,
        mesh=fine,
        in_specs=placed,
        out_specs=(P(CHAN, None), P(STRIPS, CHAN), P(None, CHAN, STRIPS)),
        check_vma=False,
    )
```

```python
import math

import jax
import jax.numpy as jnp
from jax import lax
from jax.experimental import pallas as pl
from jax.experimental.pallas import tpu as pltpu
from jax.sharding import Mesh
from jax.sharding import PartitionSpec as P

EPS = 1e-05
LANES = 256
REACH = 135
QUARTER = 64
FLAT = 16 * QUARTER
ROWS = 32
GROUP = 16
OWN = 64
KEPT = 4 * OWN
STEP = 16
EARLY = 12
MIB = 1024 * 1024

STRIPS = ("z_hi", "y")
CHAN = ("x", "z_lo", "core")


def route(dx, other):
    return [(i, (i // 4 + dx) % 4 * 4 + (i % 4 ^ other)) for i in range(16)]


def seams():
    pairs = [(16 * s + 4 * x, 16 * s - 16 + 4 * x + 3) for s in range(1, 16) for x in range(4)]
    return pairs + [(b, a) for a, b in pairs]


f32 = jnp.float32
bf16 = jnp.bfloat16


def tap(distance):
    return math.exp(-distance * distance / 8.0) if abs(distance) <= 4 else 0.0


def taps(distance):
    far = jnp.abs(distance) > 4
    distance = distance.astype(f32)
    return jnp.where(far, 0.0, jnp.exp(distance * distance * (-1.0 / 8.0)))


def places(shape):
    return tuple(lax.broadcasted_iota(jnp.int32, shape, dim) for dim in (0, 1))


def column_pool():
    lane, target = places((LANES, 128))
    return taps(2 * (target & 63) - lane + 4).astype(bf16)


def column_spread():
    target, lane = places((128, LANES))
    return taps(2 * (target & 63) - lane + 4).astype(bf16)


def row_weights(t, i):
    low, high = tap(4 * t - i), tap(4 * t + 2 - i)
    if low == 0.0 and high == 0.0:
        return None
    return jnp.where(lax.broadcasted_iota(jnp.int32, (1, 128), 1) < QUARTER, low, high)


def row_pool(odd):
    t, i = places((8, ROWS))
    return taps(4 * t + 2 * odd - i)


def split_group(row):
    q = row & (GROUP - 1)
    colour = jnp.where(q < 5, 0, jnp.where(q < 10, 1, jnp.where(q < 15, 2, 3)))
    return row >> 4, colour, q - 5 * colour


def ones(hit, dtype=bf16):
    return jnp.where(hit, 1.0, 0.0).astype(dtype)


def replicate_rows():
    out, src = places((36 * GROUP, 3 * ROWS))
    r, colour, _ = split_group(out)
    return ones(((src & 31) == r - 2) & ((src >> 5) == colour))


def fold_rows():
    out, src = places((128, 36 * GROUP))
    r, colour, _ = split_group(src)
    i = 2 * (out >> 3) + (out & 1)
    return ones((r == i + 2) & (colour == ((out & 7) >> 1)) & (colour < 3))


def entry_order(dtype, rows=75):
    entry, out = places((rows, 80))
    a, colour, b = split_group(out)
    return ones((entry == 25 * colour + 5 * a + b) & (colour < 3), dtype)


def quarter():
    return lax.axis_index("z_lo") * 2 + lax.axis_index("core")


def flipped(axis, bit):
    return lax.rem(lax.axis_index(axis) + bit, 2)


def block_of(p):
    dx, other = (0, 1, 3, 2)[p // 4], p % 4
    ex = lax.rem(lax.axis_index("x") + dx, 4)
    return ex * 4 + flipped("z_lo", other // 2) * 2 + flipped("core", other % 2)


def dot(a, b):
    return jnp.dot(a, b, preferred_element_type=f32)


def dot_nt(a, b):
    return lax.dot_general(a, b, (((1,), (1,)), ((), ())), preferred_element_type=f32)


def quarter_kernel(cotangent, anchors, own, core, zed, both, parts):
    lane = lax.broadcasted_iota(jnp.int32, (OWN, 128), 1)
    for t in range(8):
        low, high = (cotangent[:, 2 * t + n, :].astype(f32) for n in (0, 1))
        for side in range(2):
            cols = slice(side * 128, side * 128 + 128)
            even = jnp.where(lane < QUARTER, low[:, cols], pltpu.roll(high[:, cols], QUARTER, 1))
            odd = jnp.where(lane < QUARTER, pltpu.roll(low[:, cols], QUARTER, 1), high[:, cols])
            parts[2 * side, :, t * 128 : (t + 1) * 128] = even.astype(bf16)
            parts[2 * side + 1, :, t * 128 : (t + 1) * 128] = odd.astype(bf16)
    for other, part in enumerate((own, core, zed, both)):
        part[:, :FLAT] = parts[flipped("z_lo", other // 2) * 2 + flipped("core", other % 2)]
        part[:, FLAT:] = jnp.zeros((OWN, 128), bf16)
        part[:, FLAT : FLAT + 75] = anchors[...]


def join_kernel(*refs):
    *parts, _, _, joined = refs
    start = 0
    for ref in parts:
        joined[start : start + ref.shape[0]] = ref[:, :FLAT]
        start += ref.shape[0]


def bundle_kernel(whiten, after, bundle):
    del after
    bundle[:, :OWN] = whiten[0:512, :]
    bundle[:, OWN:] = whiten[512:1024, :]


def halve_kernel(first, second, after, upper, lower):
    del after
    upper[...] = first[: KEPT // 2]
    lower[...] = second[KEPT // 2 :]


def rim_kernel(stacked, *refs):
    tile = refs[-1]
    first = quarter() == 0
    for c in range(4):
        value = stacked[c].astype(f32)
        tile[c] = jnp.where(first, value[:, :128], value[:, 384:]).astype(bf16)


def patch_kernel(
    stacked, beyond, *refs,
):
    quarters = refs[:4]
    patches, tissue, scale, norm, inv_square, inv_density, anch, anch_t, wide = refs[4:]
    start = pl.multiple_of(quarter() * 128, 128)

    def part(c, shift):
        rim = beyond[c].astype(f32)
        wide[:, 0:128] = rim
        wide[:, 128:640] = stacked[c].astype(f32)
        wide[:, 640:768] = rim
        return pltpu.roll(wide[:, pl.ds(start, 384)], 384 - shift, 1)[:, :LANES]

    colours = [part(c, 122) for c in range(3)]
    here = part(3, 124)
    lane = lax.broadcasted_iota(jnp.int32, here.shape, 1)
    here = jnp.where(lane < REACH, here, 0.0)
    tissue[...] = here
    x = dot(replicate_rows(), jnp.concatenate(colours, axis=0).astype(bf16))
    offset = (lax.broadcasted_iota(jnp.int32, x.shape, 0) % GROUP) % 5
    s = x
    for b in range(1, 5):
        s = jnp.where(offset == b, pltpu.roll(x, LANES - b, 1), s)
    patches[...] = s.astype(bf16)
    square = jnp.sum((s * s).reshape(36, GROUP, LANES), axis=1)
    total = square[0:ROWS]
    for a in range(1, 5):
        total = total + square[a : a + ROWS]
    total = total + EPS
    root = lax.rsqrt(total)
    scale[...] = 4.0 * root
    norm[...] = total * root
    inv_square[...] = 1.0 / total
    counted = dot(here.astype(bf16), column_pool())
    even, odd = (
        jnp.dot(row_pool(n), counted, precision=lax.Precision.HIGHEST, preferred_element_type=f32)
        for n in (0, 1)
    )
    lane = lax.broadcasted_iota(jnp.int32, even.shape, 1)
    inv_density[...] = 1.0 / jnp.maximum(jnp.where(lane < QUARTER, even, odd), 1.0)
    anchors = jnp.concatenate([part[:, FLAT:] for part in quarters], axis=0)
    ordered = dot(anchors, entry_order(bf16, 128))
    anch[...] = ordered.astype(bf16)
    anch_t[...] = ordered.T.astype(bf16)

def turn_kernel(*refs):
    *shared, wturned = refs
    blocks = [block_of(p) for p in range(16)]
    for n, bundle in enumerate(shared):
        ordered = []
        for block in blocks:
            rows = pl.ds(pl.multiple_of(lax.rem(block, 8) * OWN, OWN), OWN)
            value = bundle[rows, :].astype(f32)
            ordered.append(jnp.where(block >= 8, pltpu.roll(value, OWN, 1), value))
        turned = jnp.concatenate(ordered, axis=0).T
        wturned[n * OWN : (n + 1) * OWN, :] = turned[:OWN].astype(bf16)


def forward_kernel(
    patches, tissue, scale, norm, inv_density, anch,
    masked, whitened,
    columned, pool,
):
    pool[...] = column_pool()

    @pl.loop(0, ROWS // STEP)
    def _(t):
        lifted = []
        for r in range(STEP):
            i = t * STEP + r
            patch = patches[pl.ds(pl.multiple_of(i * GROUP, GROUP), 80), :]
            raw = dot(anch[...], patch)
            value = jnp.exp(raw * scale[pl.ds(i, 1), :] - 4.0) * tissue[pl.ds(i, 1), :]
            masked[i] = value.astype(bf16)
            lifted.append((value * norm[pl.ds(i, 1), :]).astype(bf16))
        result = dot(jnp.concatenate(lifted, axis=0), pool[...])
        columned[pl.ds(t * STEP, STEP)] = result.reshape(STEP, KEPT, 128)

    for t in range(8):
        acc = None
        for i in range(ROWS):
            weights = row_weights(t, i)
            if weights is not None:
                term = weights * columned[i]
                acc = term if acc is None else acc + term
        whitened[:, t * 128 : (t + 1) * 128] = (acc * inv_density[t : t + 1, :]).astype(bf16)


def fold(block, rows):
    top, low = block[:rows], block[rows:]
    left = lax.broadcasted_iota(jnp.int32, top.shape, 1) < OWN
    own = jnp.where(left, top, pltpu.roll(low, OWN, 1))
    partner = jnp.where(left, pltpu.roll(top, OWN, 1), low)
    return own.astype(bf16), partner.astype(bf16)


def stacks(blocks):
    for n in range(FLAT // 256):
        cols = slice(n * 256, (n + 1) * 256)
        yield cols, jnp.concatenate([block[:, cols] for block in blocks], axis=0)


def whiten_rows(blocks, whitened):
    return sum(dot_nt(stack, whitened[:, cols]) for cols, stack in stacks(blocks))


def four_folds(block, rows):
    return fold(block[:, :128], rows) + fold(block[:, 128:], rows)


def place_rows(sums, grad_w, first):
    for n in range(grad_w.shape[0] // OWN):
        strip = block_of(first + n)
        place = lax.rem(strip, 4) * 4 + strip // 4
        rows = pl.ds(pl.multiple_of(place * 32, 32), 32)
        for ref, value in zip(sums, four_folds(grad_w[n * OWN : (n + 1) * OWN], OWN // 2)):
            ref[rows, :] = value


def early_kernel(*refs):
    blocks, (wturned, whitened, partial, *sums) = refs[:3], refs[3:]
    for ref in sums:
        ref[...] = jnp.zeros_like(ref)
    for cols, stack in stacks(blocks):
        partial[:, cols] = dot(wturned[:, : EARLY * OWN], stack)
    place_rows(sums, whiten_rows(blocks, whitened), 0)


def backward_kernel(
    first, second, partial, wturned, inv_density, masked, patches, inv_square, anch_t,
    anchor_grad, image,
    rowed, spread_grad, pool_t,
):
    pool_t[...] = column_spread()
    scaled = []
    for cols, stack in stacks((first, second)):
        pooled = partial[:, cols] + dot(wturned[:, EARLY * OWN :], stack)
        for side in range(2):
            t = len(scaled)
            part = pooled[:, side * 128 : (side + 1) * 128]
            scaled.append(part.astype(bf16).astype(f32) * (4.0 * inv_density[t : t + 1, :]))
    for i in range(ROWS):
        acc = None
        for t in range(8):
            weights = row_weights(t, i)
            if weights is not None:
                term = weights * scaled[t]
                acc = term if acc is None else acc + term
        rowed[i * KEPT : (i + 1) * KEPT, :] = acc.astype(bf16)
    spread_grad[...] = jnp.zeros_like(spread_grad)
    anchor_grad[...] = jnp.zeros_like(anchor_grad)

    @pl.loop(0, ROWS // STEP)
    def _(t):
        start = pl.multiple_of(t * (STEP * KEPT), STEP * KEPT)
        spread = dot(rowed[pl.ds(start, STEP * KEPT), :], pool_t[...])
        grads, wides, units = [], [], []
        for r in range(STEP):
            i = t * STEP + r
            patch = patches[pl.ds(pl.multiple_of(i * GROUP, GROUP), 80), :]
            grad = (spread[r * KEPT : (r + 1) * KEPT] * masked[i].astype(f32)).astype(bf16)
            unit = dot(anch_t[...], grad)
            wide = patch.astype(f32)
            along = jnp.sum(wide * unit, axis=0, keepdims=True) * inv_square[pl.ds(i, 1), :]
            units.append(unit - wide * along)
            grads.append(grad)
            wides.append(patch)
        anchor_grad[...] += dot_nt(jnp.concatenate(wides, axis=1), jnp.concatenate(grads, axis=1))
        sums = []
        for g in range(STEP + 4):
            acc = None
            for r in range(STEP):
                if 0 <= g - r < 5:
                    term = units[r][(g - r) * GROUP : (g - r + 1) * GROUP]
                    acc = term if acc is None else acc + term
            sums.append(acc)
        here = pl.ds(pl.multiple_of(t * (STEP * GROUP), STEP * GROUP), (STEP + 4) * GROUP)
        spread_grad[here, :] += jnp.concatenate(sums, axis=0)

    t = spread_grad[...]
    offset = (lax.broadcasted_iota(jnp.int32, t.shape, 0) % GROUP) % 5
    moved = t
    for b in range(1, 5):
        moved = jnp.where(offset == b, pltpu.roll(t, b, 1), moved)
    high = moved.astype(bf16)
    low = (moved - high.astype(f32)).astype(bf16)
    folder = fold_rows()
    image[...] = (dot(folder, high) + dot(folder, low)).astype(bf16)


def finish_kernel(*refs):
    first, second, whitened, *early = refs[:7]
    anchor_grad, *sums = refs[7:]
    pad = jnp.zeros((8, 128), bf16)
    for ref, start, part in zip(sums, early, four_folds(anchor_grad[...], 40)):
        ref[0:512, :] = start[...]
        ref[512:560, :] = jnp.concatenate([part, pad], axis=0)
    place_rows(sums, whiten_rows((first, second), whitened), EARLY)


def add_up(refs):
    total = refs[0][...].astype(f32)
    for ref in refs[1:]:
        total = total + ref[...].astype(f32)
    return total


def rim_lanes(rims):
    lane = lax.broadcasted_iota(jnp.int32, rims.shape, 1)
    return jnp.where(lane < 6, rims, 0.0), jnp.where(lane >= 122, rims, 0.0)


def chip_kernel(parts, own, one, two, three, middle, kept, next_one, next_two, next_three, sums):
    gap = jnp.zeros((8, 128), f32)
    whole = None
    for q in range(4):
        part = add_up([parts.at[4 * x + q] for x in range(4)])
        pieces = [gap] * q + [part] + [gap] * (3 - q)
        placed = jnp.concatenate(pieces, axis=1)
        whole = placed if whole is None else whole + placed
    turned = pltpu.roll(whole, 640 - 6, 1)
    middle[...] = turned[:, :512]
    later, earlier = rim_lanes(turned[:, 512:])
    y, z = lax.axis_index("y"), lax.axis_index("z_hi")
    later = jnp.where((y == 3) & (z == 3), 0.0, later)
    earlier = jnp.where((y == 0) & (z == 0), 0.0, earlier)
    later = jnp.where(y == 3, pltpu.roll(later, 64, 1), later)
    earlier = jnp.where(y == 0, pltpu.roll(earlier, 64, 1), earlier)
    sums[...] = add_up((own, one, two, three))
    for step, part in enumerate((kept, next_one, next_two, next_three)):
        target = lax.rem(y + step, 4)
        part[0:128, :] = sums[pl.ds(pl.multiple_of(target * 128, 128), 128), :].astype(bf16)
        rims = {1: later, 3: earlier}.get(step, gap)
        part[128:176, :] = jnp.concatenate([sums[512:552, :], rims], axis=0).astype(bf16)


def pack_kernel(kept, one, two, three, packed, sums):
    total = add_up((kept, one, two, three))
    sums[...] = total[0:128]
    straight = rim_lanes(total[168:176])
    onward = rim_lanes(pltpu.roll(total[168:176], 64, 1))
    rims = (straight[0] + straight[1], onward[0], jnp.zeros((8, 128), f32), onward[1])
    for step in range(4):
        z = lax.rem(lax.axis_index("z_hi") + step, 4)
        packed[z, 0:32, :] = sums[pl.ds(pl.multiple_of(z * 32, 32), 32), :].astype(bf16)
        packed[z, 32:80, :] = jnp.concatenate([total[128:168], rims[step]], axis=0).astype(bf16)


def unpack_kernel(received, middle, grad_anchors, grad_whiten, grad_image):
    total = add_up([received.at[z] for z in range(4)])
    other = pltpu.roll(total, OWN, 1)
    grad_whiten[0:32, :] = total[0:32, :OWN]
    grad_whiten[32:64, :] = other[0:32, :OWN]
    turned = jnp.concatenate([total[32:72], other[32:72]], axis=0).T[:OWN]
    grad_anchors[...] = lax.dot_general(
        turned, entry_order(f32), (((1,), (1,)), ((), ())),
        precision=lax.Precision.HIGHEST, preferred_element_type=f32,
    )
    first, last = rim_lanes(total[72:80])
    image = middle[...] + jnp.concatenate([first, jnp.zeros((8, 256), f32), last], axis=1)
    for colour in range(3):
        grad_image[colour] = image[2 * colour : 2 * colour + 2]


def hold(value, *after):
    def kernel(*refs):
        del refs

    return pl.pallas_call(
        kernel,
        out_shape=jax.ShapeDtypeStruct(value.shape, value.dtype),
        in_specs=[pl.BlockSpec(memory_space=pl.ANY)] * (1 + len(after)),
        out_specs=pl.BlockSpec(memory_space=pl.ANY),
        input_output_aliases={0: 0},
        compiler_params=pltpu.CompilerParams(vmem_limit_bytes=MIB),
        cost_estimate=pl.CostEstimate(flops=1000, bytes_accessed=1000, transcendentals=0),
    )(value, *after)


def call(kernel, outs, scratch, flops, limit, *args, loose=0):
    size = lambda shape, dtype: math.prod(shape) * jnp.dtype(dtype).itemsize
    tight = len(args) - loose
    moved = sum(size(a.shape, a.dtype) for a in args[:tight]) + sum(size(*out) for out in outs)
    return pl.pallas_call(
        kernel,
        out_shape=[jax.ShapeDtypeStruct(shape, dtype) for shape, dtype in outs],
        in_specs=[pl.BlockSpec(memory_space=pltpu.VMEM)] * tight
        + [pl.BlockSpec(memory_space=pl.ANY)] * loose,
        out_specs=[pl.BlockSpec(memory_space=pltpu.VMEM)] * len(outs),
        scratch_shapes=[pltpu.VMEM(shape, dtype) for shape, dtype in scratch],
        compiler_params=pltpu.CompilerParams(vmem_limit_bytes=limit * MIB),
        cost_estimate=pl.CostEstimate(flops=flops, bytes_accessed=moved, transcendentals=0),
    )(*args)


def shards(image, mask, anchors, whiten, cotangent):
    def send(value, dx, other):
        return lax.ppermute(value, CHAN, route(dx, other))

    part = ((OWN, FLAT + 128), bf16)
    own, *away = call(
        quarter_kernel, [part] * 4, [((4, OWN, FLAT), bf16)], 1_000_000, 6, cotangent, anchors
    )
    quarters = [own] + [send(value, 0, other) for other, value in enumerate(away, 1)]
    (bundle,) = call(
        bundle_kernel, [((512, 128), bf16)], [], 1_000_000, 4, whiten, away[2], loose=1
    )

    stacked = jnp.concatenate([image, mask.astype(bf16)[None]], axis=0)
    (tile,) = call(
        rim_kernel, [((4, ROWS, 128), bf16)], [], 1_000_000, 4, stacked, away[2], loose=1
    )
    (block,) = call(
        join_kernel,
        [((KEPT, FLAT), bf16)],
        [],
        1_000_000,
        4,
        *quarters, tile, bundle,
        loose=2,
    )
    last, following = send(block, 1, 0), send(block, 3, 0)
    bundle = hold(bundle, block)
    shared = [bundle] + [send(bundle, 0, other) for other in (1, 2, 3)]
    plane = ((ROWS, LANES), f32)
    patches, tissue, scale, norm, inv_square, inv_density, anch, anch_t = call(
        patch_kernel,
        [
            ((36 * GROUP, LANES), bf16),
            plane,
            plane,
            plane,
            plane,
            ((8, 128), f32),
            ((KEPT, 80), bf16),
            ((80, KEPT), bf16),
        ],
        [((ROWS, 768), f32)],
        1_000_000_000,
        12,
        stacked, lax.ppermute(tile, STRIPS + CHAN, seams()), *quarters,
    )
    (wturned,) = call(turn_kernel, [((KEPT, 1024), bf16)], [], 500_000_000, 8, *shared)
    masked, whitened = call(
        forward_kernel,
        [((ROWS, KEPT, LANES), bf16), ((KEPT, FLAT), bf16)],
        [((ROWS, KEPT, 128), f32), ((LANES, 128), bf16)],
        3_000_000_000,
        18,
        patches, tissue, scale, norm, inv_density, anch,
    )
    half = ((KEPT // 2, FLAT), bf16)
    upper, lower = call(
        halve_kernel, [half, half], [], 1_000_000, 4, last, following, whitened, loose=1
    )
    first_blocks = (block, following, last)
    last_blocks = (send(upper, 1, 0), send(lower, 3, 0))
    rows = ((512, 128), bf16)
    partial, *early = call(
        early_kernel,
        [((KEPT, FLAT), f32)] + [rows] * 4,
        [],
        2_000_000_000,
        14,
        *first_blocks, wturned, whitened,
    )
    anchor_grad, image_part = call(
        backward_kernel,
        [((80, KEPT), f32), ((128, LANES), bf16)],
        [((ROWS * KEPT, 128), bf16), ((36 * GROUP, LANES), f32), ((128, LANES), bf16)],
        5_000_000_000,
        24,
        *last_blocks, partial, wturned, inv_density, masked, patches, inv_square, anch_t,
    )

    parts = lax.all_to_all(image_part.reshape(16, 8, LANES), CHAN, 0, 0)
    rows = ((560, 128), bf16)
    own, *away = call(
        finish_kernel,
        [rows] * 4,
        [],
        20_000_000_000,
        12,
        *last_blocks, whitened, *early, anchor_grad,
    )
    middle, kept, *others = call(
        chip_kernel,
        [((8, 512), f32)] + [((176, 128), bf16)] * 4,
        [((560, 128), f32)],
        1_000_000,
        8,
        parts, own, *(send(value, 0, other) for other, value in enumerate(away, 1)),
    )
    others = [
        lax.ppermute(value, "y", [(y, (y + step) % 4) for y in range(4)])
        for step, value in enumerate(others, 1)
    ]
    (packed,) = call(
        pack_kernel, [((4, 80, 128), bf16)], [((128, 128), f32)], 1_000_000, 4, kept, *others
    )
    return tuple(
        call(
            unpack_kernel,
            [((OWN, 75), f32), ((OWN, OWN), f32), ((3, 2, 512), f32)],
            [],
            1_000_000,
            4,
            lax.all_to_all(packed, "z_hi", 0, 0), middle,
        )
    )


def solution(mesh):
    fine = Mesh(mesh.devices.reshape(4, 4, 4, 2, 2), STRIPS + CHAN)
    placed = (
        P(None, None, STRIPS),
        P(None, STRIPS),
        P(CHAN, None),
        P(None, CHAN),
        P(CHAN, None, STRIPS),
    )
    return jax.shard_map(
        shards,
        mesh=fine,
        in_specs=placed,
        out_specs=(P(CHAN, None), P(STRIPS, CHAN), P(None, CHAN, STRIPS)),
        check_vma=False,
    )
```

```python
import math

import jax
import jax.numpy as jnp
from jax import lax
from jax.experimental import pallas as pl
from jax.experimental.pallas import tpu as pltpu
from jax.sharding import Mesh
from jax.sharding import PartitionSpec as P

EPS = 1e-05
LANES = 256
REACH = 135
QUARTER = 64
FLAT = 16 * QUARTER
ROWS = 32
GROUP = 16
OWN = 64
KEPT = 4 * OWN
STEP = 16
EARLY = 12
MIB = 1024 * 1024

STRIPS = ("z_hi", "y")
CHAN = ("x", "z_lo", "core")


def route(dx, other):
    return [(i, (i // 4 + dx) % 4 * 4 + (i % 4 ^ other)) for i in range(16)]


def seams():
    pairs = [(16 * s + 4 * x, 16 * s - 16 + 4 * x + 3) for s in range(1, 16) for x in range(4)]
    return pairs + [(b, a) for a, b in pairs]


f32 = jnp.float32
bf16 = jnp.bfloat16


def tap(distance):
    return math.exp(-distance * distance / 8.0) if abs(distance) <= 4 else 0.0


def taps(distance):
    far = jnp.abs(distance) > 4
    distance = distance.astype(f32)
    return jnp.where(far, 0.0, jnp.exp(distance * distance * (-1.0 / 8.0)))


def places(shape):
    return tuple(lax.broadcasted_iota(jnp.int32, shape, dim) for dim in (0, 1))


def column_pool():
    lane, target = places((LANES, 128))
    return taps(2 * (target & 63) - lane + 4).astype(bf16)


def column_spread():
    target, lane = places((128, LANES))
    return taps(2 * (target & 63) - lane + 4).astype(bf16)


def row_weights(t, i):
    low, high = tap(4 * t - i), tap(4 * t + 2 - i)
    if low == 0.0 and high == 0.0:
        return None
    return jnp.where(lax.broadcasted_iota(jnp.int32, (1, 128), 1) < QUARTER, low, high)


def row_pool(odd):
    t, i = places((8, ROWS))
    return taps(4 * t + 2 * odd - i)


def split_group(row):
    q = row & (GROUP - 1)
    colour = jnp.where(q < 5, 0, jnp.where(q < 10, 1, jnp.where(q < 15, 2, 3)))
    return row >> 4, colour, q - 5 * colour


def ones(hit, dtype=bf16):
    return jnp.where(hit, 1.0, 0.0).astype(dtype)


def replicate_rows():
    out, src = places((36 * GROUP, 3 * ROWS))
    r, colour, _ = split_group(out)
    return ones(((src & 31) == r - 2) & ((src >> 5) == colour))


def fold_rows():
    out, src = places((128, 36 * GROUP))
    r, colour, _ = split_group(src)
    i = 2 * (out >> 3) + (out & 1)
    return ones((r == i + 2) & (colour == ((out & 7) >> 1)) & (colour < 3))


def entry_order(dtype, rows=75):
    entry, out = places((rows, 80))
    a, colour, b = split_group(out)
    return ones((entry == 25 * colour + 5 * a + b) & (colour < 3), dtype)


def quarter():
    return lax.axis_index("z_lo") * 2 + lax.axis_index("core")


def flipped(axis, bit):
    return lax.rem(lax.axis_index(axis) + bit, 2)


def block_of(p):
    dx, other = (0, 1, 3, 2)[p // 4], p % 4
    ex = lax.rem(lax.axis_index("x") + dx, 4)
    return ex * 4 + flipped("z_lo", other // 2) * 2 + flipped("core", other % 2)


def dot(a, b):
    return jnp.dot(a, b, preferred_element_type=f32)


def dot_nt(a, b):
    return lax.dot_general(a, b, (((1,), (1,)), ((), ())), preferred_element_type=f32)


def quarter_kernel(cotangent, anchors, own, core, zed, both, parts):
    lane = lax.broadcasted_iota(jnp.int32, (OWN, 128), 1)
    for t in range(8):
        low, high = (cotangent[:, 2 * t + n, :].astype(f32) for n in (0, 1))
        for side in range(2):
            cols = slice(side * 128, side * 128 + 128)
            even = jnp.where(lane < QUARTER, low[:, cols], pltpu.roll(high[:, cols], QUARTER, 1))
            odd = jnp.where(lane < QUARTER, pltpu.roll(low[:, cols], QUARTER, 1), high[:, cols])
            parts[2 * side, :, t * 128 : (t + 1) * 128] = even.astype(bf16)
            parts[2 * side + 1, :, t * 128 : (t + 1) * 128] = odd.astype(bf16)
    for other, part in enumerate((own, core, zed, both)):
        part[:, :FLAT] = parts[flipped("z_lo", other // 2) * 2 + flipped("core", other % 2)]
        part[:, FLAT:] = jnp.zeros((OWN, 128), bf16)
        part[:, FLAT : FLAT + 75] = anchors[...]


def join_kernel(upper, lower, *refs):
    refs[-1][:OWN] = upper[:, :FLAT]
    refs[-1][OWN:] = lower[:, :FLAT]


def bundle_kernel(whiten, after, bundle):
    del after
    bundle[:, :OWN] = whiten[0:512, :]
    bundle[:, OWN:] = whiten[512:1024, :]


def rim_kernel(stacked, *refs):
    tile = refs[-1]
    first = quarter() == 0
    for c in range(4):
        value = stacked[c].astype(f32)
        tile[c] = jnp.where(first, value[:, :128], value[:, 384:]).astype(bf16)


def patch_kernel(
    stacked, beyond, *refs,
):
    quarters = refs[:4]
    patches, tissue, scale, norm, inv_square, inv_density, anch, anch_t, wide = refs[4:]
    start = pl.multiple_of(quarter() * 128, 128)

    def part(c, shift):
        rim = beyond[c].astype(f32)
        wide[:, 0:128] = rim
        wide[:, 128:640] = stacked[c].astype(f32)
        wide[:, 640:768] = rim
        return pltpu.roll(wide[:, pl.ds(start, 384)], 384 - shift, 1)[:, :LANES]

    colours = [part(c, 122) for c in range(3)]
    here = part(3, 124)
    lane = lax.broadcasted_iota(jnp.int32, here.shape, 1)
    here = jnp.where(lane < REACH, here, 0.0)
    tissue[...] = here
    x = dot(replicate_rows(), jnp.concatenate(colours, axis=0).astype(bf16))
    offset = (lax.broadcasted_iota(jnp.int32, x.shape, 0) % GROUP) % 5
    s = x
    for b in range(1, 5):
        s = jnp.where(offset == b, pltpu.roll(x, LANES - b, 1), s)
    patches[...] = s.astype(bf16)
    square = jnp.sum((s * s).reshape(36, GROUP, LANES), axis=1)
    total = square[0:ROWS]
    for a in range(1, 5):
        total = total + square[a : a + ROWS]
    total = total + EPS
    root = lax.rsqrt(total)
    scale[...] = 4.0 * root
    norm[...] = total * root
    inv_square[...] = 1.0 / total
    counted = dot(here.astype(bf16), column_pool())
    even, odd = (
        jnp.dot(row_pool(n), counted, precision=lax.Precision.HIGHEST, preferred_element_type=f32)
        for n in (0, 1)
    )
    lane = lax.broadcasted_iota(jnp.int32, even.shape, 1)
    inv_density[...] = 1.0 / jnp.maximum(jnp.where(lane < QUARTER, even, odd), 1.0)
    anchors = jnp.concatenate([part[:, FLAT:] for part in quarters], axis=0)
    ordered = dot(anchors, entry_order(bf16, 128))
    anch[...] = ordered.astype(bf16)
    anch_t[...] = ordered.T.astype(bf16)

def turn_kernel(*refs):
    *shared, wturned = refs
    blocks = [block_of(p) for p in range(16)]
    for n, bundle in enumerate(shared):
        ordered = []
        for block in blocks:
            rows = pl.ds(pl.multiple_of(lax.rem(block, 8) * OWN, OWN), OWN)
            value = bundle[rows, :].astype(f32)
            ordered.append(jnp.where(block >= 8, pltpu.roll(value, OWN, 1), value))
        turned = jnp.concatenate(ordered, axis=0).T
        wturned[n * OWN : (n + 1) * OWN, :] = turned[:OWN].astype(bf16)


def forward_kernel(
    patches, tissue, scale, norm, inv_density, anch,
    masked, whitened,
    columned, pool,
):
    pool[...] = column_pool()

    @pl.loop(0, ROWS // STEP)
    def _(t):
        lifted = []
        for r in range(STEP):
            i = t * STEP + r
            patch = patches[pl.ds(pl.multiple_of(i * GROUP, GROUP), 80), :]
            raw = dot(anch[...], patch)
            value = jnp.exp(raw * scale[pl.ds(i, 1), :] - 4.0) * tissue[pl.ds(i, 1), :]
            masked[i] = value.astype(bf16)
            lifted.append((value * norm[pl.ds(i, 1), :]).astype(bf16))
        result = dot(jnp.concatenate(lifted, axis=0), pool[...])
        columned[pl.ds(t * STEP, STEP)] = result.reshape(STEP, KEPT, 128)

    for t in range(8):
        acc = None
        for i in range(ROWS):
            weights = row_weights(t, i)
            if weights is not None:
                term = weights * columned[i]
                acc = term if acc is None else acc + term
        whitened[:, t * 128 : (t + 1) * 128] = (acc * inv_density[t : t + 1, :]).astype(bf16)


def fold(block, rows):
    top, low = block[:rows], block[rows:]
    left = lax.broadcasted_iota(jnp.int32, top.shape, 1) < OWN
    own = jnp.where(left, top, pltpu.roll(low, OWN, 1))
    partner = jnp.where(left, pltpu.roll(top, OWN, 1), low)
    return own.astype(bf16), partner.astype(bf16)


def stacks(blocks):
    for n in range(FLAT // 256):
        cols = slice(n * 256, (n + 1) * 256)
        yield cols, jnp.concatenate([block[:, cols] for block in blocks], axis=0)


def whiten_rows(blocks, whitened):
    return sum(dot_nt(stack, whitened[:, cols]) for cols, stack in stacks(blocks))


def four_folds(block, rows):
    return fold(block[:, :128], rows) + fold(block[:, 128:], rows)


def place_rows(sums, grad_w, first):
    for n in range(grad_w.shape[0] // OWN):
        strip = block_of(first + n)
        place = lax.rem(strip, 4) * 4 + strip // 4
        rows = pl.ds(pl.multiple_of(place * 32, 32), 32)
        for ref, value in zip(sums, four_folds(grad_w[n * OWN : (n + 1) * OWN], OWN // 2)):
            ref[rows, :] = value


def early_kernel(*refs):
    blocks, (wturned, whitened, partial, *sums) = refs[:6], refs[6:]
    for ref in sums:
        ref[...] = jnp.zeros_like(ref)
    for cols, stack in stacks(blocks):
        partial[:, cols] = dot(wturned[:, : EARLY * OWN], stack)
    place_rows(sums, whiten_rows(blocks, whitened), 0)


def backward_kernel(
    first, second, partial, wturned, inv_density, masked, patches, inv_square, anch_t,
    anchor_grad, image,
    rowed, spread_grad, pool_t,
):
    pool_t[...] = column_spread()
    scaled = []
    for cols, stack in stacks((first, second)):
        pooled = partial[:, cols] + dot(wturned[:, EARLY * OWN :], stack)
        for side in range(2):
            t = len(scaled)
            part = pooled[:, side * 128 : (side + 1) * 128]
            scaled.append(part.astype(bf16).astype(f32) * (4.0 * inv_density[t : t + 1, :]))
    for i in range(ROWS):
        acc = None
        for t in range(8):
            weights = row_weights(t, i)
            if weights is not None:
                term = weights * scaled[t]
                acc = term if acc is None else acc + term
        rowed[i * KEPT : (i + 1) * KEPT, :] = acc.astype(bf16)
    spread_grad[...] = jnp.zeros_like(spread_grad)
    anchor_grad[...] = jnp.zeros_like(anchor_grad)

    @pl.loop(0, ROWS // STEP)
    def _(t):
        start = pl.multiple_of(t * (STEP * KEPT), STEP * KEPT)
        spread = dot(rowed[pl.ds(start, STEP * KEPT), :], pool_t[...])
        grads, wides, units = [], [], []
        for r in range(STEP):
            i = t * STEP + r
            patch = patches[pl.ds(pl.multiple_of(i * GROUP, GROUP), 80), :]
            grad = (spread[r * KEPT : (r + 1) * KEPT] * masked[i].astype(f32)).astype(bf16)
            unit = dot(anch_t[...], grad)
            wide = patch.astype(f32)
            along = jnp.sum(wide * unit, axis=0, keepdims=True) * inv_square[pl.ds(i, 1), :]
            units.append(unit - wide * along)
            grads.append(grad)
            wides.append(patch)
        anchor_grad[...] += dot_nt(jnp.concatenate(wides, axis=1), jnp.concatenate(grads, axis=1))
        sums = []
        for g in range(STEP + 4):
            acc = None
            for r in range(STEP):
                if 0 <= g - r < 5:
                    term = units[r][(g - r) * GROUP : (g - r + 1) * GROUP]
                    acc = term if acc is None else acc + term
            sums.append(acc)
        here = pl.ds(pl.multiple_of(t * (STEP * GROUP), STEP * GROUP), (STEP + 4) * GROUP)
        spread_grad[here, :] += jnp.concatenate(sums, axis=0)

    t = spread_grad[...]
    offset = (lax.broadcasted_iota(jnp.int32, t.shape, 0) % GROUP) % 5
    moved = t
    for b in range(1, 5):
        moved = jnp.where(offset == b, pltpu.roll(t, b, 1), moved)
    high = moved.astype(bf16)
    low = (moved - high.astype(f32)).astype(bf16)
    folder = fold_rows()
    image[...] = (dot(folder, high) + dot(folder, low)).astype(bf16)


def finish_kernel(*refs):
    first, second, whitened, *early = refs[:7]
    anchor_grad, *sums = refs[7:]
    pad = jnp.zeros((8, 128), bf16)
    for ref, start, part in zip(sums, early, four_folds(anchor_grad[...], 40)):
        ref[0:512, :] = start[...]
        ref[512:560, :] = jnp.concatenate([part, pad], axis=0)
    place_rows(sums, whiten_rows((first, second), whitened), EARLY)


def add_up(refs):
    total = refs[0][...].astype(f32)
    for ref in refs[1:]:
        total = total + ref[...].astype(f32)
    return total


def rim_lanes(rims):
    lane = lax.broadcasted_iota(jnp.int32, rims.shape, 1)
    return jnp.where(lane < 6, rims, 0.0), jnp.where(lane >= 122, rims, 0.0)


def chip_kernel(parts, own, one, two, three, middle, kept, next_one, next_two, next_three, sums):
    gap = jnp.zeros((8, 128), f32)
    whole = None
    for q in range(4):
        part = add_up([parts.at[4 * x + q] for x in range(4)])
        pieces = [gap] * q + [part] + [gap] * (3 - q)
        placed = jnp.concatenate(pieces, axis=1)
        whole = placed if whole is None else whole + placed
    turned = pltpu.roll(whole, 640 - 6, 1)
    middle[...] = turned[:, :512]
    later, earlier = rim_lanes(turned[:, 512:])
    y, z = lax.axis_index("y"), lax.axis_index("z_hi")
    later = jnp.where((y == 3) & (z == 3), 0.0, later)
    earlier = jnp.where((y == 0) & (z == 0), 0.0, earlier)
    later = jnp.where(y == 3, pltpu.roll(later, 64, 1), later)
    earlier = jnp.where(y == 0, pltpu.roll(earlier, 64, 1), earlier)
    sums[...] = add_up((own, one, two, three))
    for step, part in enumerate((kept, next_one, next_two, next_three)):
        target = lax.rem(y + step, 4)
        part[0:128, :] = sums[pl.ds(pl.multiple_of(target * 128, 128), 128), :].astype(bf16)
        rims = {1: later, 3: earlier}.get(step, gap)
        part[128:176, :] = jnp.concatenate([sums[512:552, :], rims], axis=0).astype(bf16)


def pack_kernel(kept, one, two, three, packed, sums):
    total = add_up((kept, one, two, three))
    sums[...] = total[0:128]
    straight = rim_lanes(total[168:176])
    onward = rim_lanes(pltpu.roll(total[168:176], 64, 1))
    rims = (straight[0] + straight[1], onward[0], jnp.zeros((8, 128), f32), onward[1])
    for step in range(4):
        z = lax.rem(lax.axis_index("z_hi") + step, 4)
        packed[z, 0:32, :] = sums[pl.ds(pl.multiple_of(z * 32, 32), 32), :].astype(bf16)
        packed[z, 32:80, :] = jnp.concatenate([total[128:168], rims[step]], axis=0).astype(bf16)


def unpack_kernel(received, middle, grad_anchors, grad_whiten, grad_image):
    total = add_up([received.at[z] for z in range(4)])
    other = pltpu.roll(total, OWN, 1)
    grad_whiten[0:32, :] = total[0:32, :OWN]
    grad_whiten[32:64, :] = other[0:32, :OWN]
    turned = jnp.concatenate([total[32:72], other[32:72]], axis=0).T[:OWN]
    grad_anchors[...] = lax.dot_general(
        turned, entry_order(f32), (((1,), (1,)), ((), ())),
        precision=lax.Precision.HIGHEST, preferred_element_type=f32,
    )
    first, last = rim_lanes(total[72:80])
    image = middle[...] + jnp.concatenate([first, jnp.zeros((8, 256), f32), last], axis=1)
    for colour in range(3):
        grad_image[colour] = image[2 * colour : 2 * colour + 2]


def hold(value, *after):
    def kernel(*refs):
        del refs

    return pl.pallas_call(
        kernel,
        out_shape=jax.ShapeDtypeStruct(value.shape, value.dtype),
        in_specs=[pl.BlockSpec(memory_space=pl.ANY)] * (1 + len(after)),
        out_specs=pl.BlockSpec(memory_space=pl.ANY),
        input_output_aliases={0: 0},
        compiler_params=pltpu.CompilerParams(vmem_limit_bytes=MIB),
        cost_estimate=pl.CostEstimate(flops=1000, bytes_accessed=1000, transcendentals=0),
    )(value, *after)


def call(kernel, outs, scratch, flops, limit, *args, loose=0):
    size = lambda shape, dtype: math.prod(shape) * jnp.dtype(dtype).itemsize
    tight = len(args) - loose
    moved = sum(size(a.shape, a.dtype) for a in args[:tight]) + sum(size(*out) for out in outs)
    return pl.pallas_call(
        kernel,
        out_shape=[jax.ShapeDtypeStruct(shape, dtype) for shape, dtype in outs],
        in_specs=[pl.BlockSpec(memory_space=pltpu.VMEM)] * tight
        + [pl.BlockSpec(memory_space=pl.ANY)] * loose,
        out_specs=[pl.BlockSpec(memory_space=pltpu.VMEM)] * len(outs),
        scratch_shapes=[pltpu.VMEM(shape, dtype) for shape, dtype in scratch],
        compiler_params=pltpu.CompilerParams(vmem_limit_bytes=limit * MIB),
        cost_estimate=pl.CostEstimate(flops=flops, bytes_accessed=moved, transcendentals=0),
    )(*args)


def shards(image, mask, anchors, whiten, cotangent):
    def send(value, dx, other):
        return lax.ppermute(value, CHAN, route(dx, other))

    part = ((OWN, FLAT + 128), bf16)
    own, *away = call(
        quarter_kernel, [part] * 4, [((4, OWN, FLAT), bf16)], 1_000_000, 6, cotangent, anchors
    )
    quarters = [own] + [send(value, 0, other) for other, value in enumerate(away, 1)]
    (bundle,) = call(
        bundle_kernel, [((512, 128), bf16)], [], 1_000_000, 4, whiten, away[2], loose=1
    )

    stacked = jnp.concatenate([image, mask.astype(bf16)[None]], axis=0)
    (tile,) = call(
        rim_kernel, [((4, ROWS, 128), bf16)], [], 1_000_000, 4, stacked, away[2], loose=1
    )
    pair = [((2 * OWN, FLAT), bf16)]
    (near,) = call(join_kernel, pair, [], 1_000_000, 4, *quarters[:2])
    last, following = [send(near, 1, 0)], [send(near, 3, 0)]
    (across,) = call(
        join_kernel,
        pair,
        [],
        1_000_000,
        4,
        *quarters[2:], tile, bundle, last[0], following[0],
        loose=4,
    )
    last.append(send(across, 1, 0))
    following.append(send(across, 3, 0))
    first_blocks = (near, across, *following, *last)
    last_blocks = (send(last[0], 1, 0), send(following[1], 3, 0))
    bundle = hold(bundle, last[1])
    shared = [bundle] + [send(bundle, 0, other) for other in (1, 2, 3)]
    plane = ((ROWS, LANES), f32)
    patches, tissue, scale, norm, inv_square, inv_density, anch, anch_t = call(
        patch_kernel,
        [
            ((36 * GROUP, LANES), bf16),
            plane,
            plane,
            plane,
            plane,
            ((8, 128), f32),
            ((KEPT, 80), bf16),
            ((80, KEPT), bf16),
        ],
        [((ROWS, 768), f32)],
        1_000_000_000,
        12,
        stacked, lax.ppermute(tile, STRIPS + CHAN, seams()), *quarters,
    )
    (wturned,) = call(turn_kernel, [((KEPT, 1024), bf16)], [], 500_000_000, 8, *shared)
    masked, whitened = call(
        forward_kernel,
        [((ROWS, KEPT, LANES), bf16), ((KEPT, FLAT), bf16)],
        [((ROWS, KEPT, 128), f32), ((LANES, 128), bf16)],
        3_000_000_000,
        18,
        patches, tissue, scale, norm, inv_density, anch,
    )
    rows = ((512, 128), bf16)
    partial, *early = call(
        early_kernel,
        [((KEPT, FLAT), f32)] + [rows] * 4,
        [],
        2_000_000_000,
        14,
        *first_blocks, wturned, whitened,
    )
    anchor_grad, image_part = call(
        backward_kernel,
        [((80, KEPT), f32), ((128, LANES), bf16)],
        [((ROWS * KEPT, 128), bf16), ((36 * GROUP, LANES), f32), ((128, LANES), bf16)],
        5_000_000_000,
        24,
        *last_blocks, partial, wturned, inv_density, masked, patches, inv_square, anch_t,
    )

    parts = lax.all_to_all(image_part.reshape(16, 8, LANES), CHAN, 0, 0)
    rows = ((560, 128), bf16)
    own, *away = call(
        finish_kernel,
        [rows] * 4,
        [],
        20_000_000_000,
        12,
        *last_blocks, whitened, *early, anchor_grad,
    )
    middle, kept, *others = call(
        chip_kernel,
        [((8, 512), f32)] + [((176, 128), bf16)] * 4,
        [((560, 128), f32)],
        1_000_000,
        8,
        parts, own, *(send(value, 0, other) for other, value in enumerate(away, 1)),
    )
    others = [
        lax.ppermute(value, "y", [(y, (y + step) % 4) for y in range(4)])
        for step, value in enumerate(others, 1)
    ]
    (packed,) = call(
        pack_kernel, [((4, 80, 128), bf16)], [((128, 128), f32)], 1_000_000, 4, kept, *others
    )
    return tuple(
        call(
            unpack_kernel,
            [((OWN, 75), f32), ((OWN, OWN), f32), ((3, 2, 512), f32)],
            [],
            1_000_000,
            4,
            lax.all_to_all(packed, "z_hi", 0, 0), middle,
        )
    )


def solution(mesh):
    fine = Mesh(mesh.devices.reshape(4, 4, 4, 2, 2), STRIPS + CHAN)
    placed = (
        P(None, None, STRIPS),
        P(None, STRIPS),
        P(CHAN, None),
        P(None, CHAN),
        P(CHAN, None, STRIPS),
    )
    return jax.shard_map(
        shards,
        mesh=fine,
        in_specs=placed,
        out_specs=(P(CHAN, None), P(STRIPS, CHAN), P(None, CHAN, STRIPS)),
        check_vma=False,
    )
```

```python
import math

import jax
import jax.numpy as jnp
from jax import lax
from jax.experimental import pallas as pl
from jax.experimental.pallas import tpu as pltpu
from jax.sharding import Mesh
from jax.sharding import PartitionSpec as P

EPS = 1e-05
LANES = 256
REACH = 135
QUARTER = 64
FLAT = 16 * QUARTER
ROWS = 32
GROUP = 16
OWN = 64
KEPT = 4 * OWN
STEP = 32
EARLY = 12
MIB = 1024 * 1024

STRIPS = ("z_hi", "y")
CHAN = ("x", "z_lo", "core")


def route(dx, other):
    return [(i, (i // 4 + dx) % 4 * 4 + (i % 4 ^ other)) for i in range(16)]


def seams():
    pairs = [(16 * s + 4 * x, 16 * s - 16 + 4 * x + 3) for s in range(1, 16) for x in range(4)]
    return pairs + [(b, a) for a, b in pairs]


f32 = jnp.float32
bf16 = jnp.bfloat16


def tap(distance):
    return math.exp(-distance * distance / 8.0) if abs(distance) <= 4 else 0.0


def taps(distance):
    far = jnp.abs(distance) > 4
    distance = distance.astype(f32)
    return jnp.where(far, 0.0, jnp.exp(distance * distance * (-1.0 / 8.0)))


def places(shape):
    return tuple(lax.broadcasted_iota(jnp.int32, shape, dim) for dim in (0, 1))


def column_pool():
    lane, target = places((LANES, 128))
    return taps(2 * (target & 63) - lane + 4).astype(bf16)


def column_spread():
    target, lane = places((128, LANES))
    return taps(2 * (target & 63) - lane + 4).astype(bf16)


def row_weights(t, i):
    low, high = tap(4 * t - i), tap(4 * t + 2 - i)
    if low == 0.0 and high == 0.0:
        return None
    return jnp.where(lax.broadcasted_iota(jnp.int32, (1, 128), 1) < QUARTER, low, high)


def row_pool(odd):
    t, i = places((8, ROWS))
    return taps(4 * t + 2 * odd - i)


def split_group(row):
    q = row & (GROUP - 1)
    colour = jnp.where(q < 5, 0, jnp.where(q < 10, 1, jnp.where(q < 15, 2, 3)))
    return row >> 4, colour, q - 5 * colour


def ones(hit, dtype=bf16):
    return jnp.where(hit, 1.0, 0.0).astype(dtype)


def replicate_rows():
    out, src = places((36 * GROUP, 3 * ROWS))
    r, colour, _ = split_group(out)
    return ones(((src & 31) == r - 2) & ((src >> 5) == colour))


def fold_rows():
    out, src = places((128, 36 * GROUP))
    r, colour, _ = split_group(src)
    i = 2 * (out >> 3) + (out & 1)
    return ones((r == i + 2) & (colour == ((out & 7) >> 1)) & (colour < 3))


def entry_order(dtype, rows=75):
    entry, out = places((rows, 80))
    a, colour, b = split_group(out)
    return ones((entry == 25 * colour + 5 * a + b) & (colour < 3), dtype)


def quarter():
    return lax.axis_index("z_lo") * 2 + lax.axis_index("core")


def flipped(axis, bit):
    return lax.rem(lax.axis_index(axis) + bit, 2)


def block_of(p):
    dx, other = (0, 1, 3, 2)[p // 4], p % 4
    ex = lax.rem(lax.axis_index("x") + dx, 4)
    return ex * 4 + flipped("z_lo", other // 2) * 2 + flipped("core", other % 2)


def dot(a, b):
    return jnp.dot(a, b, preferred_element_type=f32)


def dot_nt(a, b):
    return lax.dot_general(a, b, (((1,), (1,)), ((), ())), preferred_element_type=f32)


def quarter_kernel(cotangent, anchors, own, core, zed, both, parts):
    lane = lax.broadcasted_iota(jnp.int32, (OWN, 128), 1)
    for t in range(8):
        low, high = (cotangent[:, 2 * t + n, :].astype(f32) for n in (0, 1))
        for side in range(2):
            cols = slice(side * 128, side * 128 + 128)
            even = jnp.where(lane < QUARTER, low[:, cols], pltpu.roll(high[:, cols], QUARTER, 1))
            odd = jnp.where(lane < QUARTER, pltpu.roll(low[:, cols], QUARTER, 1), high[:, cols])
            parts[2 * side, :, t * 128 : (t + 1) * 128] = even.astype(bf16)
            parts[2 * side + 1, :, t * 128 : (t + 1) * 128] = odd.astype(bf16)
    for other, part in enumerate((own, core, zed, both)):
        part[:, :FLAT] = parts[flipped("z_lo", other // 2) * 2 + flipped("core", other % 2)]
        part[:, FLAT:] = jnp.zeros((OWN, 128), bf16)
        part[:, FLAT : FLAT + 75] = anchors[...]


def join_kernel(*refs):
    *parts, _, _, joined = refs
    start = 0
    for ref in parts:
        joined[start : start + ref.shape[0]] = ref[:, :FLAT]
        start += ref.shape[0]


def bundle_kernel(whiten, after, bundle):
    del after
    bundle[:, :OWN] = whiten[0:512, :]
    bundle[:, OWN:] = whiten[512:1024, :]


def halve_kernel(first, second, after, upper, lower):
    del after
    upper[...] = first[: KEPT // 2]
    lower[...] = second[KEPT // 2 :]


def rim_kernel(stacked, *refs):
    tile = refs[-1]
    first = quarter() == 0
    for c in range(4):
        value = stacked[c].astype(f32)
        tile[c] = jnp.where(first, value[:, :128], value[:, 384:]).astype(bf16)


def patch_kernel(
    stacked, beyond, *refs,
):
    quarters = refs[:4]
    patches, tissue, scale, norm, inv_square, inv_density, anch, anch_t, wide = refs[4:]
    start = pl.multiple_of(quarter() * 128, 128)

    def part(c, shift):
        rim = beyond[c].astype(f32)
        wide[:, 0:128] = rim
        wide[:, 128:640] = stacked[c].astype(f32)
        wide[:, 640:768] = rim
        return pltpu.roll(wide[:, pl.ds(start, 384)], 384 - shift, 1)[:, :LANES]

    colours = [part(c, 122) for c in range(3)]
    here = part(3, 124)
    lane = lax.broadcasted_iota(jnp.int32, here.shape, 1)
    here = jnp.where(lane < REACH, here, 0.0)
    tissue[...] = here
    x = dot(replicate_rows(), jnp.concatenate(colours, axis=0).astype(bf16))
    offset = (lax.broadcasted_iota(jnp.int32, x.shape, 0) % GROUP) % 5
    s = x
    for b in range(1, 5):
        s = jnp.where(offset == b, pltpu.roll(x, LANES - b, 1), s)
    patches[...] = s.astype(bf16)
    square = jnp.sum((s * s).reshape(36, GROUP, LANES), axis=1)
    total = square[0:ROWS]
    for a in range(1, 5):
        total = total + square[a : a + ROWS]
    total = total + EPS
    root = lax.rsqrt(total)
    scale[...] = 4.0 * root
    norm[...] = total * root
    inv_square[...] = 1.0 / total
    counted = dot(here.astype(bf16), column_pool())
    even, odd = (
        jnp.dot(row_pool(n), counted, precision=lax.Precision.HIGHEST, preferred_element_type=f32)
        for n in (0, 1)
    )
    lane = lax.broadcasted_iota(jnp.int32, even.shape, 1)
    inv_density[...] = 1.0 / jnp.maximum(jnp.where(lane < QUARTER, even, odd), 1.0)
    anchors = jnp.concatenate([part[:, FLAT:] for part in quarters], axis=0)
    ordered = dot(anchors, entry_order(bf16, 128))
    anch[...] = ordered.astype(bf16)
    anch_t[...] = ordered.T.astype(bf16)

def turn_kernel(*refs):
    *shared, wturned = refs
    blocks = [block_of(p) for p in range(16)]
    for n, bundle in enumerate(shared):
        ordered = []
        for block in blocks:
            rows = pl.ds(pl.multiple_of(lax.rem(block, 8) * OWN, OWN), OWN)
            value = bundle[rows, :].astype(f32)
            ordered.append(jnp.where(block >= 8, pltpu.roll(value, OWN, 1), value))
        turned = jnp.concatenate(ordered, axis=0).T
        wturned[n * OWN : (n + 1) * OWN, :] = turned[:OWN].astype(bf16)


def forward_kernel(
    patches, tissue, scale, norm, inv_density, anch,
    masked, whitened,
    columned, pool,
):
    pool[...] = column_pool()

    @pl.loop(0, ROWS // STEP)
    def _(t):
        lifted = []
        for r in range(STEP):
            i = t * STEP + r
            patch = patches[pl.ds(pl.multiple_of(i * GROUP, GROUP), 80), :]
            raw = dot(anch[...], patch)
            value = jnp.exp(raw * scale[pl.ds(i, 1), :] - 4.0) * tissue[pl.ds(i, 1), :]
            masked[i] = value.astype(bf16)
            lifted.append((value * norm[pl.ds(i, 1), :]).astype(bf16))
        result = dot(jnp.concatenate(lifted, axis=0), pool[...])
        columned[pl.ds(t * STEP, STEP)] = result.reshape(STEP, KEPT, 128)

    for t in range(8):
        acc = None
        for i in range(ROWS):
            weights = row_weights(t, i)
            if weights is not None:
                term = weights * columned[i]
                acc = term if acc is None else acc + term
        whitened[:, t * 128 : (t + 1) * 128] = (acc * inv_density[t : t + 1, :]).astype(bf16)


def fold(block, rows):
    top, low = block[:rows], block[rows:]
    left = lax.broadcasted_iota(jnp.int32, top.shape, 1) < OWN
    own = jnp.where(left, top, pltpu.roll(low, OWN, 1))
    partner = jnp.where(left, pltpu.roll(top, OWN, 1), low)
    return own.astype(bf16), partner.astype(bf16)


def stacks(blocks):
    for n in range(FLAT // 256):
        cols = slice(n * 256, (n + 1) * 256)
        yield cols, jnp.concatenate([block[:, cols] for block in blocks], axis=0)


def whiten_rows(blocks, whitened):
    return sum(dot_nt(stack, whitened[:, cols]) for cols, stack in stacks(blocks))


def four_folds(block, rows):
    return fold(block[:, :128], rows) + fold(block[:, 128:], rows)


def place_rows(sums, grad_w, first):
    for n in range(grad_w.shape[0] // OWN):
        strip = block_of(first + n)
        place = lax.rem(strip, 4) * 4 + strip // 4
        rows = pl.ds(pl.multiple_of(place * 32, 32), 32)
        for ref, value in zip(sums, four_folds(grad_w[n * OWN : (n + 1) * OWN], OWN // 2)):
            ref[rows, :] = value


def early_kernel(*refs):
    blocks, (wturned, whitened, partial, *sums) = refs[:3], refs[3:]
    for ref in sums:
        ref[...] = jnp.zeros_like(ref)
    for cols, stack in stacks(blocks):
        partial[:, cols] = dot(wturned[:, : EARLY * OWN], stack)
    place_rows(sums, whiten_rows(blocks, whitened), 0)


def backward_kernel(
    first, second, partial, wturned, inv_density, masked, patches, inv_square, anch_t,
    anchor_grad, image,
    rowed, spread_grad, pool_t,
):
    pool_t[...] = column_spread()
    scaled = []
    for cols, stack in stacks((first, second)):
        pooled = partial[:, cols] + dot(wturned[:, EARLY * OWN :], stack)
        for side in range(2):
            t = len(scaled)
            part = pooled[:, side * 128 : (side + 1) * 128]
            scaled.append(part.astype(bf16).astype(f32) * (4.0 * inv_density[t : t + 1, :]))
    for i in range(ROWS):
        acc = None
        for t in range(8):
            weights = row_weights(t, i)
            if weights is not None:
                term = weights * scaled[t]
                acc = term if acc is None else acc + term
        rowed[i * KEPT : (i + 1) * KEPT, :] = acc.astype(bf16)
    spread_grad[...] = jnp.zeros_like(spread_grad)
    anchor_grad[...] = jnp.zeros_like(anchor_grad)

    @pl.loop(0, ROWS // STEP)
    def _(t):
        start = pl.multiple_of(t * (STEP * KEPT), STEP * KEPT)
        spread = dot(rowed[pl.ds(start, STEP * KEPT), :], pool_t[...])
        grads, wides, units = [], [], []
        for r in range(STEP):
            i = t * STEP + r
            patch = patches[pl.ds(pl.multiple_of(i * GROUP, GROUP), 80), :]
            grad = (spread[r * KEPT : (r + 1) * KEPT] * masked[i].astype(f32)).astype(bf16)
            unit = dot(anch_t[...], grad)
            wide = patch.astype(f32)
            along = jnp.sum(wide * unit, axis=0, keepdims=True) * inv_square[pl.ds(i, 1), :]
            units.append(unit - wide * along)
            grads.append(grad)
            wides.append(patch)
        anchor_grad[...] += dot_nt(jnp.concatenate(wides, axis=1), jnp.concatenate(grads, axis=1))
        sums = []
        for g in range(STEP + 4):
            acc = None
            for r in range(STEP):
                if 0 <= g - r < 5:
                    term = units[r][(g - r) * GROUP : (g - r + 1) * GROUP]
                    acc = term if acc is None else acc + term
            sums.append(acc)
        here = pl.ds(pl.multiple_of(t * (STEP * GROUP), STEP * GROUP), (STEP + 4) * GROUP)
        spread_grad[here, :] += jnp.concatenate(sums, axis=0)

    t = spread_grad[...]
    offset = (lax.broadcasted_iota(jnp.int32, t.shape, 0) % GROUP) % 5
    moved = t
    for b in range(1, 5):
        moved = jnp.where(offset == b, pltpu.roll(t, b, 1), moved)
    high = moved.astype(bf16)
    low = (moved - high.astype(f32)).astype(bf16)
    folder = fold_rows()
    image[...] = (dot(folder, high) + dot(folder, low)).astype(bf16)


def finish_kernel(*refs):
    first, second, whitened, *early = refs[:7]
    anchor_grad, *sums = refs[7:]
    pad = jnp.zeros((8, 128), bf16)
    for ref, start, part in zip(sums, early, four_folds(anchor_grad[...], 40)):
        ref[0:512, :] = start[...]
        ref[512:560, :] = jnp.concatenate([part, pad], axis=0)
    place_rows(sums, whiten_rows((first, second), whitened), EARLY)


def add_up(refs):
    total = refs[0][...].astype(f32)
    for ref in refs[1:]:
        total = total + ref[...].astype(f32)
    return total


def rim_lanes(rims):
    lane = lax.broadcasted_iota(jnp.int32, rims.shape, 1)
    return jnp.where(lane < 6, rims, 0.0), jnp.where(lane >= 122, rims, 0.0)


def chip_kernel(parts, own, one, two, three, middle, kept, next_one, next_two, next_three, sums):
    gap = jnp.zeros((8, 128), f32)
    whole = None
    for q in range(4):
        part = add_up([parts.at[4 * x + q] for x in range(4)])
        pieces = [gap] * q + [part] + [gap] * (3 - q)
        placed = jnp.concatenate(pieces, axis=1)
        whole = placed if whole is None else whole + placed
    turned = pltpu.roll(whole, 640 - 6, 1)
    middle[...] = turned[:, :512]
    later, earlier = rim_lanes(turned[:, 512:])
    y, z = lax.axis_index("y"), lax.axis_index("z_hi")
    later = jnp.where((y == 3) & (z == 3), 0.0, later)
    earlier = jnp.where((y == 0) & (z == 0), 0.0, earlier)
    later = jnp.where(y == 3, pltpu.roll(later, 64, 1), later)
    earlier = jnp.where(y == 0, pltpu.roll(earlier, 64, 1), earlier)
    sums[...] = add_up((own, one, two, three))
    for step, part in enumerate((kept, next_one, next_two, next_three)):
        target = lax.rem(y + step, 4)
        part[0:128, :] = sums[pl.ds(pl.multiple_of(target * 128, 128), 128), :].astype(bf16)
        rims = {1: later, 3: earlier}.get(step, gap)
        part[128:176, :] = jnp.concatenate([sums[512:552, :], rims], axis=0).astype(bf16)


def pack_kernel(kept, one, two, three, packed, sums):
    total = add_up((kept, one, two, three))
    sums[...] = total[0:128]
    straight = rim_lanes(total[168:176])
    onward = rim_lanes(pltpu.roll(total[168:176], 64, 1))
    rims = (straight[0] + straight[1], onward[0], jnp.zeros((8, 128), f32), onward[1])
    for step in range(4):
        z = lax.rem(lax.axis_index("z_hi") + step, 4)
        packed[z, 0:32, :] = sums[pl.ds(pl.multiple_of(z * 32, 32), 32), :].astype(bf16)
        packed[z, 32:80, :] = jnp.concatenate([total[128:168], rims[step]], axis=0).astype(bf16)


def unpack_kernel(received, middle, grad_anchors, grad_whiten, grad_image):
    total = add_up([received.at[z] for z in range(4)])
    other = pltpu.roll(total, OWN, 1)
    grad_whiten[0:32, :] = total[0:32, :OWN]
    grad_whiten[32:64, :] = other[0:32, :OWN]
    turned = jnp.concatenate([total[32:72], other[32:72]], axis=0).T[:OWN]
    grad_anchors[...] = lax.dot_general(
        turned, entry_order(f32), (((1,), (1,)), ((), ())),
        precision=lax.Precision.HIGHEST, preferred_element_type=f32,
    )
    first, last = rim_lanes(total[72:80])
    image = middle[...] + jnp.concatenate([first, jnp.zeros((8, 256), f32), last], axis=1)
    for colour in range(3):
        grad_image[colour] = image[2 * colour : 2 * colour + 2]


def hold(value, *after):
    def kernel(*refs):
        del refs

    return pl.pallas_call(
        kernel,
        out_shape=jax.ShapeDtypeStruct(value.shape, value.dtype),
        in_specs=[pl.BlockSpec(memory_space=pl.ANY)] * (1 + len(after)),
        out_specs=pl.BlockSpec(memory_space=pl.ANY),
        input_output_aliases={0: 0},
        compiler_params=pltpu.CompilerParams(vmem_limit_bytes=MIB),
        cost_estimate=pl.CostEstimate(flops=1000, bytes_accessed=1000, transcendentals=0),
    )(value, *after)


def call(kernel, outs, scratch, flops, limit, *args, loose=0):
    size = lambda shape, dtype: math.prod(shape) * jnp.dtype(dtype).itemsize
    tight = len(args) - loose
    moved = sum(size(a.shape, a.dtype) for a in args[:tight]) + sum(size(*out) for out in outs)
    return pl.pallas_call(
        kernel,
        out_shape=[jax.ShapeDtypeStruct(shape, dtype) for shape, dtype in outs],
        in_specs=[pl.BlockSpec(memory_space=pltpu.VMEM)] * tight
        + [pl.BlockSpec(memory_space=pl.ANY)] * loose,
        out_specs=[pl.BlockSpec(memory_space=pltpu.VMEM)] * len(outs),
        scratch_shapes=[pltpu.VMEM(shape, dtype) for shape, dtype in scratch],
        compiler_params=pltpu.CompilerParams(vmem_limit_bytes=limit * MIB),
        cost_estimate=pl.CostEstimate(flops=flops, bytes_accessed=moved, transcendentals=0),
    )(*args)


def shards(image, mask, anchors, whiten, cotangent):
    def send(value, dx, other):
        return lax.ppermute(value, CHAN, route(dx, other))

    part = ((OWN, FLAT + 128), bf16)
    own, *away = call(
        quarter_kernel, [part] * 4, [((4, OWN, FLAT), bf16)], 1_000_000, 6, cotangent, anchors
    )
    quarters = [own] + [send(value, 0, other) for other, value in enumerate(away, 1)]
    (bundle,) = call(
        bundle_kernel, [((512, 128), bf16)], [], 1_000_000, 4, whiten, away[2], loose=1
    )

    stacked = jnp.concatenate([image, mask.astype(bf16)[None]], axis=0)
    (tile,) = call(
        rim_kernel, [((4, ROWS, 128), bf16)], [], 1_000_000, 4, stacked, away[2], loose=1
    )
    (block,) = call(
        join_kernel,
        [((KEPT, FLAT), bf16)],
        [],
        1_000_000,
        4,
        *quarters, tile, bundle,
        loose=2,
    )
    last, following = send(block, 1, 0), send(block, 3, 0)
    bundle = hold(bundle, block)
    shared = [bundle] + [send(bundle, 0, other) for other in (1, 2, 3)]
    plane = ((ROWS, LANES), f32)
    patches, tissue, scale, norm, inv_square, inv_density, anch, anch_t = call(
        patch_kernel,
        [
            ((36 * GROUP, LANES), bf16),
            plane,
            plane,
            plane,
            plane,
            ((8, 128), f32),
            ((KEPT, 80), bf16),
            ((80, KEPT), bf16),
        ],
        [((ROWS, 768), f32)],
        1_000_000_000,
        12,
        stacked, lax.ppermute(tile, STRIPS + CHAN, seams()), *quarters,
    )
    (wturned,) = call(turn_kernel, [((KEPT, 1024), bf16)], [], 500_000_000, 8, *shared)
    masked, whitened = call(
        forward_kernel,
        [((ROWS, KEPT, LANES), bf16), ((KEPT, FLAT), bf16)],
        [((ROWS, KEPT, 128), f32), ((LANES, 128), bf16)],
        3_000_000_000,
        18,
        patches, tissue, scale, norm, inv_density, anch,
    )
    half = ((KEPT // 2, FLAT), bf16)
    upper, lower = call(
        halve_kernel, [half, half], [], 1_000_000, 4, last, following, whitened, loose=1
    )
    first_blocks = (block, following, last)
    last_blocks = (send(upper, 1, 0), send(lower, 3, 0))
    rows = ((512, 128), bf16)
    partial, *early = call(
        early_kernel,
        [((KEPT, FLAT), f32)] + [rows] * 4,
        [],
        2_000_000_000,
        14,
        *first_blocks, wturned, whitened,
    )
    anchor_grad, image_part = call(
        backward_kernel,
        [((80, KEPT), f32), ((128, LANES), bf16)],
        [((ROWS * KEPT, 128), bf16), ((36 * GROUP, LANES), f32), ((128, LANES), bf16)],
        5_000_000_000,
        24,
        *last_blocks, partial, wturned, inv_density, masked, patches, inv_square, anch_t,
    )

    parts = lax.all_to_all(image_part.reshape(16, 8, LANES), CHAN, 0, 0)
    rows = ((560, 128), bf16)
    own, *away = call(
        finish_kernel,
        [rows] * 4,
        [],
        20_000_000_000,
        12,
        *last_blocks, whitened, *early, anchor_grad,
    )
    middle, kept, *others = call(
        chip_kernel,
        [((8, 512), f32)] + [((176, 128), bf16)] * 4,
        [((560, 128), f32)],
        1_000_000,
        8,
        parts, own, *(send(value, 0, other) for other, value in enumerate(away, 1)),
    )
    others = [
        lax.ppermute(value, "y", [(y, (y + step) % 4) for y in range(4)])
        for step, value in enumerate(others, 1)
    ]
    (packed,) = call(
        pack_kernel, [((4, 80, 128), bf16)], [((128, 128), f32)], 1_000_000, 4, kept, *others
    )
    return tuple(
        call(
            unpack_kernel,
            [((OWN, 75), f32), ((OWN, OWN), f32), ((3, 2, 512), f32)],
            [],
            1_000_000,
            4,
            lax.all_to_all(packed, "z_hi", 0, 0), middle,
        )
    )


def solution(mesh):
    fine = Mesh(mesh.devices.reshape(4, 4, 4, 2, 2), STRIPS + CHAN)
    placed = (
        P(None, None, STRIPS),
        P(None, STRIPS),
        P(CHAN, None),
        P(None, CHAN),
        P(CHAN, None, STRIPS),
    )
    return jax.shard_map(
        shards,
        mesh=fine,
        in_specs=placed,
        out_specs=(P(CHAN, None), P(STRIPS, CHAN), P(None, CHAN, STRIPS)),
        check_vma=False,
    )
```
